32 devices in a mesh: group: 2 (over x), lat: 16 (over z, y, core).
Axes of the slice: x: 2, y: 2, z: 4, core: 2. Of those that a mesh axis runs over, the one named last changes fastest.
Arguments:
- field: bfloat16 [1024, 512, 512], P(('group', 'lat')), parts along dimension 0, may hold values from -6 to 6
- lat_modes: float32 [64, 16, 16], replicated, may hold values from -1.5 to 1.5
- lat_gains: float32 [64, 16], replicated, may hold values from 2 to 16
- lat_local: float32 [16, 16], replicated, may hold values from -1.5 to 1.5
- depth_modes: float32 [16, 16, 16], replicated, may hold values from -1.5 to 1.5
- depth_local: float32 [16, 16], replicated, may hold values from -1.5 to 1.5
Outputs:
- result: bfloat16 [1024, 512, 512], P(('group', 'lat')), parts along dimension 0
The draws below stay inside these ranges and needn't reach their ends.
There are 2 independent parts, one for each index of `group`. The reference program is written for one: setup_inputs(seed, part) draws one part's arguments, and reference() takes and returns one part's arrays. A program takes and returns all parts, laid end to end along the dimension named above; an argument that names none is the same for every part. Nothing has to cross between parts.
All inputs are finite; a program needn't handle non-finite values.
Results may differ from the reference program's by a relative error of at most 0.001.
Values may be sent and summed in bfloat16 or wider, within the bound.
No kernel may reach another device: no remote copies, remote signals or barrier semaphores. Data moves between devices by JAX's collectives and lax.ppermute only.
A program may use at most 192 MiB of HBM per device.

```python
import math
import jax
import jax.numpy as jnp
from jax import lax

X = 512
Y = 512
Z = 32
C = 16
KX = 64
KY = 64
KZ = 16
ZC = 512


def levels(rng, dims, pieces, smallest, top_value):
    factor_of, own = 1.0, jax.random.fold_in(rng, 6)
    for axis_at, parts in pieces:
        draws = jnp.exp(jax.random.uniform(jax.random.fold_in(own, axis_at), (parts,), jnp.float32, smallest / len(pieces), top_value / len(pieces)))
        factor_of = factor_of * jnp.repeat(draws, dims[axis_at] // parts).reshape([-1 if axis == axis_at else 1 for axis in range(len(dims))])
    return factor_of


def gaussian(rng, shape, deviation, most, shards=(), kind=jnp.bfloat16):
    values = deviation * jax.random.normal(rng, shape, jnp.float32)
    if shards:
        values = values * levels(rng, shape, shards, -0.22, 0.18)
    return jnp.clip(values, -most, most).astype(kind)


def setup_inputs(seed: int = 0, part: int = 0) -> dict:
    keys = jax.random.split(jax.random.key(seed), 7)
    part_splits = jax.random.split(jax.random.fold_in(keys[6], part), 7)
    field = gaussian(part_splits[0], (X, Y, ZC), 1.0, 6.0, ((0, 16),))
    lat_modes = gaussian(keys[1], (KX, C, C), C ** -0.5, 1.5, (), jnp.float32)
    lat_gains = jnp.clip(jnp.exp(jax.random.uniform(keys[2], (KY, C), jnp.float32, math.log(2.0), math.log(16.0))), 2.0, 16.0)
    lat_local = gaussian(keys[3], (C, C), C ** -0.5, 1.5, (), jnp.float32)
    depth_modes = gaussian(keys[4], (KZ, C, C), C ** -0.5, 1.5, (), jnp.float32)
    depth_local = gaussian(keys[5], (C, C), C ** -0.5, 1.5, (), jnp.float32)
    return {"field": field, "lat_modes": lat_modes, "lat_gains": lat_gains, "lat_local": lat_local, "depth_modes": depth_modes, "depth_local": depth_local}


def cosine_basis(length, modes):
    order = jnp.arange(modes, dtype=jnp.float32)[:, None]
    place = jnp.arange(length, dtype=jnp.float32)[None, :]
    scales = jnp.where(order == 0.0, math.sqrt(1.0 / length), math.sqrt(2.0 / length))
    return jnp.cos(math.pi * order * (place + 0.5) / length) * scales

def row_tail(u_rows, spect, lat_local, depth_modes, depth_local, depth_basis):
    highest = lax.Precision.HIGHEST
    rows, width, cells = u_rows.shape
    chans = lat_local.shape[0]
    depth = cells // chans
    u4 = u_rows.reshape(rows, width, depth, chans)
    s4 = spect.reshape(rows, width, depth, chans)
    first = u4 + jax.nn.gelu(s4 + jnp.einsum('xyzc,cd->xyzd', u4, lat_local, precision=highest))
    dcoef = jnp.einsum('kz,xyzc->xykc', depth_basis, first, precision=highest)
    dmix = jnp.einsum('xykc,kcd->xykd', dcoef, depth_modes, precision=highest)
    dspect = jnp.einsum('kz,xykd->xyzd', depth_basis, dmix, precision=highest)
    final = first + jax.nn.gelu(dspect + jnp.einsum('xyzc,cd->xyzd', first, depth_local, precision=highest))
    return final.reshape(rows, width, cells).astype(jnp.bfloat16)

def reference(field, lat_modes, lat_gains, lat_local, depth_modes, depth_local):
    highest = lax.Precision.HIGHEST
    basis_x = cosine_basis(X, KX)
    basis_y = cosine_basis(Y, KY)
    basis_z = cosine_basis(Z, KZ)
    block = min(X, 32)
    blocks = field.reshape(X // block, block, Y, Z * C)

    def forward_rows(rows):
        return jnp.einsum('qy,xyw->xqw', basis_y, rows.astype(jnp.float32), precision=highest)
    partial_coef = lax.map(forward_rows, blocks).reshape(X, KY, Z * C)
    coef = jnp.einsum('px,xqw->pqw', basis_x, partial_coef, precision=highest)
    coef4 = coef.reshape(KX, KY, Z, C) * lat_gains[None, :, None, :]
    mixed = jnp.einsum('pqzc,pcd->pqzd', coef4, lat_modes, precision=highest).reshape(KX, KY, Z * C)
    back_rows = jnp.einsum('px,pqw->xqw', basis_x, mixed, precision=highest)
    back_blocks = back_rows.reshape(X // block, block, KY, Z * C)

    def finish(pair):
        rows, back = pair
        spect = jnp.einsum('qy,xqw->xyw', basis_y, back, precision=highest)
        return row_tail(rows.astype(jnp.float32), spect, lat_local, depth_modes, depth_local, basis_z)
    out = lax.map(finish, (blocks, back_blocks))
    return out.reshape(X, Y, Z * C)
```

```python
import functools
import math

import jax
import jax.numpy as jnp
import ml_dtypes
import numpy as np
from jax import lax
from jax.experimental import pallas as pl
from jax.experimental.pallas import tpu as pltpu
from jax.sharding import PartitionSpec as P


def cosine_basis(length, modes):
    order = jnp.arange(modes, dtype=jnp.float32)[:, None]
    place = jnp.arange(length, dtype=jnp.float32)[None, :]
    scales = jnp.where(order == 0.0, math.sqrt(1.0 / length), math.sqrt(2.0 / length))
    return jnp.cos(math.pi * order * (place + 0.5) / length) * scales


def row_tail(u_rows, spect, lat_local, depth_modes, depth_local, depth_basis):
    highest = lax.Precision.HIGHEST
    rows, width, cells = u_rows.shape
    chans = lat_local.shape[0]
    depth = cells // chans
    u4 = u_rows.reshape(rows, width, depth, chans)
    s4 = spect.reshape(rows, width, depth, chans)
    first = u4 + jax.nn.gelu(s4 + jnp.einsum("xyzc,cd->xyzd", u4, lat_local, precision=highest))
    dcoef = jnp.einsum("kz,xyzc->xykc", depth_basis, first, precision=highest)
    dmix = jnp.einsum("xykc,kcd->xykd", dcoef, depth_modes, precision=highest)
    dspect = jnp.einsum("kz,xykd->xyzd", depth_basis, dmix, precision=highest)
    final = first + jax.nn.gelu(
        dspect + jnp.einsum("xyzc,cd->xyzd", first, depth_local, precision=highest)
    )
    return final.reshape(rows, width, cells).astype(jnp.bfloat16)


def one_hot(ids, count):
    return (ids[:, None] == jnp.arange(count, dtype=jnp.int32)[None, :]).astype(jnp.float32)


def plain_shards(field, lat_modes, lat_gains, lat_local, depth_modes, depth_local):
    highest = lax.Precision.HIGHEST
    devices = lax.axis_size("lat")
    rows_dev, width_y, cells = field.shape
    modes_x, chans, _ = lat_modes.shape
    modes_y = lat_gains.shape[0]
    modes_z = depth_modes.shape[0]
    depth = cells // chans
    width_x = rows_dev * devices
    basis_x = cosine_basis(width_x, modes_x)
    basis_y = cosine_basis(width_y, modes_y)
    basis_z = cosine_basis(depth, modes_z)
    start = lax.axis_index("lat")
    u_rows = field.astype(jnp.float32)
    coef_y = jnp.einsum("qy,xyw->xqw", basis_y, u_rows, precision=highest)
    packed = coef_y.reshape(rows_dev, modes_y * cells)
    gathered = lax.all_to_all(packed, "lat", split_axis=1, concat_axis=0, tiled=True)
    span = gathered.shape[1]
    pairs = span // chans
    coef = jnp.dot(basis_x, gathered, precision=highest).reshape(modes_x, pairs, chans)
    mode_ids = (start * pairs + jnp.arange(pairs, dtype=jnp.int32)) // depth
    gain_rows = jnp.dot(one_hot(mode_ids, modes_y), lat_gains, precision=highest)
    mixed = jnp.einsum("jpc,jcd->jpd", coef * gain_rows[None, :, :], lat_modes, precision=highest)
    back_x = jnp.dot(basis_x.T, mixed.reshape(modes_x, span), precision=highest)
    returned = lax.all_to_all(back_x, "lat", split_axis=0, concat_axis=1, tiled=True)
    spect = jnp.einsum(
        "qy,xqw->xyw", basis_y, returned.reshape(rows_dev, modes_y, cells), precision=highest
    )
    return row_tail(u_rows, spect, lat_local, depth_modes, depth_local, basis_z)


BF16 = jnp.bfloat16
F32 = jnp.float32
LANE = 128
GROUP = 8
SPAN = 256
TANH_A = 2.0 * math.sqrt(2.0 / math.pi)
TANH_B = 8.0 * 0.044715 * math.sqrt(2.0 / math.pi)


def basis64(length, modes):
    order = np.arange(modes)[:, None]
    place = np.arange(length)[None, :]
    scales = np.where(order == 0, math.sqrt(1.0 / length), math.sqrt(2.0 / length))
    return np.cos(math.pi * order * (place + 0.5) / length) * scales


def split64(array):
    high = array.astype(ml_dtypes.bfloat16)
    return high, (array - high.astype(np.float64)).astype(ml_dtypes.bfloat16)


def split(array):
    high = array.astype(BF16)
    return high, (array - high.astype(F32)).astype(BF16)


def split_outside(array):
    high = lax.reduce_precision(array, 8, 7)
    return high.astype(BF16), (array - high).astype(BF16)


def window_modes(rows, length, modes):
    place = np.arange(rows) - (rows - 1) / 2
    order = np.arange(modes)[:, None]
    _, se, ve = np.linalg.svd(np.cos(math.pi * order * place / length))
    _, so, vo = np.linalg.svd(np.sin(math.pi * order * place / length))
    top = max(se[0], so[0])
    half = rows // 2
    count = max(int(np.sum(se[:half] > top * 2.0**-24)), int(np.sum(so[:half] > top * 2.0**-24)))
    fine = max(int(np.sum(se[:half] > top * 0.1)), int(np.sum(so[:half] > top * 0.1)))
    funcs = np.stack([ve[:count], vo[:count]], axis=1).reshape(2 * count, rows)
    return funcs, 2 * fine


def forward_kernel(funcs, fine, by_ref, u_ref, o_ref, cy_ref):
    step = pl.program_id(0)
    block = u_ref.shape[0]
    rows, modes_y, _ = cy_ref.shape
    for r in range(block):
        z = jnp.dot(by_ref[...], u_ref[r], preferred_element_type=F32)
        cy_ref[step * block + r] = z[:modes_y] + z[modes_y:]

    @pl.when(step == pl.num_programs(0) - 1)
    def _():
        halves = cy_ref.shape[2] // SPAN
        count = funcs.shape[0]

        def compress(g, carry):
            q0 = pl.multiple_of(g * GROUP, GROUP)
            for h in range(halves):
                for k in range(SPAN // LANE):
                    lanes = slice(h * SPAN + k * LANE, h * SPAN + (k + 1) * LANE)
                    totals = [None] * count
                    for t in range(rows // 2):
                        a = cy_ref[t, pl.ds(q0, GROUP), lanes]
                        b = cy_ref[rows - 1 - t, pl.ds(q0, GROUP), lanes]
                        pair = (a + b, a - b)
                        for j in range(count):
                            term = pair[j % 2] * float(funcs[j, t])
                            totals[j] = term if t == 0 else totals[j] + term
                    place = slice(k * LANE, (k + 1) * LANE)
                    for j in range(0, count, 2):
                        high, low = split(jnp.concatenate(totals[j : j + 2], axis=0))
                        o_ref[g * halves + h, j * GROUP : (j + 2) * GROUP, place] = high
                        if j < fine:
                            at = (count + j) * GROUP
                            o_ref[g * halves + h, at : at + 2 * GROUP, place] = low
            return carry

        lax.fori_loop(0, modes_y // GROUP, compress, 0)


def mix_kernel(count, fine, r_ref, fh_ref, fl_ref, bh_ref, bl_ref, g_ref, wh_ref, wl_ref, o_ref, c_ref, mh_ref, ml_ref):
    devices, packed, span = r_ref.shape
    modes_x = wh_ref.shape[0]
    got = r_ref[...].reshape(devices * packed, span)
    for at in range(0, modes_x * GROUP, SPAN):
        part = slice(at, at + SPAN)
        c_ref[part] = jnp.dot(fh_ref[part], got, preferred_element_type=F32) + jnp.dot(
            fl_ref[part], got, preferred_element_type=F32
        )
    gains = g_ref[...]

    def mix(pair, carry):
        done = []
        for p in range(2):
            at = pl.multiple_of((2 * pair + p) * GROUP, GROUP)
            coef = c_ref[pl.ds(at, GROUP), :] * gains
            high, low = split(jnp.concatenate([coef[:, :LANE], coef[:, LANE:]], axis=0))
            both = jnp.concatenate([high, low], axis=0)
            z = jnp.dot(both, wh_ref[2 * pair + p], preferred_element_type=F32)
            z2 = jnp.dot(high, wl_ref[2 * pair + p], preferred_element_type=F32)
            z = z[: 2 * GROUP] + z[2 * GROUP :] + z2
            done.append(jnp.concatenate([z[:GROUP], z[GROUP:]], axis=1))
        high, low = split(jnp.concatenate(done, axis=0))
        at = pl.multiple_of(pair * 2 * GROUP, 2 * GROUP)
        mh_ref[pl.ds(at, 2 * GROUP), :] = high
        ml_ref[pl.ds(at, 2 * GROUP), :] = low
        return carry

    lax.fori_loop(0, modes_x // 2, mix, 0, unroll=4)
    right = jnp.concatenate([mh_ref[...], mh_ref[...], ml_ref[...]], axis=0)
    for i in range(devices):
        rows = slice(i * count * GROUP, (i + 1) * count * GROUP)
        left = jnp.concatenate([bh_ref[rows], bl_ref[rows], bh_ref[rows]], axis=1)
        z = jnp.dot(left, right, preferred_element_type=F32)
        high, low = split(z)
        o_ref[i, : count * GROUP] = high
        o_ref[i, count * GROUP :] = low[: fine * GROUP]


def tail_kernel(funcs, fine, yb, r_ref, u_ref, by_ref, l_ref, me_ref, mo_ref, flip_ref, o_ref, b_ref):
    step = pl.program_id(0)
    count, rows = funcs.shape
    modes_y = b_ref.shape[1] // 4
    flip = flip_ref[...]

    @pl.when(step == 0)
    def _():
        halves = b_ref.shape[2] // SPAN

        def expand(g, carry):
            at = pl.multiple_of(g * 2 * GROUP, 2 * GROUP)
            for h in range(halves):
                got = []
                for k in range(2):
                    block = r_ref[(2 * g + k) * halves + h]
                    turned = jnp.dot(block, flip, preferred_element_type=F32) if h else block.astype(F32)
                    got.append(turned)
                for c in range(SPAN // LANE):
                    part = slice(c * LANE, (c + 1) * LANE)
                    modes = []
                    for j in range(count):
                        pieces = []
                        for k in range(2):
                            piece = got[k][j * GROUP : (j + 1) * GROUP, part]
                            if j < fine:
                                low = got[k][(count + j) * GROUP : (count + j + 1) * GROUP, part]
                                piece = piece + low
                            pieces.append(piece)
                        modes.append(jnp.concatenate(pieces, axis=0))
                    lanes = slice(h * SPAN + c * LANE, h * SPAN + (c + 1) * LANE)
                    for t in range(rows // 2):
                        sums = []
                        for parity in range(2):
                            total = modes[parity] * float(0.5 * funcs[parity, t])
                            for j in range(parity + 2, count, 2):
                                total = total + modes[j] * float(0.5 * funcs[j, t])
                            sums.append(total)
                        for row, value in ((t, sums[0] + sums[1]), (rows - 1 - t, sums[0] - sums[1])):
                            high, low = split(value)
                            for n, half in enumerate((high, high, low, low)):
                                b_ref[row, pl.ds(at + n * modes_y, 2 * GROUP), lanes] = half
            return carry

        lax.fori_loop(0, modes_y // (2 * GROUP), expand, 0)

    row = step
    width = u_ref.shape[1]
    for y0 in range(0, width, yb):
        ys = slice(y0, y0 + yb)
        firsts = []
        for h in range(2):
            lanes = slice(h * SPAN, (h + 1) * SPAN)
            u = u_ref[0, ys, lanes]
            left = jnp.concatenate([by_ref[ys], u, u], axis=1)
            right = jnp.concatenate([b_ref[row, :, lanes], l_ref[h]], axis=0)
            x = jnp.dot(left, right, preferred_element_type=F32)
            seen = jnp.dot(u, flip, preferred_element_type=F32) if h else u.astype(F32)
            firsts.append(seen + twice_gelu(x))
        even, odd = firsts[0] + firsts[1], firsts[0] - firsts[1]
        outs = []
        for value, w_ref in ((even, me_ref), (odd, mo_ref)):
            high, low = split(value)
            left = jnp.concatenate([high, low, high], axis=1)
            outs.append(jnp.dot(left, w_ref[...], preferred_element_type=F32))
        near = firsts[0] + twice_gelu(outs[0] + outs[1])
        far = firsts[1] + twice_gelu(outs[0] - outs[1])
        o_ref[0, ys, :SPAN] = near.astype(BF16)
        turned = jnp.dot(far.astype(BF16), flip, preferred_element_type=F32)
        o_ref[0, ys, SPAN:] = turned.astype(BF16)


def twice_gelu(half):
    return half + half * jnp.tanh(half * (TANH_A + TANH_B * (half * half)))


def kron_eye(matrix, count):
    *lead, n, m = matrix.shape
    eye = jnp.eye(count, dtype=matrix.dtype)
    return (eye[:, None, :, None] * matrix[..., None, :, None, :]).reshape(*lead, count * n, count * m)


def fits(mesh_lat, rows, width_y, cells, chans, modes_x, modes_y):
    return (
        cells == 2 * SPAN
        and SPAN % (LANE // chans * chans) == 0
        and mesh_lat * GROUP * SPAN == modes_y * cells
        and rows % 4 == 0
        and rows >= 16
        and width_y % 256 == 0
        and 4 * modes_y == SPAN
        and modes_x % 8 == 0
    )


def shards(field, lat_modes, lat_gains, lat_local, depth_modes, depth_local):
    highest = lax.Precision.HIGHEST
    devices = lax.axis_size("lat")
    rows, width_y, cells = field.shape
    modes_x, chans, _ = lat_modes.shape
    modes_y = lat_gains.shape[0]
    modes_z = depth_modes.shape[0]
    if not fits(devices, rows, width_y, cells, chans, modes_x, modes_y):
        return plain_shards(field, lat_modes, lat_gains, lat_local, depth_modes, depth_local)
    depth = cells // chans
    width_x = rows * devices
    basis_x = basis64(width_x, modes_x)
    basis_y = basis64(width_y, modes_y)
    basis_z = basis64(depth, modes_z)
    funcs, fine = window_modes(rows, width_x, modes_x)
    count = funcs.shape[0]
    packed = (count + fine) * GROUP
    halves = cells // SPAN
    me = lax.axis_index("lat")

    by_high, by_low = split64(basis_y)
    by_forward = np.concatenate([by_high, by_low], axis=0)
    block = 4
    sent = pl.pallas_call(
        functools.partial(forward_kernel, funcs, fine),
        grid=(rows // block,),
        in_specs=[
            pl.BlockSpec((2 * modes_y, width_y), lambda s: (0, 0)),
            pl.BlockSpec((block, width_y, cells), lambda s: (s, 0, 0)),
        ],
        out_specs=pl.BlockSpec((devices, packed, SPAN), lambda s: (0, 0, 0)),
        out_shape=jax.ShapeDtypeStruct((devices, packed, SPAN), BF16),
        scratch_shapes=[pltpu.VMEM((rows, modes_y, cells), F32)],
        compiler_params=pltpu.CompilerParams(vmem_limit_bytes=48 * 2**20),
        name="forward",
    )(by_forward, field)
    gathered = lax.all_to_all(sent, "lat", split_axis=0, concat_axis=0, tiled=True)

    weights = np.einsum("pit,jt->pij", basis_x.reshape(modes_x, devices, rows), funcs)
    eye = np.eye(GROUP)

    def spread(array):
        n, m = array.shape
        return (array[:, None, :, None] * eye[None, :, None, :]).reshape(n * GROUP, m * GROUP)

    both = np.concatenate([weights, weights[:, :, :fine]], axis=2)
    fh, fl = split64(spread(both.reshape(modes_x, devices * (count + fine))))
    bh, bl = split64(spread(weights.reshape(modes_x, devices * count).T))
    gains = lax.dynamic_slice_in_dim(lat_gains, (me // halves) * GROUP, GROUP, axis=0)
    gains = jnp.tile(gains, (1, SPAN // chans))
    wh, wl = split_outside(kron_eye(lat_modes, LANE // chans))
    mixed = pl.pallas_call(
        functools.partial(mix_kernel, count, fine),
        out_shape=jax.ShapeDtypeStruct((devices, packed, SPAN), BF16),
        scratch_shapes=[
            pltpu.VMEM((modes_x * GROUP, SPAN), F32),
            pltpu.VMEM((modes_x * GROUP, SPAN), BF16),
            pltpu.VMEM((modes_x * GROUP, SPAN), BF16),
        ],
        compiler_params=pltpu.CompilerParams(vmem_limit_bytes=48 * 2**20),
        name="mix",
    )(gathered, fh, fl, bh, bl, gains, wh, wl)
    returned = lax.all_to_all(mixed, "lat", split_axis=0, concat_axis=0, tiled=True)

    by_back = np.concatenate([by_high, by_low, by_high, by_low], axis=0).T.copy()
    per = SPAN // chans
    flip = np.kron(np.eye(per)[::-1], np.eye(chans)).astype(ml_dtypes.bfloat16)
    local_high, local_low = split_outside(kron_eye(0.5 * lat_local, per))
    local = jnp.concatenate([local_high, local_low], axis=0)
    turned = local.reshape(2 * SPAN, per, chans)[:, ::-1].reshape(2 * SPAN, SPAN)
    local = jnp.stack([local, turned])
    near_z = basis_z[:, :per].astype(np.float32)

    def depth_matrix(parity):
        b = near_z[parity::2]
        full = 0.5 * jnp.einsum(
            "kz,kw,kcd->zcwd", b, b, depth_modes[parity::2], precision=highest
        ).reshape(SPAN, SPAN) + 0.25 * kron_eye(depth_local, per)
        high, low = split_outside(full)
        return jnp.concatenate([high, high, low], axis=0)

    yb = 256
    return pl.pallas_call(
        functools.partial(tail_kernel, funcs, fine, yb),
        grid=(rows,),
        in_specs=[
            pl.BlockSpec((devices, packed, SPAN), lambda s: (0, 0, 0)),
            pl.BlockSpec((1, width_y, cells), lambda s: (s, 0, 0)),
            pl.BlockSpec((width_y, SPAN), lambda s: (0, 0)),
            pl.BlockSpec((2, 2 * SPAN, SPAN), lambda s: (0, 0, 0)),
            pl.BlockSpec((3 * SPAN, SPAN), lambda s: (0, 0)),
            pl.BlockSpec((3 * SPAN, SPAN), lambda s: (0, 0)),
            pl.BlockSpec((SPAN, SPAN), lambda s: (0, 0)),
        ],
        out_specs=pl.BlockSpec((1, width_y, cells), lambda s: (s, 0, 0)),
        out_shape=jax.ShapeDtypeStruct(field.shape, BF16),
        scratch_shapes=[pltpu.VMEM((rows, 4 * modes_y, cells), BF16)],
        compiler_params=pltpu.CompilerParams(vmem_limit_bytes=48 * 2**20),
        name="tail",
    )(returned, field, by_back, local, depth_matrix(0), depth_matrix(1), flip)


def solution(mesh):
    placed = (P(("group", "lat"), None, None), P(), P(), P(), P(), P())
    return jax.shard_map(
        shards,
        mesh=mesh,
        in_specs=placed,
        out_specs=P(("group", "lat"), None, None),
        check_vma=False,
    )
```

```python
import functools
import math

import jax
import jax.numpy as jnp
import ml_dtypes
import numpy as np
from jax import lax
from jax.experimental import pallas as pl
from jax.experimental.pallas import tpu as pltpu
from jax.sharding import PartitionSpec as P


def cosine_basis(length, modes):
    order = jnp.arange(modes, dtype=jnp.float32)[:, None]
    place = jnp.arange(length, dtype=jnp.float32)[None, :]
    scales = jnp.where(order == 0.0, math.sqrt(1.0 / length), math.sqrt(2.0 / length))
    return jnp.cos(math.pi * order * (place + 0.5) / length) * scales


def row_tail(u_rows, spect, lat_local, depth_modes, depth_local, depth_basis):
    highest = lax.Precision.HIGHEST
    rows, width, cells = u_rows.shape
    chans = lat_local.shape[0]
    depth = cells // chans
    u4 = u_rows.reshape(rows, width, depth, chans)
    s4 = spect.reshape(rows, width, depth, chans)
    first = u4 + jax.nn.gelu(s4 + jnp.einsum("xyzc,cd->xyzd", u4, lat_local, precision=highest))
    dcoef = jnp.einsum("kz,xyzc->xykc", depth_basis, first, precision=highest)
    dmix = jnp.einsum("xykc,kcd->xykd", dcoef, depth_modes, precision=highest)
    dspect = jnp.einsum("kz,xykd->xyzd", depth_basis, dmix, precision=highest)
    final = first + jax.nn.gelu(
        dspect + jnp.einsum("xyzc,cd->xyzd", first, depth_local, precision=highest)
    )
    return final.reshape(rows, width, cells).astype(jnp.bfloat16)


def one_hot(ids, count):
    return (ids[:, None] == jnp.arange(count, dtype=jnp.int32)[None, :]).astype(jnp.float32)


def plain_shards(field, lat_modes, lat_gains, lat_local, depth_modes, depth_local):
    highest = lax.Precision.HIGHEST
    devices = lax.axis_size("lat")
    rows_dev, width_y, cells = field.shape
    modes_x, chans, _ = lat_modes.shape
    modes_y = lat_gains.shape[0]
    modes_z = depth_modes.shape[0]
    depth = cells // chans
    width_x = rows_dev * devices
    basis_x = cosine_basis(width_x, modes_x)
    basis_y = cosine_basis(width_y, modes_y)
    basis_z = cosine_basis(depth, modes_z)
    start = lax.axis_index("lat")
    u_rows = field.astype(jnp.float32)
    coef_y = jnp.einsum("qy,xyw->xqw", basis_y, u_rows, precision=highest)
    packed = coef_y.reshape(rows_dev, modes_y * cells)
    gathered = lax.all_to_all(packed, "lat", split_axis=1, concat_axis=0, tiled=True)
    span = gathered.shape[1]
    pairs = span // chans
    coef = jnp.dot(basis_x, gathered, precision=highest).reshape(modes_x, pairs, chans)
    mode_ids = (start * pairs + jnp.arange(pairs, dtype=jnp.int32)) // depth
    gain_rows = jnp.dot(one_hot(mode_ids, modes_y), lat_gains, precision=highest)
    mixed = jnp.einsum("jpc,jcd->jpd", coef * gain_rows[None, :, :], lat_modes, precision=highest)
    back_x = jnp.dot(basis_x.T, mixed.reshape(modes_x, span), precision=highest)
    returned = lax.all_to_all(back_x, "lat", split_axis=0, concat_axis=1, tiled=True)
    spect = jnp.einsum(
        "qy,xqw->xyw", basis_y, returned.reshape(rows_dev, modes_y, cells), precision=highest
    )
    return row_tail(u_rows, spect, lat_local, depth_modes, depth_local, basis_z)


BF16 = jnp.bfloat16
F32 = jnp.float32
LANE = 128
GROUP = 8
SPAN = 256
TANH_A = 2.0 * math.sqrt(2.0 / math.pi)
TANH_B = 8.0 * 0.044715 * math.sqrt(2.0 / math.pi)


def basis64(length, modes):
    order = np.arange(modes)[:, None]
    place = np.arange(length)[None, :]
    scales = np.where(order == 0, math.sqrt(1.0 / length), math.sqrt(2.0 / length))
    return np.cos(math.pi * order * (place + 0.5) / length) * scales


def split64(array):
    high = array.astype(ml_dtypes.bfloat16)
    return high, (array - high.astype(np.float64)).astype(ml_dtypes.bfloat16)


def split(array):
    high = array.astype(BF16)
    return high, (array - high.astype(F32)).astype(BF16)


def split_outside(array):
    high = lax.reduce_precision(array, 8, 7)
    return high.astype(BF16), (array - high).astype(BF16)


def window_modes(rows, length, modes):
    place = np.arange(rows) - (rows - 1) / 2
    order = np.arange(modes)[:, None]
    _, se, ve = np.linalg.svd(np.cos(math.pi * order * place / length))
    _, so, vo = np.linalg.svd(np.sin(math.pi * order * place / length))
    top = max(se[0], so[0])
    half = rows // 2
    count = max(int(np.sum(se[:half] > top * 2.0**-24)), int(np.sum(so[:half] > top * 2.0**-24)))
    fine = max(int(np.sum(se[:half] > top * 0.1)), int(np.sum(so[:half] > top * 0.1)))
    funcs = np.stack([ve[:count], vo[:count]], axis=1).reshape(2 * count, rows)
    return funcs, 2 * fine


def forward_kernel(funcs, fine, by_ref, near_ref, far_ref, o_ref, cy_ref, acc_ref):
    step = pl.program_id(0)
    pairs = near_ref.shape[0]
    steps = funcs.shape[1] // (2 * pairs)
    modes_y = by_ref.shape[0] // 2
    count = funcs.shape[0]
    halves = cy_ref.shape[2] // SPAN

    def compress(before):
        for g in range(modes_y // GROUP):
            rows = slice(g * GROUP, (g + 1) * GROUP)
            for c in range(halves * SPAN // LANE):
                lanes = slice(c * LANE, (c + 1) * LANE)
                totals = [None if before == 0 else acc_ref[j, rows, lanes] for j in range(count)]
                for r in range(pairs):
                    x, y = cy_ref[r, rows, lanes], cy_ref[pairs + r, rows, lanes]
                    pair = (x + y, x - y)
                    for j in range(count):
                        term = pair[j % 2] * float(funcs[j, before * pairs + r])
                        totals[j] = term if totals[j] is None else totals[j] + term
                if before < steps - 1:
                    for j in range(count):
                        acc_ref[j, rows, lanes] = totals[j]
                    continue
                h, k = divmod(c, SPAN // LANE)
                place = slice(k * LANE, (k + 1) * LANE)
                for j in range(0, count, 2):
                    high, low = split(jnp.concatenate(totals[j : j + 2], axis=0))
                    o_ref[g * halves + h, j * GROUP : (j + 2) * GROUP, place] = high
                    if j < fine:
                        at = (count + j) * GROUP
                        o_ref[g * halves + h, at : at + 2 * GROUP, place] = low

    def body(at):
        if at > 0:
            compress(at - 1)
        if at < steps:
            for r in range(pairs):
                for slot, row in ((r, near_ref[r]), (pairs + r, far_ref[pairs - 1 - r])):
                    z = jnp.dot(by_ref[...], row, preferred_element_type=F32)
                    cy_ref[slot] = z[:modes_y] + z[modes_y:]

    for at in range(steps + 1):
        pl.when(step == at)(functools.partial(body, at))


def mix_kernel(count, fine, r_ref, a_ref, b_ref, g_ref, w_ref, o_ref, m_ref, back_ref):
    devices, packed, span = r_ref.shape
    modes_x = w_ref.shape[1]
    depth = a_ref.shape[1]
    highs, lows = count * GROUP, fine * GROUP
    tiles = [(k, slice(k * LANE, (k + 1) * LANE)) for k in range(span // LANE)]
    for i in range(devices):
        got = r_ref[i].astype(F32)
        for k, lanes in tiles:
            m_ref[k, i * highs : i * highs + lows] = got[:lows, lanes] + got[highs:, lanes]
            m_ref[k, i * highs + lows : (i + 1) * highs] = got[lows:highs, lanes]
    if depth > devices * count:
        for k, _ in tiles:
            m_ref[k, devices * highs :] = jnp.zeros((depth * GROUP - devices * highs, LANE), F32)
    shifts = w_ref.shape[0]
    for q in range(GROUP):
        modes = [m_ref[k, pl.ds(q, depth, stride=GROUP), :] for k, _ in tiles]
        high, low = split(jnp.concatenate(modes, axis=1))
        z = jnp.dot(a_ref[...], jnp.concatenate([high, low], axis=1), preferred_element_type=F32)
        coef = z[:modes_x, :span] + z[modes_x:, :span] + z[:modes_x, span:]
        coef = coef * g_ref[q : q + 1, :]
        mixed = []
        for k, lanes in tiles:
            part = coef[:, lanes]
            total = part * w_ref[shifts // 2]
            for n in range(shifts):
                shift = n - shifts // 2
                if shift:
                    total = total + pltpu.roll(part, shift % LANE, 1) * w_ref[n]
            mixed.append(total)
        high, low = split(jnp.concatenate(mixed, axis=1))
        right = jnp.concatenate([high, high, low, low], axis=0)
        z = jnp.dot(b_ref[...], right, preferred_element_type=F32)
        for k, lanes in tiles:
            back_ref[k, pl.ds(q, devices * count, stride=GROUP), :] = z[:, lanes]
    for i in range(devices):
        for k, lanes in tiles:
            high, low = split(back_ref[k, i * highs : (i + 1) * highs])
            o_ref[i, :highs, lanes] = high
            o_ref[i, highs:, lanes] = low[:lows]


def expand(funcs, fine, r_ref, flip_ref, b_ref):
    count, rows = funcs.shape
    modes_y = b_ref.shape[1] // 4
    halves = b_ref.shape[2] // SPAN
    flip = flip_ref[...]

    def some(g, carry):
        at = pl.multiple_of(g * 2 * GROUP, 2 * GROUP)
        for h in range(halves):
            got = []
            for k in range(2):
                block = r_ref[(2 * g + k) * halves + h]
                turned = jnp.dot(block, flip, preferred_element_type=F32) if h else block.astype(F32)
                got.append(turned)
            for c in range(SPAN // LANE):
                part = slice(c * LANE, (c + 1) * LANE)
                modes = []
                for j in range(count):
                    pieces = []
                    for k in range(2):
                        piece = got[k][j * GROUP : (j + 1) * GROUP, part]
                        if j < fine:
                            low = got[k][(count + j) * GROUP : (count + j + 1) * GROUP, part]
                            piece = piece + low
                        pieces.append(piece)
                    modes.append(jnp.concatenate(pieces, axis=0))
                lanes = slice(h * SPAN + c * LANE, h * SPAN + (c + 1) * LANE)
                for t in range(rows // 2):
                    sums = []
                    for parity in range(2):
                        total = modes[parity] * float(0.5 * funcs[parity, t])
                        for j in range(parity + 2, count, 2):
                            total = total + modes[j] * float(0.5 * funcs[j, t])
                        sums.append(total)
                    for row, value in ((t, sums[0] + sums[1]), (rows - 1 - t, sums[0] - sums[1])):
                        high, low = split(value)
                        for n, half in enumerate((high, high, low, low)):
                            b_ref[row, pl.ds(at + n * modes_y, 2 * GROUP), lanes] = half
        return carry

    lax.fori_loop(0, modes_y // (2 * GROUP), some, 0)


def tail_kernel(funcs, fine, chunk, r_ref, u_ref, by_ref, l_ref, w_ref, flip_ref, o_ref, b_ref, *scratch):
    step = pl.program_id(0)
    last = pl.num_programs(0) - 1
    width = u_ref.shape[1]
    pre, seen, first, parts, post, done = (scratch[n : n + 2] for n in range(0, 12, 2))
    near, far = slice(0, SPAN), slice(SPAN, 2 * SPAN)
    chunks = [slice(y, y + chunk) for y in range(0, width, chunk)]

    def lateral_product(n):
        for h, lanes in enumerate((near, far)):
            u = u_ref[n, :, lanes]
            left = jnp.concatenate([by_ref[...], u, u], axis=1)
            right = jnp.concatenate([b_ref[2 * step + n, :, lanes], l_ref[h]], axis=0)
            pre[n][:, lanes] = jnp.dot(left, right, preferred_element_type=F32)
        seen[n][...] = jnp.dot(u, flip_ref[...], preferred_element_type=F32)

    def lateral_points(n):
        for ys in chunks:
            f0 = u_ref[n, ys, near].astype(F32) + twice_gelu(pre[n][ys, near])
            f1 = seen[n][ys] + twice_gelu(pre[n][ys, far])
            first[n][ys, near] = f0
            first[n][ys, far] = f1
            for m, value in enumerate((f0 + f1, f0 - f1)):
                high, low = split(value)
                parts[n][ys, 2 * m * SPAN : (2 * m + 1) * SPAN] = high
                parts[n][ys, (2 * m + 1) * SPAN : (2 * m + 2) * SPAN] = low

    def depth_product(n):
        for m, lanes in enumerate((near, far)):
            high = parts[n][:, 2 * m * SPAN : (2 * m + 1) * SPAN]
            low = parts[n][:, (2 * m + 1) * SPAN : (2 * m + 2) * SPAN]
            left = jnp.concatenate([high, low, high], axis=1)
            post[n][:, lanes] = jnp.dot(left, w_ref[m], preferred_element_type=F32)

    def depth_points(n):
        for ys in chunks:
            even, odd = post[n][ys, near], post[n][ys, far]
            o_ref[n, ys, near] = (first[n][ys, near] + twice_gelu(even + odd)).astype(BF16)
            done[n][ys] = (first[n][ys, far] + twice_gelu(even - odd)).astype(BF16)

    def finish(n):
        o_ref[n, :, far] = jnp.dot(done[n][...], flip_ref[...], preferred_element_type=F32).astype(BF16)

    @pl.when(step == 0)
    def _():
        expand(funcs, fine, r_ref, flip_ref, b_ref)
        lateral_product(0)
        lateral_product(1)
        lateral_points(0)
        depth_product(0)
        lateral_points(1)

    @pl.when(jnp.logical_and(step > 0, step < last))
    def _():
        depth_product(1)
        depth_points(0)
        lateral_product(0)
        depth_points(1)
        finish(0)
        lateral_product(1)
        lateral_points(0)
        finish(1)
        depth_product(0)
        lateral_points(1)

    @pl.when(step == last)
    def _():
        depth_product(1)
        depth_points(0)
        finish(0)
        depth_points(1)
        finish(1)


def twice_gelu(half):
    return half + half * jnp.tanh(half * (TANH_A + TANH_B * (half * half)))


def diagonals(matrices):
    p, n, _ = matrices.shape
    turned = jnp.pad(jnp.swapaxes(matrices, 1, 2)[:, :, ::-1], ((0, 0), (0, 0), (0, n)))
    skewed = turned.reshape(p, 2 * n * n)[:, : n * (2 * n - 1)].reshape(p, n, 2 * n - 1)
    return jnp.tile(jnp.transpose(skewed, (2, 0, 1)), (1, 1, LANE // n))


def kron_eye(matrix, count):
    *lead, n, m = matrix.shape
    eye = jnp.eye(count, dtype=matrix.dtype)
    return (eye[:, None, :, None] * matrix[..., None, :, None, :]).reshape(*lead, count * n, count * m)


def fits(mesh_lat, rows, width_y, cells, chans, modes_x, modes_y):
    return (
        cells == 2 * SPAN
        and SPAN % (LANE // chans * chans) == 0
        and mesh_lat * GROUP * SPAN == modes_y * cells
        and rows % 4 == 0
        and rows >= 16
        and width_y % 256 == 0
        and 4 * modes_y == SPAN
        and modes_x % 8 == 0
    )


def shards(field, lat_modes, lat_gains, lat_local, depth_modes, depth_local):
    highest = lax.Precision.HIGHEST
    devices = lax.axis_size("lat")
    rows, width_y, cells = field.shape
    modes_x, chans, _ = lat_modes.shape
    modes_y = lat_gains.shape[0]
    modes_z = depth_modes.shape[0]
    if not fits(devices, rows, width_y, cells, chans, modes_x, modes_y):
        return plain_shards(field, lat_modes, lat_gains, lat_local, depth_modes, depth_local)
    depth = cells // chans
    width_x = rows * devices
    basis_x = basis64(width_x, modes_x)
    basis_y = basis64(width_y, modes_y)
    basis_z = basis64(depth, modes_z)
    funcs, fine = window_modes(rows, width_x, modes_x)
    count = funcs.shape[0]
    packed = (count + fine) * GROUP
    halves = cells // SPAN
    me = lax.axis_index("lat")

    by_high, by_low = split64(basis_y)
    by_forward = np.concatenate([by_high, by_low], axis=0)
    pairs = 2
    steps = rows // (2 * pairs)
    sent = pl.pallas_call(
        functools.partial(forward_kernel, funcs, fine),
        grid=(steps + 1,),
        in_specs=[
            pl.BlockSpec((2 * modes_y, width_y), lambda s: (0, 0)),
            pl.BlockSpec((pairs, width_y, cells), lambda s: (jnp.minimum(s, steps - 1), 0, 0)),
            pl.BlockSpec((pairs, width_y, cells), lambda s: (2 * steps - 1 - jnp.minimum(s, steps - 1), 0, 0)),
        ],
        out_specs=pl.BlockSpec((devices, packed, SPAN), lambda s: (0, 0, 0)),
        out_shape=jax.ShapeDtypeStruct((devices, packed, SPAN), BF16),
        scratch_shapes=[
            pltpu.VMEM((2 * pairs, modes_y, cells), F32),
            pltpu.VMEM((count, modes_y, cells), F32),
        ],
        compiler_params=pltpu.CompilerParams(vmem_limit_bytes=48 * 2**20),
        name="forward",
    )(by_forward, field, field)
    gathered = lax.all_to_all(sent, "lat", split_axis=0, concat_axis=0, tiled=True)

    weights = np.einsum("pit,jt->pij", basis_x.reshape(modes_x, devices, rows), funcs)
    flat = weights.reshape(modes_x, devices * count)
    ah, al = split64(np.pad(flat, ((0, 0), (0, -flat.shape[1] % LANE))))
    a_forward = np.concatenate([ah, al], axis=0)
    bh, bl = split64(flat.T)
    a_back = np.concatenate([bh, bl, bh, bl], axis=1)
    gains = lax.dynamic_slice_in_dim(lat_gains, (me // halves) * GROUP, GROUP, axis=0)
    gains = jnp.tile(gains, (1, SPAN // chans))
    mixed = pl.pallas_call(
        functools.partial(mix_kernel, count, fine),
        out_shape=jax.ShapeDtypeStruct((devices, packed, SPAN), BF16),
        scratch_shapes=[
            pltpu.VMEM((SPAN // LANE, a_forward.shape[1] * GROUP, LANE), F32),
            pltpu.VMEM((SPAN // LANE, devices * count * GROUP, LANE), F32),
        ],
        compiler_params=pltpu.CompilerParams(vmem_limit_bytes=48 * 2**20),
        name="mix",
    )(gathered, a_forward, a_back, gains, diagonals(lat_modes))
    returned = lax.all_to_all(mixed, "lat", split_axis=0, concat_axis=0, tiled=True)

    by_back = np.concatenate([by_high, by_low, by_high, by_low], axis=0).T.copy()
    per = SPAN // chans
    flip = np.kron(np.eye(per)[::-1], np.eye(chans)).astype(ml_dtypes.bfloat16)
    local_high, local_low = split_outside(kron_eye(0.5 * lat_local, per))
    local = jnp.concatenate([local_high, local_low], axis=0)
    turned = local.reshape(2 * SPAN, per, chans)[:, ::-1].reshape(2 * SPAN, SPAN)
    local = jnp.stack([local, turned])
    near_z = basis_z[:, :per].astype(np.float32)

    def depth_matrix(parity):
        b = near_z[parity::2]
        full = 0.5 * jnp.einsum(
            "kz,kw,kcd->zcwd", b, b, depth_modes[parity::2], precision=highest
        ).reshape(SPAN, SPAN) + 0.25 * kron_eye(depth_local, per)
        high, low = split_outside(full)
        return jnp.concatenate([high, high, low], axis=0)

    wide = (width_y, cells)
    narrow = (width_y, SPAN)
    steps = rows // 2
    return pl.pallas_call(
        functools.partial(tail_kernel, funcs, fine, 64),
        grid=(steps + 1,),
        in_specs=[
            pl.BlockSpec((devices, packed, SPAN), lambda s: (0, 0, 0)),
            pl.BlockSpec((2, width_y, cells), lambda s: (jnp.minimum(s, steps - 1), 0, 0)),
            pl.BlockSpec((width_y, SPAN), lambda s: (0, 0)),
            pl.BlockSpec((2, 2 * SPAN, SPAN), lambda s: (0, 0, 0)),
            pl.BlockSpec((2, 3 * SPAN, SPAN), lambda s: (0, 0, 0)),
            pl.BlockSpec((SPAN, SPAN), lambda s: (0, 0)),
        ],
        out_specs=pl.BlockSpec((2, width_y, cells), lambda s: (jnp.maximum(s - 1, 0), 0, 0)),
        out_shape=jax.ShapeDtypeStruct(field.shape, BF16),
        scratch_shapes=[pltpu.VMEM((rows, 4 * modes_y, cells), BF16)]
        + 2 * [pltpu.VMEM(wide, F32)]
        + 2 * [pltpu.VMEM(narrow, F32)]
        + 2 * [pltpu.VMEM(wide, F32)]
        + 2 * [pltpu.VMEM((width_y, 4 * SPAN), BF16)]
        + 2 * [pltpu.VMEM(wide, F32)]
        + 2 * [pltpu.VMEM(narrow, BF16)],
        compiler_params=pltpu.CompilerParams(vmem_limit_bytes=52 * 2**20),
        name="tail",
    )(returned, field, by_back, local, jnp.stack([depth_matrix(0), depth_matrix(1)]), flip)


def solution(mesh):
    placed = (P(("group", "lat"), None, None), P(), P(), P(), P(), P())
    return jax.shard_map(
        shards,
        mesh=mesh,
        in_specs=placed,
        out_specs=P(("group", "lat"), None, None),
        check_vma=False,
    )
```

```python
import functools
import math

import jax
import jax.numpy as jnp
import ml_dtypes
import numpy as np
from jax import lax
from jax.experimental import pallas as pl
from jax.experimental.pallas import tpu as pltpu
from jax.sharding import PartitionSpec as P


def cosine_basis(length, modes):
    order = jnp.arange(modes, dtype=jnp.float32)[:, None]
    place = jnp.arange(length, dtype=jnp.float32)[None, :]
    scales = jnp.where(order == 0.0, math.sqrt(1.0 / length), math.sqrt(2.0 / length))
    return jnp.cos(math.pi * order * (place + 0.5) / length) * scales


def row_tail(u_rows, spect, lat_local, depth_modes, depth_local, depth_basis):
    highest = lax.Precision.HIGHEST
    rows, width, cells = u_rows.shape
    chans = lat_local.shape[0]
    depth = cells // chans
    u4 = u_rows.reshape(rows, width, depth, chans)
    s4 = spect.reshape(rows, width, depth, chans)
    first = u4 + jax.nn.gelu(s4 + jnp.einsum("xyzc,cd->xyzd", u4, lat_local, precision=highest))
    dcoef = jnp.einsum("kz,xyzc->xykc", depth_basis, first, precision=highest)
    dmix = jnp.einsum("xykc,kcd->xykd", dcoef, depth_modes, precision=highest)
    dspect = jnp.einsum("kz,xykd->xyzd", depth_basis, dmix, precision=highest)
    final = first + jax.nn.gelu(
        dspect + jnp.einsum("xyzc,cd->xyzd", first, depth_local, precision=highest)
    )
    return final.reshape(rows, width, cells).astype(jnp.bfloat16)


def one_hot(ids, count):
    return (ids[:, None] == jnp.arange(count, dtype=jnp.int32)[None, :]).astype(jnp.float32)


def plain_shards(field, lat_modes, lat_gains, lat_local, depth_modes, depth_local):
    highest = lax.Precision.HIGHEST
    devices = lax.axis_size("lat")
    rows_dev, width_y, cells = field.shape
    modes_x, chans, _ = lat_modes.shape
    modes_y = lat_gains.shape[0]
    modes_z = depth_modes.shape[0]
    depth = cells // chans
    width_x = rows_dev * devices
    basis_x = cosine_basis(width_x, modes_x)
    basis_y = cosine_basis(width_y, modes_y)
    basis_z = cosine_basis(depth, modes_z)
    start = lax.axis_index("lat")
    u_rows = field.astype(jnp.float32)
    coef_y = jnp.einsum("qy,xyw->xqw", basis_y, u_rows, precision=highest)
    packed = coef_y.reshape(rows_dev, modes_y * cells)
    gathered = lax.all_to_all(packed, "lat", split_axis=1, concat_axis=0, tiled=True)
    span = gathered.shape[1]
    pairs = span // chans
    coef = jnp.dot(basis_x, gathered, precision=highest).reshape(modes_x, pairs, chans)
    mode_ids = (start * pairs + jnp.arange(pairs, dtype=jnp.int32)) // depth
    gain_rows = jnp.dot(one_hot(mode_ids, modes_y), lat_gains, precision=highest)
    mixed = jnp.einsum("jpc,jcd->jpd", coef * gain_rows[None, :, :], lat_modes, precision=highest)
    back_x = jnp.dot(basis_x.T, mixed.reshape(modes_x, span), precision=highest)
    returned = lax.all_to_all(back_x, "lat", split_axis=0, concat_axis=1, tiled=True)
    spect = jnp.einsum(
        "qy,xqw->xyw", basis_y, returned.reshape(rows_dev, modes_y, cells), precision=highest
    )
    return row_tail(u_rows, spect, lat_local, depth_modes, depth_local, basis_z)


BF16 = jnp.bfloat16
F32 = jnp.float32
LANE = 128
GROUP = 8
SPAN = 256
TANH_A = 2.0 * math.sqrt(2.0 / math.pi)
TANH_B = 8.0 * 0.044715 * math.sqrt(2.0 / math.pi)


def basis64(length, modes):
    order = np.arange(modes)[:, None]
    place = np.arange(length)[None, :]
    scales = np.where(order == 0, math.sqrt(1.0 / length), math.sqrt(2.0 / length))
    return np.cos(math.pi * order * (place + 0.5) / length) * scales


def split64(array):
    high = array.astype(ml_dtypes.bfloat16)
    return high, (array - high.astype(np.float64)).astype(ml_dtypes.bfloat16)


def split(array):
    high = array.astype(BF16)
    return high, (array - high.astype(F32)).astype(BF16)


def split_outside(array):
    high = lax.reduce_precision(array, 8, 7)
    return high.astype(BF16), (array - high).astype(BF16)


def window_modes(rows, length, modes):
    place = np.arange(rows) - (rows - 1) / 2
    order = np.arange(modes)[:, None]
    _, se, ve = np.linalg.svd(np.cos(math.pi * order * place / length))
    _, so, vo = np.linalg.svd(np.sin(math.pi * order * place / length))
    top = max(se[0], so[0])
    half = rows // 2
    count = max(int(np.sum(se[:half] > top * 2.0**-24)), int(np.sum(so[:half] > top * 2.0**-24)))
    fine = max(int(np.sum(se[:half] > top * 0.1)), int(np.sum(so[:half] > top * 0.1)))
    funcs = np.stack([ve[:count], vo[:count]], axis=1).reshape(2 * count, rows)
    return funcs, 2 * fine


def forward_kernel(funcs, fine, by_ref, near_ref, far_ref, o_ref, cy_ref, acc_ref):
    step = pl.program_id(0)
    pairs = near_ref.shape[0]
    steps = funcs.shape[1] // (2 * pairs)
    modes_y = by_ref.shape[0] // 2
    count = funcs.shape[0]
    halves = cy_ref.shape[2] // SPAN

    def compress(before):
        for g in range(modes_y // GROUP):
            rows = slice(g * GROUP, (g + 1) * GROUP)
            for c in range(halves * SPAN // LANE):
                lanes = slice(c * LANE, (c + 1) * LANE)
                totals = [None if before == 0 else acc_ref[j, rows, lanes] for j in range(count)]
                for r in range(pairs):
                    x, y = cy_ref[r, rows, lanes], cy_ref[pairs + r, rows, lanes]
                    pair = (x + y, x - y)
                    for j in range(count):
                        term = pair[j % 2] * float(funcs[j, before * pairs + r])
                        totals[j] = term if totals[j] is None else totals[j] + term
                if before < steps - 1:
                    for j in range(count):
                        acc_ref[j, rows, lanes] = totals[j]
                    continue
                h, k = divmod(c, SPAN // LANE)
                place = slice(k * LANE, (k + 1) * LANE)
                for j in range(0, count, 2):
                    high, low = split(jnp.concatenate(totals[j : j + 2], axis=0))
                    o_ref[g * halves + h, j * GROUP : (j + 2) * GROUP, place] = high
                    if j < fine:
                        at = (count + j) * GROUP
                        o_ref[g * halves + h, at : at + 2 * GROUP, place] = low

    def body(at):
        if at > 0:
            compress(at - 1)
        if at < steps:
            for r in range(pairs):
                for slot, row in ((r, near_ref[r]), (pairs + r, far_ref[pairs - 1 - r])):
                    z = jnp.dot(by_ref[...], row, preferred_element_type=F32)
                    cy_ref[slot] = z[:modes_y] + z[modes_y:]

    for at in range(steps + 1):
        pl.when(step == at)(functools.partial(body, at))


def mix_kernel(count, fine, r_ref, a_ref, b_ref, g_ref, w_ref, order_ref, o_ref, m_ref, back_ref):
    devices, packed, span = r_ref.shape
    modes_x = w_ref.shape[1]
    depth = a_ref.shape[1]
    highs, lows = count * GROUP, fine * GROUP
    tiles = [(k, slice(k * LANE, (k + 1) * LANE)) for k in range(span // LANE)]
    for i in range(devices):
        got = jnp.dot(r_ref[i], order_ref[...], preferred_element_type=F32)
        for k, lanes in tiles:
            m_ref[k, i * highs : i * highs + lows] = got[:lows, lanes] + got[highs:, lanes]
            m_ref[k, i * highs + lows : (i + 1) * highs] = got[lows:highs, lanes]
    if depth > devices * count:
        for k, _ in tiles:
            m_ref[k, devices * highs :] = jnp.zeros((depth * GROUP - devices * highs, LANE), F32)
    shifts = w_ref.shape[0]
    for q in range(GROUP):
        modes = [m_ref[k, pl.ds(q, depth, stride=GROUP), :] for k, _ in tiles]
        high, low = split(jnp.concatenate(modes, axis=1))
        z = jnp.dot(a_ref[...], jnp.concatenate([high, low], axis=1), preferred_element_type=F32)
        coef = z[:modes_x, :span] + z[modes_x:, :span] + z[:modes_x, span:]
        coef = coef * g_ref[q : q + 1, :]
        mixed = []
        for k, lanes in tiles:
            part = coef[:, lanes]
            total = part * w_ref[0]
            for n in range(1, shifts):
                total = total + pltpu.roll(part, n * (LANE // shifts), 1) * w_ref[n]
            mixed.append(total)
        high, low = split(jnp.concatenate(mixed, axis=1))
        right = jnp.concatenate([high, high, low, low], axis=0)
        z = jnp.dot(b_ref[...], right, preferred_element_type=F32)
        for k, lanes in tiles:
            back_ref[k, pl.ds(q, devices * count, stride=GROUP), :] = z[:, lanes]
    for i in range(devices):
        for k, lanes in tiles:
            high, low = split(back_ref[k, i * highs : (i + 1) * highs])
            o_ref[i, :highs, lanes] = high
            o_ref[i, highs:, lanes] = low[:lows]


def expand(funcs, fine, r_ref, place_ref, b_ref):
    count, rows = funcs.shape
    modes_y = b_ref.shape[1] // 4
    halves = b_ref.shape[2] // SPAN

    def some(g, carry):
        at = pl.multiple_of(g * 2 * GROUP, 2 * GROUP)
        for h in range(halves):
            got = []
            for k in range(2):
                block = r_ref[(2 * g + k) * halves + h]
                got.append(jnp.dot(block, place_ref[h], preferred_element_type=F32))
            for c in range(SPAN // LANE):
                part = slice(c * LANE, (c + 1) * LANE)
                modes = []
                for j in range(count):
                    pieces = []
                    for k in range(2):
                        piece = got[k][j * GROUP : (j + 1) * GROUP, part]
                        if j < fine:
                            low = got[k][(count + j) * GROUP : (count + j + 1) * GROUP, part]
                            piece = piece + low
                        pieces.append(piece)
                    modes.append(jnp.concatenate(pieces, axis=0))
                lanes = slice(h * SPAN + c * LANE, h * SPAN + (c + 1) * LANE)
                for t in range(rows // 2):
                    sums = []
                    for parity in range(2):
                        total = modes[parity] * float(0.5 * funcs[parity, t])
                        for j in range(parity + 2, count, 2):
                            total = total + modes[j] * float(0.5 * funcs[j, t])
                        sums.append(total)
                    for row, value in ((t, sums[0] + sums[1]), (rows - 1 - t, sums[0] - sums[1])):
                        high, low = split(value)
                        for n, half in enumerate((high, high, low, low)):
                            b_ref[row, pl.ds(at + n * modes_y, 2 * GROUP), lanes] = half
        return carry

    lax.fori_loop(0, modes_y // (2 * GROUP), some, 0)


def local_kernel(u_ref, l_ref, flip_ref, x_ref, f_ref):
    rows, width, _ = u_ref.shape
    for h in range(2):
        lanes = slice(h * SPAN, (h + 1) * SPAN)
        u = u_ref[:, :, lanes].reshape(rows * width, SPAN)
        x = jnp.dot(jnp.concatenate([u, u], axis=1), l_ref[h], preferred_element_type=F32)
        x_ref[:, :, lanes] = x.reshape(rows, width, SPAN)
    f = jnp.dot(u, flip_ref[...], preferred_element_type=F32)
    f_ref[...] = f.astype(BF16).reshape(rows, width, SPAN)


def weave(one, other):
    done = 0
    for n, step in enumerate(one):
        step()
        until = len(other) * (n + 1) // len(one)
        for at in range(done, until):
            other[at]()
        done = until


def tail_kernel(funcs, fine, chunk, r_ref, x_ref, u_ref, f_ref, by_ref, w_ref, place_ref, flip_ref, o_ref, b_ref, *scratch):
    step = pl.program_id(0)
    last = pl.num_programs(0) - 1
    width = u_ref.shape[1]
    pre, first, parts, post, done = (scratch[n : n + 2] for n in range(0, 10, 2))
    near, far = slice(0, SPAN), slice(SPAN, 2 * SPAN)
    pieces = [(r, y) for r in range(2) for y in range(0, width, chunk)]

    def lateral_product(n):
        def piece(r, lanes):
            right = b_ref[4 * step + 2 * n + r, :, lanes]
            z = jnp.dot(by_ref[...], right, preferred_element_type=F32)
            pre[n][r * width : (r + 1) * width, lanes] = z

        return [functools.partial(piece, r, lanes) for r in range(2) for lanes in (near, far)]

    def lateral_points(n):
        def piece(r, y):
            at, ys = slice(r * width + y, r * width + y + chunk), slice(y, y + chunk)
            f0 = u_ref[2 * n + r, ys].astype(F32) + twice_gelu(pre[n][at, near] + x_ref[2 * n + r, ys, near])
            f1 = f_ref[2 * n + r, ys].astype(F32) + twice_gelu(pre[n][at, far] + x_ref[2 * n + r, ys, far])
            first[n][at, near] = f0
            first[n][at, far] = f1
            for m, value in enumerate((f0 + f1, f0 - f1)):
                high, low = split(value)
                parts[n][at, 2 * m * SPAN : (2 * m + 1) * SPAN] = high
                parts[n][at, (2 * m + 1) * SPAN : (2 * m + 2) * SPAN] = low

        return [functools.partial(piece, r, y) for r, y in pieces]

    def depth_product(n):
        def piece(m, lanes):
            high = parts[n][:, 2 * m * SPAN : (2 * m + 1) * SPAN]
            low = parts[n][:, (2 * m + 1) * SPAN : (2 * m + 2) * SPAN]
            left = jnp.concatenate([high, low, high], axis=1)
            post[n][:, lanes] = jnp.dot(left, w_ref[m], preferred_element_type=F32)

        return [functools.partial(piece, m, lanes) for m, lanes in enumerate((near, far))]

    def depth_points(n):
        def piece(r, y):
            at, ys = slice(r * width + y, r * width + y + chunk), slice(y, y + chunk)
            even, odd = post[n][at, near], post[n][at, far]
            o_ref[2 * n + r, ys, near] = (first[n][at, near] + twice_gelu(even + odd)).astype(BF16)
            done[n][at] = (first[n][at, far] + twice_gelu(even - odd)).astype(BF16)

        return [functools.partial(piece, r, y) for r, y in pieces]

    def finish(n):
        def piece():
            z = jnp.dot(done[n][...], flip_ref[...], preferred_element_type=F32).astype(BF16)
            o_ref[2 * n : 2 * n + 2, :, far] = z.reshape(2, width, SPAN)

        return [piece]

    @pl.when(step == 0)
    def _():
        expand(funcs, fine, r_ref, place_ref, b_ref)
        weave(lateral_product(0), [])
        weave(lateral_product(1), lateral_points(0))
        weave(depth_product(0), lateral_points(1))

    @pl.when(jnp.logical_and(step > 0, step < last))
    def _():
        weave(depth_product(1), depth_points(0))
        weave(lateral_product(0) + finish(0), depth_points(1))
        weave(lateral_product(1) + finish(1), lateral_points(0))
        weave(depth_product(0), lateral_points(1))

    @pl.when(step == last)
    def _():
        weave(depth_product(1), depth_points(0))
        weave(finish(0), depth_points(1))
        weave(finish(1), [])


def twice_gelu(half):
    return half + half * jnp.tanh(half * (TANH_A + TANH_B * (half * half)))


def diagonals(matrices):
    n = matrices.shape[1]
    ids = np.arange(n)
    picks = (ids[None, :, None] == (ids[None, None, :] - ids[:, None, None]) % n).astype(np.float32)
    rows = jnp.sum(matrices[None] * picks[:, None], axis=2)
    return jnp.repeat(rows, LANE // n, axis=2)


def kron_eye(matrix, count):
    *lead, n, m = matrix.shape
    eye = jnp.eye(count, dtype=matrix.dtype)
    return (eye[:, None, :, None] * matrix[..., None, :, None, :]).reshape(*lead, count * n, count * m)


def fits(mesh_lat, rows, width_y, cells, chans, modes_x, modes_y):
    return (
        cells == 2 * SPAN
        and SPAN % (LANE // chans * chans) == 0
        and mesh_lat * GROUP * SPAN == modes_y * cells
        and rows % 4 == 0
        and rows >= 16
        and width_y % 256 == 0
        and 4 * modes_y == SPAN
        and modes_x % 8 == 0
    )


def shards(field, lat_modes, lat_gains, lat_local, depth_modes, depth_local):
    highest = lax.Precision.HIGHEST
    devices = lax.axis_size("lat")
    rows, width_y, cells = field.shape
    modes_x, chans, _ = lat_modes.shape
    modes_y = lat_gains.shape[0]
    modes_z = depth_modes.shape[0]
    if not fits(devices, rows, width_y, cells, chans, modes_x, modes_y):
        return plain_shards(field, lat_modes, lat_gains, lat_local, depth_modes, depth_local)
    depth = cells // chans
    width_x = rows * devices
    basis_x = basis64(width_x, modes_x)
    basis_y = basis64(width_y, modes_y)
    basis_z = basis64(depth, modes_z)
    funcs, fine = window_modes(rows, width_x, modes_x)
    count = funcs.shape[0]
    packed = (count + fine) * GROUP
    halves = cells // SPAN
    me = lax.axis_index("lat")

    by_high, by_low = split64(basis_y)
    by_forward = np.concatenate([by_high, by_low], axis=0)
    pairs = 2
    steps = rows // (2 * pairs)
    sent = pl.pallas_call(
        functools.partial(forward_kernel, funcs, fine),
        grid=(steps + 1,),
        in_specs=[
            pl.BlockSpec((2 * modes_y, width_y), lambda s: (0, 0)),
            pl.BlockSpec((pairs, width_y, cells), lambda s: (jnp.minimum(s, steps - 1), 0, 0)),
            pl.BlockSpec((pairs, width_y, cells), lambda s: (2 * steps - 1 - jnp.minimum(s, steps - 1), 0, 0)),
        ],
        out_specs=pl.BlockSpec((devices, packed, SPAN), lambda s: (0, 0, 0)),
        out_shape=jax.ShapeDtypeStruct((devices, packed, SPAN), BF16),
        scratch_shapes=[
            pltpu.VMEM((2 * pairs, modes_y, cells), F32),
            pltpu.VMEM((count, modes_y, cells), F32),
        ],
        compiler_params=pltpu.CompilerParams(vmem_limit_bytes=48 * 2**20),
        name="forward",
    )(by_forward, field, field)
    gathered = lax.all_to_all(sent, "lat", split_axis=0, concat_axis=0, tiled=True)

    per = SPAN // chans
    flip = np.kron(np.eye(per)[::-1], np.eye(chans)).astype(ml_dtypes.bfloat16)
    local_high, local_low = split_outside(kron_eye(0.5 * lat_local, per))
    local = jnp.concatenate([local_high, local_low], axis=0)
    turned = local.reshape(2 * SPAN, per, chans)[:, ::-1].reshape(2 * SPAN, SPAN)
    four = 4
    local_part, mirrored = pl.pallas_call(
        local_kernel,
        grid=(rows // four,),
        in_specs=[
            pl.BlockSpec((four, width_y, cells), lambda s: (s, 0, 0)),
            pl.BlockSpec((2, 2 * SPAN, SPAN), lambda s: (0, 0, 0)),
            pl.BlockSpec((SPAN, SPAN), lambda s: (0, 0)),
        ],
        out_specs=[
            pl.BlockSpec((four, width_y, cells), lambda s: (s, 0, 0)),
            pl.BlockSpec((four, width_y, SPAN), lambda s: (s, 0, 0)),
        ],
        out_shape=[
            jax.ShapeDtypeStruct(field.shape, F32),
            jax.ShapeDtypeStruct((rows, width_y, SPAN), BF16),
        ],
        compiler_params=pltpu.CompilerParams(vmem_limit_bytes=48 * 2**20),
        name="local",
    )(field, jnp.stack([local, turned]), flip)

    weights = np.einsum("pit,jt->pij", basis_x.reshape(modes_x, devices, rows), funcs)
    flat = weights.reshape(modes_x, devices * count)
    ah, al = split64(np.pad(flat, ((0, 0), (0, -flat.shape[1] % LANE))))
    a_forward = np.concatenate([ah, al], axis=0)
    bh, bl = split64(flat.T)
    a_back = np.concatenate([bh, bl, bh, bl], axis=1)
    gains = lax.dynamic_slice_in_dim(lat_gains, (me // halves) * GROUP, GROUP, axis=0)
    gains = jnp.tile(jnp.repeat(gains, LANE // chans, axis=1), (1, SPAN // LANE))
    per_lane = LANE // chans
    ids = np.arange(LANE)
    order = np.zeros((LANE, LANE))
    order[ids, ids % chans * per_lane + ids // chans] = 1
    order = np.kron(np.eye(SPAN // LANE), order).astype(ml_dtypes.bfloat16)
    mixed = pl.pallas_call(
        functools.partial(mix_kernel, count, fine),
        out_shape=jax.ShapeDtypeStruct((devices, packed, SPAN), BF16),
        scratch_shapes=[
            pltpu.VMEM((SPAN // LANE, a_forward.shape[1] * GROUP, LANE), F32),
            pltpu.VMEM((SPAN // LANE, devices * count * GROUP, LANE), F32),
        ],
        compiler_params=pltpu.CompilerParams(vmem_limit_bytes=48 * 2**20),
        name="mix",
    )(gathered, a_forward, a_back, gains, diagonals(lat_modes), order)
    returned = lax.all_to_all(mixed, "lat", split_axis=0, concat_axis=0, tiled=True)

    by_back = np.concatenate([by_high, by_low, by_high, by_low], axis=0).T.copy()
    near_z = basis_z[:, :per].astype(np.float32)

    def depth_matrix(parity):
        b = near_z[parity::2]
        full = 0.5 * jnp.einsum(
            "kz,kw,kcd->zcwd", b, b, depth_modes[parity::2], precision=highest
        ).reshape(SPAN, SPAN) + 0.25 * kron_eye(depth_local, per)
        high, low = split_outside(full)
        return jnp.concatenate([high, high, low], axis=0)

    place = np.stack([order.T, order.T @ flip])
    wide = (2 * width_y, cells)
    narrow = (2 * width_y, SPAN)
    steps = rows // four
    return pl.pallas_call(
        functools.partial(tail_kernel, funcs, fine, 64),
        grid=(steps + 1,),
        in_specs=[
            pl.BlockSpec((devices, packed, SPAN), lambda s: (0, 0, 0)),
            pl.BlockSpec((four, width_y, cells), lambda s: (jnp.minimum(s, steps - 1), 0, 0)),
            pl.BlockSpec((four, width_y, SPAN), lambda s: (jnp.minimum(s, steps - 1), 0, 0)),
            pl.BlockSpec((four, width_y, SPAN), lambda s: (jnp.minimum(s, steps - 1), 0, 0)),
            pl.BlockSpec((width_y, SPAN), lambda s: (0, 0)),
            pl.BlockSpec((2, 3 * SPAN, SPAN), lambda s: (0, 0, 0)),
            pl.BlockSpec((2, SPAN, SPAN), lambda s: (0, 0, 0)),
            pl.BlockSpec((SPAN, SPAN), lambda s: (0, 0)),
        ],
        out_specs=pl.BlockSpec((four, width_y, cells), lambda s: (jnp.maximum(s - 1, 0), 0, 0)),
        out_shape=jax.ShapeDtypeStruct(field.shape, BF16),
        scratch_shapes=[pltpu.VMEM((rows, 4 * modes_y, cells), BF16)]
        + 2 * [pltpu.VMEM(wide, F32)]
        + 2 * [pltpu.VMEM(wide, F32)]
        + 2 * [pltpu.VMEM((2 * width_y, 4 * SPAN), BF16)]
        + 2 * [pltpu.VMEM(wide, F32)]
        + 2 * [pltpu.VMEM(narrow, BF16)],
        compiler_params=pltpu.CompilerParams(vmem_limit_bytes=58 * 2**20),
        name="tail",
    )(
        returned,
        local_part,
        field,
        mirrored,
        by_back,
        jnp.stack([depth_matrix(0), depth_matrix(1)]),
        place,
        flip,
    )


def solution(mesh):
    placed = (P(("group", "lat"), None, None), P(), P(), P(), P(), P())
    return jax.shard_map(
        shards,
        mesh=mesh,
        in_specs=placed,
        out_specs=P(("group", "lat"), None, None),
        check_vma=False,
    )
```

```python
import functools
import math

import jax
import jax.numpy as jnp
import ml_dtypes
import numpy as np
from jax import lax
from jax.experimental import pallas as pl
from jax.experimental.pallas import tpu as pltpu
from jax.sharding import PartitionSpec as P


def cosine_basis(length, modes):
    order = jnp.arange(modes, dtype=jnp.float32)[:, None]
    place = jnp.arange(length, dtype=jnp.float32)[None, :]
    scales = jnp.where(order == 0.0, math.sqrt(1.0 / length), math.sqrt(2.0 / length))
    return jnp.cos(math.pi * order * (place + 0.5) / length) * scales


def row_tail(u_rows, spect, lat_local, depth_modes, depth_local, depth_basis):
    highest = lax.Precision.HIGHEST
    rows, width, cells = u_rows.shape
    chans = lat_local.shape[0]
    depth = cells // chans
    u4 = u_rows.reshape(rows, width, depth, chans)
    s4 = spect.reshape(rows, width, depth, chans)
    first = u4 + jax.nn.gelu(s4 + jnp.einsum("xyzc,cd->xyzd", u4, lat_local, precision=highest))
    dcoef = jnp.einsum("kz,xyzc->xykc", depth_basis, first, precision=highest)
    dmix = jnp.einsum("xykc,kcd->xykd", dcoef, depth_modes, precision=highest)
    dspect = jnp.einsum("kz,xykd->xyzd", depth_basis, dmix, precision=highest)
    final = first + jax.nn.gelu(
        dspect + jnp.einsum("xyzc,cd->xyzd", first, depth_local, precision=highest)
    )
    return final.reshape(rows, width, cells).astype(jnp.bfloat16)


def one_hot(ids, count):
    return (ids[:, None] == jnp.arange(count, dtype=jnp.int32)[None, :]).astype(jnp.float32)


def plain_shards(field, lat_modes, lat_gains, lat_local, depth_modes, depth_local):
    highest = lax.Precision.HIGHEST
    devices = lax.axis_size("lat")
    rows_dev, width_y, cells = field.shape
    modes_x, chans, _ = lat_modes.shape
    modes_y = lat_gains.shape[0]
    modes_z = depth_modes.shape[0]
    depth = cells // chans
    width_x = rows_dev * devices
    basis_x = cosine_basis(width_x, modes_x)
    basis_y = cosine_basis(width_y, modes_y)
    basis_z = cosine_basis(depth, modes_z)
    start = lax.axis_index("lat")
    u_rows = field.astype(jnp.float32)
    coef_y = jnp.einsum("qy,xyw->xqw", basis_y, u_rows, precision=highest)
    packed = coef_y.reshape(rows_dev, modes_y * cells)
    gathered = lax.all_to_all(packed, "lat", split_axis=1, concat_axis=0, tiled=True)
    span = gathered.shape[1]
    pairs = span // chans
    coef = jnp.dot(basis_x, gathered, precision=highest).reshape(modes_x, pairs, chans)
    mode_ids = (start * pairs + jnp.arange(pairs, dtype=jnp.int32)) // depth
    gain_rows = jnp.dot(one_hot(mode_ids, modes_y), lat_gains, precision=highest)
    mixed = jnp.einsum("jpc,jcd->jpd", coef * gain_rows[None, :, :], lat_modes, precision=highest)
    back_x = jnp.dot(basis_x.T, mixed.reshape(modes_x, span), precision=highest)
    returned = lax.all_to_all(back_x, "lat", split_axis=0, concat_axis=1, tiled=True)
    spect = jnp.einsum(
        "qy,xqw->xyw", basis_y, returned.reshape(rows_dev, modes_y, cells), precision=highest
    )
    return row_tail(u_rows, spect, lat_local, depth_modes, depth_local, basis_z)


BF16 = jnp.bfloat16
F32 = jnp.float32
LANE = 128
GROUP = 8
SPAN = 256
TANH_A = 2.0 * math.sqrt(2.0 / math.pi)
TANH_B = 8.0 * 0.044715 * math.sqrt(2.0 / math.pi)


def basis64(length, modes):
    order = np.arange(modes)[:, None]
    place = np.arange(length)[None, :]
    scales = np.where(order == 0, math.sqrt(1.0 / length), math.sqrt(2.0 / length))
    return np.cos(math.pi * order * (place + 0.5) / length) * scales


def split64(array):
    high = array.astype(ml_dtypes.bfloat16)
    return high, (array - high.astype(np.float64)).astype(ml_dtypes.bfloat16)


def split(array):
    high = array.astype(BF16)
    return high, (array - high.astype(F32)).astype(BF16)


def split_outside(array):
    high = lax.reduce_precision(array, 8, 7)
    return high.astype(BF16), (array - high).astype(BF16)


def window_modes(rows, length, modes):
    place = np.arange(rows) - (rows - 1) / 2
    order = np.arange(modes)[:, None]
    _, se, ve = np.linalg.svd(np.cos(math.pi * order * place / length))
    _, so, vo = np.linalg.svd(np.sin(math.pi * order * place / length))
    top = max(se[0], so[0])
    both = sorted([(-w, 2 * n) for n, w in enumerate(se[: rows // 2])] + [(-w, 2 * n + 1) for n, w in enumerate(so[: rows // 2])])
    weights = np.array([-w for w, _ in both])
    count = int(np.sum(weights > top * 2.0**-23))
    fine = int(np.sum(weights > top * 0.25))
    fine += (count + fine) % 2
    funcs = np.stack([ve[: rows // 2], vo[: rows // 2]], axis=1).reshape(rows // 2 * 2, rows)
    assert [n for _, n in both[:count]] == list(range(count))
    return funcs[:count], fine


def forward_kernel(funcs, fine, by_ref, near_ref, far_ref, o_ref, cy_ref, acc_ref):
    step = pl.program_id(0)
    pairs = near_ref.shape[0]
    steps = funcs.shape[1] // (2 * pairs)
    modes_y = by_ref.shape[0] // 2
    count = funcs.shape[0]
    halves = cy_ref.shape[2] // SPAN

    def compress(before):
        for g in range(modes_y // GROUP):
            rows = slice(g * GROUP, (g + 1) * GROUP)
            for c in range(halves * SPAN // LANE):
                lanes = slice(c * LANE, (c + 1) * LANE)
                totals = [None if before == 0 else acc_ref[j, rows, lanes] for j in range(count)]
                for r in range(pairs):
                    x, y = cy_ref[r, rows, lanes], cy_ref[pairs + r, rows, lanes]
                    pair = (x + y, x - y)
                    for j in range(count):
                        term = pair[j % 2] * float(funcs[j, before * pairs + r])
                        totals[j] = term if totals[j] is None else totals[j] + term
                if before < steps - 1:
                    for j in range(count):
                        acc_ref[j, rows, lanes] = totals[j]
                    continue
                h, k = divmod(c, SPAN // LANE)
                place = slice(k * LANE, (k + 1) * LANE)
                slots = [total.astype(BF16).astype(F32) for total in totals]
                slots += [totals[j] - slots[j] for j in range(fine)]
                for j in range(0, count + fine, 2):
                    two = jnp.concatenate(slots[j : j + 2], axis=0).astype(BF16)
                    o_ref[g * halves + h, j * GROUP : (j + 2) * GROUP, place] = two

    def body(at):
        if at > 0:
            compress(at - 1)
        if at < steps:
            for r in range(pairs):
                for slot, row in ((r, near_ref[r]), (pairs + r, far_ref[pairs - 1 - r])):
                    z = jnp.dot(by_ref[...], row, preferred_element_type=F32)
                    cy_ref[slot] = z[:modes_y] + z[modes_y:]

    for at in range(steps + 1):
        pl.when(step == at)(functools.partial(body, at))


def mix_kernel(count, fine, r_ref, a_ref, b_ref, g_ref, w_ref, order_ref, after_ref, o_ref, m_ref, back_ref):
    devices, packed, span = r_ref.shape
    modes_x = w_ref.shape[1]
    depth = a_ref.shape[1]
    highs, lows = count * GROUP, fine * GROUP
    tiles = [(k, slice(k * LANE, (k + 1) * LANE)) for k in range(span // LANE)]
    for i in range(devices):
        got = jnp.dot(r_ref[i], order_ref[...], preferred_element_type=F32)
        for k, lanes in tiles:
            m_ref[k, i * highs : i * highs + lows] = got[:lows, lanes] + got[highs:, lanes]
            m_ref[k, i * highs + lows : (i + 1) * highs] = got[lows:highs, lanes]
    if depth > devices * count:
        for k, _ in tiles:
            m_ref[k, devices * highs :] = jnp.zeros((depth * GROUP - devices * highs, LANE), F32)
    shifts = w_ref.shape[0]
    for q in range(GROUP):
        modes = [m_ref[k, pl.ds(q, depth, stride=GROUP), :] for k, _ in tiles]
        high, low = split(jnp.concatenate(modes, axis=1))
        z = jnp.dot(a_ref[...], jnp.concatenate([high, low], axis=1), preferred_element_type=F32)
        coef = z[:modes_x, :span] + z[modes_x:, :span] + z[:modes_x, span:]
        coef = coef * g_ref[q : q + 1, :]
        mixed = []
        for k, lanes in tiles:
            part = coef[:, lanes]
            total = part * w_ref[0]
            for n in range(1, shifts):
                total = total + pltpu.roll(part, n * (LANE // shifts), 1) * w_ref[n]
            mixed.append(total)
        high, low = split(jnp.concatenate(mixed, axis=1))
        right = jnp.concatenate([high, high, low, low], axis=0)
        z = jnp.dot(b_ref[...], right, preferred_element_type=F32)
        for k, lanes in tiles:
            back_ref[k, pl.ds(q, devices * count, stride=GROUP), :] = z[:, lanes]
    for i in range(devices):
        for k, lanes in tiles:
            z = back_ref[k, i * highs : (i + 1) * highs]
            high = z.astype(BF16).astype(F32)
            low = z[:lows] - high[:lows]
            o_ref[i, :, lanes] = jnp.concatenate([high, low], axis=0).astype(BF16)


def expand(funcs, fine, r_ref, place_ref, b_ref):
    count, rows = funcs.shape
    modes_y = b_ref.shape[1] // 4
    halves = b_ref.shape[2] // SPAN

    def some(g, carry):
        at = pl.multiple_of(g * 2 * GROUP, 2 * GROUP)
        for h in range(halves):
            got = []
            for k in range(2):
                block = r_ref[(2 * g + k) * halves + h]
                got.append(jnp.dot(block, place_ref[h], preferred_element_type=F32))
            for c in range(SPAN // LANE):
                part = slice(c * LANE, (c + 1) * LANE)
                modes = []
                for j in range(count):
                    pieces = []
                    for k in range(2):
                        piece = got[k][j * GROUP : (j + 1) * GROUP, part]
                        if j < fine:
                            low = got[k][(count + j) * GROUP : (count + j + 1) * GROUP, part]
                            piece = piece + low
                        pieces.append(piece)
                    modes.append(jnp.concatenate(pieces, axis=0))
                lanes = slice(h * SPAN + c * LANE, h * SPAN + (c + 1) * LANE)
                for t in range(rows // 2):
                    sums = []
                    for parity in range(2):
                        total = modes[parity] * float(0.5 * funcs[parity, t])
                        for j in range(parity + 2, count, 2):
                            total = total + modes[j] * float(0.5 * funcs[j, t])
                        sums.append(total)
                    for row, value in ((t, sums[0] + sums[1]), (rows - 1 - t, sums[0] - sums[1])):
                        high, low = split(value)
                        for n, half in enumerate((high, high, low, low)):
                            b_ref[row, pl.ds(at + n * modes_y, 2 * GROUP), lanes] = half
        return carry

    lax.fori_loop(0, modes_y // (2 * GROUP), some, 0)


def local_kernel(u_ref, l_ref, flip_ref, x_ref, f_ref):
    rows, width, _ = u_ref.shape
    for h in range(2):
        lanes = slice(h * SPAN, (h + 1) * SPAN)
        u = u_ref[:, :, lanes].reshape(rows * width, SPAN)
        x = jnp.dot(jnp.concatenate([u, u], axis=1), l_ref[h], preferred_element_type=F32)
        x_ref[:, :, lanes] = x.reshape(rows, width, SPAN)
    f = jnp.dot(u, flip_ref[...], preferred_element_type=F32)
    f_ref[...] = f.astype(BF16).reshape(rows, width, SPAN)


def weave(one, other):
    done = 0
    for n, step in enumerate(one):
        step()
        until = len(other) * (n + 1) // len(one)
        for at in range(done, until):
            other[at]()
        done = until


def tail_kernel(funcs, fine, chunk, r_ref, x_ref, u_ref, f_ref, by_ref, w_ref, place_ref, flip_ref, o_ref, b_ref, *scratch):
    step = pl.program_id(0)
    last = pl.num_programs(0) - 1
    width = u_ref.shape[1]
    pre, first, parts, post, done = (scratch[n : n + 2] for n in range(0, 10, 2))
    near, far = slice(0, SPAN), slice(SPAN, 2 * SPAN)
    unit = pre[0].shape[0]
    pieces = range(0, unit, chunk)

    def where(n, y):
        return divmod(n * unit + y, width)

    def lateral_product(n):
        tall = min(unit, width)

        def piece(at, lanes):
            r, y = where(n, at)
            right = b_ref[u_ref.shape[0] * step + r, :, lanes]
            z = jnp.dot(by_ref[y : y + tall], right, preferred_element_type=F32)
            pre[n][at : at + tall, lanes] = z

        return [functools.partial(piece, at, lanes) for at in range(0, unit, tall) for lanes in (near, far)]

    def lateral_points(n):
        def piece(y):
            r, y0 = where(n, y)
            at, ys = slice(y, y + chunk), slice(y0, y0 + chunk)
            f0 = u_ref[r, ys].astype(F32) + twice_gelu(pre[n][at, near] + x_ref[r, ys, near])
            f1 = f_ref[r, ys].astype(F32) + twice_gelu(pre[n][at, far] + x_ref[r, ys, far])
            first[n][at, near] = f0
            first[n][at, far] = f1
            for m, value in enumerate((f0 + f1, f0 - f1)):
                high, low = split(value)
                parts[n][at, 2 * m * SPAN : (2 * m + 1) * SPAN] = high
                parts[n][at, (2 * m + 1) * SPAN : (2 * m + 2) * SPAN] = low

        return [functools.partial(piece, y) for y in pieces]

    def depth_product(n):
        def piece(m, lanes):
            high = parts[n][:, 2 * m * SPAN : (2 * m + 1) * SPAN]
            low = parts[n][:, (2 * m + 1) * SPAN : (2 * m + 2) * SPAN]
            left = jnp.concatenate([high, low, high], axis=1)
            post[n][:, lanes] = jnp.dot(left, w_ref[m], preferred_element_type=F32)

        return [functools.partial(piece, m, lanes) for m, lanes in enumerate((near, far))]

    def depth_points(n):
        def piece(y):
            r, y0 = where(n, y)
            at, ys = slice(y, y + chunk), slice(y0, y0 + chunk)
            even, odd = post[n][at, near], post[n][at, far]
            o_ref[r, ys, near] = (first[n][at, near] + twice_gelu(even + odd)).astype(BF16)
            done[n][at] = (first[n][at, far] + twice_gelu(even - odd)).astype(BF16)

        return [functools.partial(piece, y) for y in pieces]

    def finish(n):
        def piece():
            z = jnp.dot(done[n][...], flip_ref[...], preferred_element_type=F32).astype(BF16)
            for at in range(0, unit, min(unit, width)):
                r, y0 = where(n, at)
                o_ref[r, y0 : y0 + min(unit, width), far] = z[at : at + min(unit, width)]

        return [piece]

    @pl.when(step == 0)
    def _():
        expand(funcs, fine, r_ref, place_ref, b_ref)
        weave(lateral_product(0), [])
        weave(lateral_product(1), lateral_points(0))
        weave(depth_product(0), lateral_points(1))

    @pl.when(jnp.logical_and(step > 0, step < last))
    def _():
        weave(depth_product(1), depth_points(0))
        weave(lateral_product(0) + finish(0), depth_points(1))
        weave(lateral_product(1) + finish(1), lateral_points(0))
        weave(depth_product(0), lateral_points(1))

    @pl.when(step == last)
    def _():
        weave(depth_product(1), depth_points(0))
        weave(finish(0), depth_points(1))
        weave(finish(1), [])


def twice_gelu(half):
    return half + half * jnp.tanh(half * (TANH_A + TANH_B * (half * half)))


def diagonals(matrices):
    n = matrices.shape[1]
    ids = np.arange(n)
    picks = (ids[None, :, None] == (ids[None, None, :] - ids[:, None, None]) % n).astype(np.float32)
    rows = jnp.sum(matrices[None] * picks[:, None], axis=2)
    return jnp.repeat(rows, LANE // n, axis=2)


def kron_eye(matrix, count):
    *lead, n, m = matrix.shape
    eye = jnp.eye(count, dtype=matrix.dtype)
    return (eye[:, None, :, None] * matrix[..., None, :, None, :]).reshape(*lead, count * n, count * m)


def fits(mesh_lat, rows, width_y, cells, chans, modes_x, modes_y):
    return (
        cells == 2 * SPAN
        and SPAN % (LANE // chans * chans) == 0
        and mesh_lat * GROUP * SPAN == modes_y * cells
        and rows % 4 == 0
        and rows >= 16
        and width_y % 256 == 0
        and 4 * modes_y == SPAN
        and modes_x % 8 == 0
    )


def shards(field, lat_modes, lat_gains, lat_local, depth_modes, depth_local):
    highest = lax.Precision.HIGHEST
    devices = lax.axis_size("lat")
    rows, width_y, cells = field.shape
    modes_x, chans, _ = lat_modes.shape
    modes_y = lat_gains.shape[0]
    modes_z = depth_modes.shape[0]
    if not fits(devices, rows, width_y, cells, chans, modes_x, modes_y):
        return plain_shards(field, lat_modes, lat_gains, lat_local, depth_modes, depth_local)
    depth = cells // chans
    width_x = rows * devices
    basis_x = basis64(width_x, modes_x)
    basis_y = basis64(width_y, modes_y)
    basis_z = basis64(depth, modes_z)
    funcs, fine = window_modes(rows, width_x, modes_x)
    count = funcs.shape[0]
    packed = (count + fine) * GROUP
    halves = cells // SPAN
    me = lax.axis_index("lat")

    by_high, by_low = split64(basis_y)
    by_forward = np.concatenate([by_high, by_low], axis=0)
    pairs = 2
    steps = rows // (2 * pairs)
    sent = pl.pallas_call(
        functools.partial(forward_kernel, funcs, fine),
        grid=(steps + 1,),
        in_specs=[
            pl.BlockSpec((2 * modes_y, width_y), lambda s: (0, 0)),
            pl.BlockSpec((pairs, width_y, cells), lambda s: (jnp.minimum(s, steps - 1), 0, 0)),
            pl.BlockSpec((pairs, width_y, cells), lambda s: (2 * steps - 1 - jnp.minimum(s, steps - 1), 0, 0)),
        ],
        out_specs=pl.BlockSpec((devices, packed, SPAN), lambda s: (0, 0, 0)),
        out_shape=jax.ShapeDtypeStruct((devices, packed, SPAN), BF16),
        scratch_shapes=[
            pltpu.VMEM((2 * pairs, modes_y, cells), F32),
            pltpu.VMEM((count, modes_y, cells), F32),
        ],
        compiler_params=pltpu.CompilerParams(vmem_limit_bytes=48 * 2**20),
        name="forward",
    )(by_forward, field, field)
    gathered = lax.all_to_all(sent, "lat", split_axis=0, concat_axis=0, tiled=True)

    per = SPAN // chans
    flip = np.kron(np.eye(per)[::-1], np.eye(chans)).astype(ml_dtypes.bfloat16)
    local_high, local_low = split_outside(kron_eye(0.5 * lat_local, per))
    local = jnp.concatenate([local_high, local_low], axis=0)
    turned = local.reshape(2 * SPAN, per, chans)[:, ::-1].reshape(2 * SPAN, SPAN)
    four = 4
    local_part, mirrored = pl.pallas_call(
        local_kernel,
        grid=(rows // four,),
        in_specs=[
            pl.BlockSpec((four, width_y, cells), lambda s: (s, 0, 0)),
            pl.BlockSpec((2, 2 * SPAN, SPAN), lambda s: (0, 0, 0)),
            pl.BlockSpec((SPAN, SPAN), lambda s: (0, 0)),
        ],
        out_specs=[
            pl.BlockSpec((four, width_y, cells), lambda s: (s, 0, 0)),
            pl.BlockSpec((four, width_y, SPAN), lambda s: (s, 0, 0)),
        ],
        out_shape=[
            jax.ShapeDtypeStruct(field.shape, F32),
            jax.ShapeDtypeStruct((rows, width_y, SPAN), BF16),
        ],
        compiler_params=pltpu.CompilerParams(vmem_limit_bytes=48 * 2**20),
        name="local",
    )(field, jnp.stack([local, turned]), flip)

    weights = np.einsum("pit,jt->pij", basis_x.reshape(modes_x, devices, rows), funcs)
    flat = weights.reshape(modes_x, devices * count)
    ah, al = split64(np.pad(flat, ((0, 0), (0, -flat.shape[1] % LANE))))
    a_forward = np.concatenate([ah, al], axis=0)
    bh, bl = split64(flat.T)
    a_back = np.concatenate([bh, bl, bh, bl], axis=1)
    gains = lax.dynamic_slice_in_dim(lat_gains, (me // halves) * GROUP, GROUP, axis=0)
    gains = jnp.tile(jnp.repeat(gains, LANE // chans, axis=1), (1, SPAN // LANE))
    per_lane = LANE // chans
    ids = np.arange(LANE)
    order = np.zeros((LANE, LANE))
    order[ids, ids % chans * per_lane + ids // chans] = 1
    order = np.kron(np.eye(SPAN // LANE), order).astype(ml_dtypes.bfloat16)
    mixed = pl.pallas_call(
        functools.partial(mix_kernel, count, fine),
        in_specs=6 * [pl.BlockSpec(memory_space=pltpu.VMEM)] + [pl.BlockSpec(memory_space=pl.ANY)],
        out_shape=jax.ShapeDtypeStruct((devices, packed, SPAN), BF16),
        scratch_shapes=[
            pltpu.VMEM((SPAN // LANE, a_forward.shape[1] * GROUP, LANE), F32),
            pltpu.VMEM((SPAN // LANE, devices * count * GROUP, LANE), F32),
        ],
        compiler_params=pltpu.CompilerParams(vmem_limit_bytes=48 * 2**20),
        name="mix",
    )(gathered, a_forward, a_back, gains, diagonals(lat_modes), order, mirrored)
    returned = lax.all_to_all(mixed, "lat", split_axis=0, concat_axis=0, tiled=True)

    by_back = np.concatenate([by_high, by_low, by_high, by_low], axis=0).T.copy()
    near_z = basis_z[:, :per].astype(np.float32)

    def depth_matrix(parity):
        b = near_z[parity::2]
        full = 0.5 * jnp.einsum(
            "kz,kw,kcd->zcwd", b, b, depth_modes[parity::2], precision=highest
        ).reshape(SPAN, SPAN) + 0.25 * kron_eye(depth_local, per)
        high, low = split_outside(full)
        return jnp.concatenate([high, high, low], axis=0)

    place = np.stack([order.T, order.T @ flip])
    block = 1
    unit = block * width_y // 2
    wide = (unit, cells)
    narrow = (unit, SPAN)
    steps = rows // block
    return pl.pallas_call(
        functools.partial(tail_kernel, funcs, fine, 64),
        grid=(steps + 1,),
        in_specs=[
            pl.BlockSpec((devices, packed, SPAN), lambda s: (0, 0, 0)),
            pl.BlockSpec((block, width_y, cells), lambda s: (jnp.minimum(s, steps - 1), 0, 0)),
            pl.BlockSpec((block, width_y, SPAN), lambda s: (jnp.minimum(s, steps - 1), 0, 0)),
            pl.BlockSpec((block, width_y, SPAN), lambda s: (jnp.minimum(s, steps - 1), 0, 0)),
            pl.BlockSpec((width_y, SPAN), lambda s: (0, 0)),
            pl.BlockSpec((2, 3 * SPAN, SPAN), lambda s: (0, 0, 0)),
            pl.BlockSpec((2, SPAN, SPAN), lambda s: (0, 0, 0)),
            pl.BlockSpec((SPAN, SPAN), lambda s: (0, 0)),
        ],
        out_specs=pl.BlockSpec((block, width_y, cells), lambda s: (jnp.maximum(s - 1, 0), 0, 0)),
        out_shape=jax.ShapeDtypeStruct(field.shape, BF16),
        scratch_shapes=[pltpu.VMEM((rows, 4 * modes_y, cells), BF16)]
        + 2 * [pltpu.VMEM(wide, F32)]
        + 2 * [pltpu.VMEM(wide, F32)]
        + 2 * [pltpu.VMEM((unit, 4 * SPAN), BF16)]
        + 2 * [pltpu.VMEM(wide, F32)]
        + 2 * [pltpu.VMEM(narrow, BF16)],
        compiler_params=pltpu.CompilerParams(vmem_limit_bytes=58 * 2**20),
        name="tail",
    )(
        returned,
        local_part,
        field,
        mirrored,
        by_back,
        jnp.stack([depth_matrix(0), depth_matrix(1)]),
        place,
        flip,
    )


def solution(mesh):
    placed = (P(("group", "lat"), None, None), P(), P(), P(), P(), P())
    return jax.shard_map(
        shards,
        mesh=mesh,
        in_specs=placed,
        out_specs=P(("group", "lat"), None, None),
        check_vma=False,
    )
```

```python
import functools
import math

import jax
import jax.numpy as jnp
import ml_dtypes
import numpy as np
from jax import lax
from jax.experimental import pallas as pl
from jax.experimental.pallas import tpu as pltpu
from jax.sharding import PartitionSpec as P


def cosine_basis(length, modes):
    order = jnp.arange(modes, dtype=jnp.float32)[:, None]
    place = jnp.arange(length, dtype=jnp.float32)[None, :]
    scales = jnp.where(order == 0.0, math.sqrt(1.0 / length), math.sqrt(2.0 / length))
    return jnp.cos(math.pi * order * (place + 0.5) / length) * scales


def row_tail(u_rows, spect, lat_local, depth_modes, depth_local, depth_basis):
    highest = lax.Precision.HIGHEST
    rows, width, cells = u_rows.shape
    chans = lat_local.shape[0]
    depth = cells // chans
    u4 = u_rows.reshape(rows, width, depth, chans)
    s4 = spect.reshape(rows, width, depth, chans)
    first = u4 + jax.nn.gelu(s4 + jnp.einsum("xyzc,cd->xyzd", u4, lat_local, precision=highest))
    dcoef = jnp.einsum("kz,xyzc->xykc", depth_basis, first, precision=highest)
    dmix = jnp.einsum("xykc,kcd->xykd", dcoef, depth_modes, precision=highest)
    dspect = jnp.einsum("kz,xykd->xyzd", depth_basis, dmix, precision=highest)
    final = first + jax.nn.gelu(
        dspect + jnp.einsum("xyzc,cd->xyzd", first, depth_local, precision=highest)
    )
    return final.reshape(rows, width, cells).astype(jnp.bfloat16)


def one_hot(ids, count):
    return (ids[:, None] == jnp.arange(count, dtype=jnp.int32)[None, :]).astype(jnp.float32)


def plain_shards(field, lat_modes, lat_gains, lat_local, depth_modes, depth_local):
    highest = lax.Precision.HIGHEST
    devices = lax.axis_size("lat")
    rows_dev, width_y, cells = field.shape
    modes_x, chans, _ = lat_modes.shape
    modes_y = lat_gains.shape[0]
    modes_z = depth_modes.shape[0]
    depth = cells // chans
    width_x = rows_dev * devices
    basis_x = cosine_basis(width_x, modes_x)
    basis_y = cosine_basis(width_y, modes_y)
    basis_z = cosine_basis(depth, modes_z)
    start = lax.axis_index("lat")
    u_rows = field.astype(jnp.float32)
    coef_y = jnp.einsum("qy,xyw->xqw", basis_y, u_rows, precision=highest)
    packed = coef_y.reshape(rows_dev, modes_y * cells)
    gathered = lax.all_to_all(packed, "lat", split_axis=1, concat_axis=0, tiled=True)
    span = gathered.shape[1]
    pairs = span // chans
    coef = jnp.dot(basis_x, gathered, precision=highest).reshape(modes_x, pairs, chans)
    mode_ids = (start * pairs + jnp.arange(pairs, dtype=jnp.int32)) // depth
    gain_rows = jnp.dot(one_hot(mode_ids, modes_y), lat_gains, precision=highest)
    mixed = jnp.einsum("jpc,jcd->jpd", coef * gain_rows[None, :, :], lat_modes, precision=highest)
    back_x = jnp.dot(basis_x.T, mixed.reshape(modes_x, span), precision=highest)
    returned = lax.all_to_all(back_x, "lat", split_axis=0, concat_axis=1, tiled=True)
    spect = jnp.einsum(
        "qy,xqw->xyw", basis_y, returned.reshape(rows_dev, modes_y, cells), precision=highest
    )
    return row_tail(u_rows, spect, lat_local, depth_modes, depth_local, basis_z)


BF16 = jnp.bfloat16
F32 = jnp.float32
LANE = 128
GROUP = 8
SPAN = 256
TANH_A = 2.0 * math.sqrt(2.0 / math.pi)
TANH_B = 8.0 * 0.044715 * math.sqrt(2.0 / math.pi)


def basis64(length, modes):
    order = np.arange(modes)[:, None]
    place = np.arange(length)[None, :]
    scales = np.where(order == 0, math.sqrt(1.0 / length), math.sqrt(2.0 / length))
    return np.cos(math.pi * order * (place + 0.5) / length) * scales


def split64(array):
    high = array.astype(ml_dtypes.bfloat16)
    return high, (array - high.astype(np.float64)).astype(ml_dtypes.bfloat16)


def split(array):
    high = array.astype(BF16)
    return high, (array - high.astype(F32)).astype(BF16)


def split_outside(array):
    high = lax.reduce_precision(array, 8, 7)
    return high.astype(BF16), (array - high).astype(BF16)


def window_modes(rows, length, modes):
    place = np.arange(rows) - (rows - 1) / 2
    order = np.arange(modes)[:, None]
    _, se, ve = np.linalg.svd(np.cos(math.pi * order * place / length))
    _, so, vo = np.linalg.svd(np.sin(math.pi * order * place / length))
    top = max(se[0], so[0])
    both = sorted([(-w, 2 * n) for n, w in enumerate(se[: rows // 2])] + [(-w, 2 * n + 1) for n, w in enumerate(so[: rows // 2])])
    weights = np.array([-w for w, _ in both])
    count = int(np.sum(weights > top * 2.0**-23))
    fine = int(np.sum(weights > top * 0.25))
    fine += (count + fine) % 2
    funcs = np.stack([ve[: rows // 2], vo[: rows // 2]], axis=1).reshape(rows // 2 * 2, rows)
    assert [n for _, n in both[:count]] == list(range(count))
    return funcs[:count], fine


def forward_kernel(funcs, fine, by_ref, near_ref, far_ref, o_ref, cy_ref, acc_ref):
    step = pl.program_id(0)
    pairs = near_ref.shape[0]
    steps = funcs.shape[1] // (2 * pairs)
    modes_y = by_ref.shape[0] // 2
    count = funcs.shape[0]
    halves = cy_ref.shape[2] // SPAN

    def compress(before):
        for g in range(modes_y // GROUP):
            rows = slice(g * GROUP, (g + 1) * GROUP)
            for c in range(halves * SPAN // LANE):
                lanes = slice(c * LANE, (c + 1) * LANE)
                totals = [None if before == 0 else acc_ref[j, rows, lanes] for j in range(count)]
                for r in range(pairs):
                    x, y = cy_ref[r, rows, lanes], cy_ref[pairs + r, rows, lanes]
                    pair = (x + y, x - y)
                    for j in range(count):
                        term = pair[j % 2] * float(funcs[j, before * pairs + r])
                        totals[j] = term if totals[j] is None else totals[j] + term
                if before < steps - 1:
                    for j in range(count):
                        acc_ref[j, rows, lanes] = totals[j]
                    continue
                h, k = divmod(c, SPAN // LANE)
                place = slice(k * LANE, (k + 1) * LANE)
                slots = [total.astype(BF16).astype(F32) for total in totals]
                slots += [totals[j] - slots[j] for j in range(fine)]
                for j in range(0, count + fine, 2):
                    two = jnp.concatenate(slots[j : j + 2], axis=0).astype(BF16)
                    o_ref[g * halves + h, j * GROUP : (j + 2) * GROUP, place] = two

    def body(at):
        if at > 0:
            compress(at - 1)
        if at < steps:
            for r in range(pairs):
                for slot, row in ((r, near_ref[r]), (pairs + r, far_ref[pairs - 1 - r])):
                    z = jnp.dot(by_ref[...], row, preferred_element_type=F32)
                    cy_ref[slot] = z[:modes_y] + z[modes_y:]

    for at in range(steps + 1):
        pl.when(step == at)(functools.partial(body, at))


def mix_kernel(count, fine, r_ref, a_ref, b_ref, g_ref, w_ref, order_ref, after_ref, o_ref, m_ref, back_ref):
    devices, packed, span = r_ref.shape
    modes_x = w_ref.shape[1]
    depth = a_ref.shape[1]
    highs, lows = count * GROUP, fine * GROUP
    tiles = [(k, slice(k * LANE, (k + 1) * LANE)) for k in range(span // LANE)]
    for i in range(devices):
        got = jnp.dot(r_ref[i], order_ref[...], preferred_element_type=F32)
        for k, lanes in tiles:
            m_ref[k, i * highs : i * highs + lows] = got[:lows, lanes] + got[highs:, lanes]
            m_ref[k, i * highs + lows : (i + 1) * highs] = got[lows:highs, lanes]
    if depth > devices * count:
        for k, _ in tiles:
            m_ref[k, devices * highs :] = jnp.zeros((depth * GROUP - devices * highs, LANE), F32)
    shifts = w_ref.shape[0]
    for q in range(GROUP):
        modes = [m_ref[k, pl.ds(q, depth, stride=GROUP), :] for k, _ in tiles]
        high, low = split(jnp.concatenate(modes, axis=1))
        z = jnp.dot(a_ref[...], jnp.concatenate([high, low], axis=1), preferred_element_type=F32)
        coef = z[:modes_x, :span] + z[modes_x:, :span] + z[:modes_x, span:]
        coef = coef * g_ref[q : q + 1, :]
        mixed = []
        for k, lanes in tiles:
            part = coef[:, lanes]
            total = part * w_ref[0]
            for n in range(1, shifts):
                total = total + pltpu.roll(part, n * (LANE // shifts), 1) * w_ref[n]
            mixed.append(total)
        high, low = split(jnp.concatenate(mixed, axis=1))
        right = jnp.concatenate([high, high, low, low], axis=0)
        z = jnp.dot(b_ref[...], right, preferred_element_type=F32)
        for k, lanes in tiles:
            back_ref[k, pl.ds(q, devices * count, stride=GROUP), :] = z[:, lanes]
    for i in range(devices):
        for k, lanes in tiles:
            z = back_ref[k, i * highs : (i + 1) * highs]
            high = z.astype(BF16).astype(F32)
            low = z[:lows] - high[:lows]
            o_ref[i, :, lanes] = jnp.concatenate([high, low], axis=0).astype(BF16)


def expand(funcs, fine, r_ref, place_ref, b_ref):
    count, rows = funcs.shape
    modes_y = b_ref.shape[1] // 4
    halves = b_ref.shape[2] // SPAN

    def some(g, carry):
        at = pl.multiple_of(g * 2 * GROUP, 2 * GROUP)
        for h in range(halves):
            got = []
            for k in range(2):
                block = r_ref[(2 * g + k) * halves + h]
                got.append(jnp.dot(block, place_ref[h], preferred_element_type=F32))
            for c in range(SPAN // LANE):
                part = slice(c * LANE, (c + 1) * LANE)
                modes = []
                for j in range(count):
                    pieces = []
                    for k in range(2):
                        piece = got[k][j * GROUP : (j + 1) * GROUP, part]
                        if j < fine:
                            low = got[k][(count + j) * GROUP : (count + j + 1) * GROUP, part]
                            piece = piece + low
                        pieces.append(piece)
                    modes.append(jnp.concatenate(pieces, axis=0))
                lanes = slice(h * SPAN + c * LANE, h * SPAN + (c + 1) * LANE)
                for t in range(rows // 2):
                    sums = []
                    for parity in range(2):
                        total = modes[parity] * float(0.5 * funcs[parity, t])
                        for j in range(parity + 2, count, 2):
                            total = total + modes[j] * float(0.5 * funcs[j, t])
                        sums.append(total)
                    for row, value in ((t, sums[0] + sums[1]), (rows - 1 - t, sums[0] - sums[1])):
                        high, low = split(value)
                        for n, half in enumerate((high, high, low, low)):
                            b_ref[row, pl.ds(at + n * modes_y, 2 * GROUP), lanes] = half
        return carry

    lax.fori_loop(0, modes_y // (2 * GROUP), some, 0)


def local_near_kernel(u_ref, l_ref, x_ref):
    rows, width, _ = u_ref.shape
    u = u_ref[...].reshape(rows * width, SPAN)
    x = jnp.dot(jnp.concatenate([u, u], axis=1), l_ref[...], preferred_element_type=F32)
    x_ref[...] = x.reshape(rows, width, SPAN)


def local_far_kernel(u_ref, l_ref, flip_ref, after_ref, x_ref, f_ref):
    local_near_kernel(u_ref, l_ref, x_ref)
    rows, width, _ = u_ref.shape
    u = u_ref[...].reshape(rows * width, SPAN)
    f = jnp.dot(u, flip_ref[...], preferred_element_type=F32)
    f_ref[...] = f.astype(BF16).reshape(rows, width, SPAN)


def weave(one, other):
    done = 0
    for n, step in enumerate(one):
        step()
        until = len(other) * (n + 1) // len(one)
        for at in range(done, until):
            other[at]()
        done = until


def tail_kernel(funcs, fine, chunk, r_ref, x0_ref, x1_ref, u_ref, f_ref, by_ref, w_ref, place_ref, flip_ref, o_ref, b_ref, *scratch):
    step = pl.program_id(0)
    last = pl.num_programs(0) - 1
    width = u_ref.shape[1]
    pre, first, parts, post, done = (scratch[n : n + 2] for n in range(0, 10, 2))
    near, far = slice(0, SPAN), slice(SPAN, 2 * SPAN)
    unit = pre[0].shape[0]
    pieces = range(0, unit, chunk)

    def where(n, y):
        return divmod(n * unit + y, width)

    def lateral_product(n):
        tall = min(unit, width)

        def piece(at, lanes):
            r, y = where(n, at)
            right = b_ref[u_ref.shape[0] * step + r, :, lanes]
            z = jnp.dot(by_ref[y : y + tall], right, preferred_element_type=F32)
            pre[n][at : at + tall, lanes] = z

        return [functools.partial(piece, at, lanes) for at in range(0, unit, tall) for lanes in (near, far)]

    def lateral_points(n):
        def piece(y):
            r, y0 = where(n, y)
            at, ys = slice(y, y + chunk), slice(y0, y0 + chunk)
            f0 = u_ref[r, ys].astype(F32) + twice_gelu(pre[n][at, near] + x0_ref[r, ys])
            f1 = f_ref[r, ys].astype(F32) + twice_gelu(pre[n][at, far] + x1_ref[r, ys])
            first[n][at, near] = f0
            first[n][at, far] = f1
            for m, value in enumerate((f0 + f1, f0 - f1)):
                high, low = split(value)
                parts[n][at, 2 * m * SPAN : (2 * m + 1) * SPAN] = high
                parts[n][at, (2 * m + 1) * SPAN : (2 * m + 2) * SPAN] = low

        return [functools.partial(piece, y) for y in pieces]

    def depth_product(n):
        def piece(m, lanes):
            high = parts[n][:, 2 * m * SPAN : (2 * m + 1) * SPAN]
            low = parts[n][:, (2 * m + 1) * SPAN : (2 * m + 2) * SPAN]
            left = jnp.concatenate([high, low, high], axis=1)
            post[n][:, lanes] = jnp.dot(left, w_ref[m], preferred_element_type=F32)

        return [functools.partial(piece, m, lanes) for m, lanes in enumerate((near, far))]

    def depth_points(n):
        def piece(y):
            r, y0 = where(n, y)
            at, ys = slice(y, y + chunk), slice(y0, y0 + chunk)
            even, odd = post[n][at, near], post[n][at, far]
            o_ref[r, ys, near] = (first[n][at, near] + twice_gelu(even + odd)).astype(BF16)
            done[n][at] = (first[n][at, far] + twice_gelu(even - odd)).astype(BF16)

        return [functools.partial(piece, y) for y in pieces]

    def finish(n):
        def piece():
            z = jnp.dot(done[n][...], flip_ref[...], preferred_element_type=F32).astype(BF16)
            for at in range(0, unit, min(unit, width)):
                r, y0 = where(n, at)
                o_ref[r, y0 : y0 + min(unit, width), far] = z[at : at + min(unit, width)]

        return [piece]

    @pl.when(step == 0)
    def _():
        expand(funcs, fine, r_ref, place_ref, b_ref)
        weave(lateral_product(0), [])
        weave(lateral_product(1), lateral_points(0))
        weave(depth_product(0), lateral_points(1))

    @pl.when(jnp.logical_and(step > 0, step < last))
    def _():
        weave(depth_product(1), depth_points(0))
        weave(lateral_product(0) + finish(0), depth_points(1))
        weave(lateral_product(1) + finish(1), lateral_points(0))
        weave(depth_product(0), lateral_points(1))

    @pl.when(step == last)
    def _():
        weave(depth_product(1), depth_points(0))
        weave(finish(0), depth_points(1))
        weave(finish(1), [])


def twice_gelu(half):
    return half + half * jnp.tanh(half * (TANH_A + TANH_B * (half * half)))


def diagonals(matrices):
    n = matrices.shape[1]
    ids = np.arange(n)
    picks = (ids[None, :, None] == (ids[None, None, :] - ids[:, None, None]) % n).astype(np.float32)
    rows = jnp.sum(matrices[None] * picks[:, None], axis=2)
    return jnp.repeat(rows, LANE // n, axis=2)


def kron_eye(matrix, count):
    *lead, n, m = matrix.shape
    eye = jnp.eye(count, dtype=matrix.dtype)
    return (eye[:, None, :, None] * matrix[..., None, :, None, :]).reshape(*lead, count * n, count * m)


def fits(mesh_lat, rows, width_y, cells, chans, modes_x, modes_y):
    return (
        cells == 2 * SPAN
        and SPAN % (LANE // chans * chans) == 0
        and mesh_lat * GROUP * SPAN == modes_y * cells
        and rows % 4 == 0
        and rows >= 16
        and width_y % 256 == 0
        and 4 * modes_y == SPAN
        and modes_x % 8 == 0
    )


def shards(field, lat_modes, lat_gains, lat_local, depth_modes, depth_local):
    highest = lax.Precision.HIGHEST
    devices = lax.axis_size("lat")
    rows, width_y, cells = field.shape
    modes_x, chans, _ = lat_modes.shape
    modes_y = lat_gains.shape[0]
    modes_z = depth_modes.shape[0]
    if not fits(devices, rows, width_y, cells, chans, modes_x, modes_y):
        return plain_shards(field, lat_modes, lat_gains, lat_local, depth_modes, depth_local)
    depth = cells // chans
    width_x = rows * devices
    basis_x = basis64(width_x, modes_x)
    basis_y = basis64(width_y, modes_y)
    basis_z = basis64(depth, modes_z)
    funcs, fine = window_modes(rows, width_x, modes_x)
    count = funcs.shape[0]
    packed = (count + fine) * GROUP
    halves = cells // SPAN
    me = lax.axis_index("lat")

    by_high, by_low = split64(basis_y)
    by_forward = np.concatenate([by_high, by_low], axis=0)
    pairs = 2
    steps = rows // (2 * pairs)
    sent = pl.pallas_call(
        functools.partial(forward_kernel, funcs, fine),
        grid=(steps + 1,),
        in_specs=[
            pl.BlockSpec((2 * modes_y, width_y), lambda s: (0, 0)),
            pl.BlockSpec((pairs, width_y, cells), lambda s: (jnp.minimum(s, steps - 1), 0, 0)),
            pl.BlockSpec((pairs, width_y, cells), lambda s: (2 * steps - 1 - jnp.minimum(s, steps - 1), 0, 0)),
        ],
        out_specs=pl.BlockSpec((devices, packed, SPAN), lambda s: (0, 0, 0)),
        out_shape=jax.ShapeDtypeStruct((devices, packed, SPAN), BF16),
        scratch_shapes=[
            pltpu.VMEM((2 * pairs, modes_y, cells), F32),
            pltpu.VMEM((count, modes_y, cells), F32),
        ],
        compiler_params=pltpu.CompilerParams(vmem_limit_bytes=48 * 2**20),
        name="forward",
    )(by_forward, field, field)
    gathered = lax.all_to_all(sent, "lat", split_axis=0, concat_axis=0, tiled=True)

    per = SPAN // chans
    flip = np.kron(np.eye(per)[::-1], np.eye(chans)).astype(ml_dtypes.bfloat16)
    local_high, local_low = split_outside(kron_eye(0.5 * lat_local, per))
    local = jnp.concatenate([local_high, local_low], axis=0)
    turned = local.reshape(2 * SPAN, per, chans)[:, ::-1].reshape(2 * SPAN, SPAN)
    four = 4
    local_near = pl.pallas_call(
        local_near_kernel,
        grid=(rows // four,),
        in_specs=[
            pl.BlockSpec((four, width_y, SPAN), lambda s: (s, 0, 0)),
            pl.BlockSpec((2 * SPAN, SPAN), lambda s: (0, 0)),
        ],
        out_specs=pl.BlockSpec((four, width_y, SPAN), lambda s: (s, 0, 0)),
        out_shape=jax.ShapeDtypeStruct((rows, width_y, SPAN), F32),
        compiler_params=pltpu.CompilerParams(vmem_limit_bytes=48 * 2**20),
        name="local_near",
    )(field, local)

    weights = np.einsum("pit,jt->pij", basis_x.reshape(modes_x, devices, rows), funcs)
    flat = weights.reshape(modes_x, devices * count)
    ah, al = split64(np.pad(flat, ((0, 0), (0, -flat.shape[1] % LANE))))
    a_forward = np.concatenate([ah, al], axis=0)
    bh, bl = split64(flat.T)
    a_back = np.concatenate([bh, bl, bh, bl], axis=1)
    gains = lax.dynamic_slice_in_dim(lat_gains, (me // halves) * GROUP, GROUP, axis=0)
    gains = jnp.tile(jnp.repeat(gains, LANE // chans, axis=1), (1, SPAN // LANE))
    per_lane = LANE // chans
    ids = np.arange(LANE)
    order = np.zeros((LANE, LANE))
    order[ids, ids % chans * per_lane + ids // chans] = 1
    order = np.kron(np.eye(SPAN // LANE), order).astype(ml_dtypes.bfloat16)
    mixed = pl.pallas_call(
        functools.partial(mix_kernel, count, fine),
        in_specs=6 * [pl.BlockSpec(memory_space=pltpu.VMEM)] + [pl.BlockSpec(memory_space=pl.ANY)],
        out_shape=jax.ShapeDtypeStruct((devices, packed, SPAN), BF16),
        scratch_shapes=[
            pltpu.VMEM((SPAN // LANE, a_forward.shape[1] * GROUP, LANE), F32),
            pltpu.VMEM((SPAN // LANE, devices * count * GROUP, LANE), F32),
        ],
        compiler_params=pltpu.CompilerParams(vmem_limit_bytes=48 * 2**20),
        name="mix",
    )(gathered, a_forward, a_back, gains, diagonals(lat_modes), order, local_near)
    returned = lax.all_to_all(mixed, "lat", split_axis=0, concat_axis=0, tiled=True)

    local_far, mirrored = pl.pallas_call(
        local_far_kernel,
        grid=(rows // four,),
        in_specs=[
            pl.BlockSpec((four, width_y, SPAN), lambda s: (s, 0, 1)),
            pl.BlockSpec((2 * SPAN, SPAN), lambda s: (0, 0)),
            pl.BlockSpec((SPAN, SPAN), lambda s: (0, 0)),
            pl.BlockSpec(memory_space=pl.ANY),
        ],
        out_specs=2 * [pl.BlockSpec((four, width_y, SPAN), lambda s: (s, 0, 0))],
        out_shape=[
            jax.ShapeDtypeStruct((rows, width_y, SPAN), F32),
            jax.ShapeDtypeStruct((rows, width_y, SPAN), BF16),
        ],
        compiler_params=pltpu.CompilerParams(vmem_limit_bytes=48 * 2**20),
        name="local_far",
    )(field, turned, flip, mixed)

    by_back = np.concatenate([by_high, by_low, by_high, by_low], axis=0).T.copy()
    near_z = basis_z[:, :per].astype(np.float32)

    def depth_matrix(parity):
        b = near_z[parity::2]
        full = 0.5 * jnp.einsum(
            "kz,kw,kcd->zcwd", b, b, depth_modes[parity::2], precision=highest
        ).reshape(SPAN, SPAN) + 0.25 * kron_eye(depth_local, per)
        high, low = split_outside(full)
        return jnp.concatenate([high, high, low], axis=0)

    place = np.stack([order.T, order.T @ flip])
    block = 4
    unit = block * width_y // 2
    wide = (unit, cells)
    narrow = (unit, SPAN)
    steps = rows // block
    return pl.pallas_call(
        functools.partial(tail_kernel, funcs, fine, 16),
        grid=(steps + 1,),
        in_specs=[
            pl.BlockSpec((devices, packed, SPAN), lambda s: (0, 0, 0)),
            pl.BlockSpec((block, width_y, SPAN), lambda s: (jnp.minimum(s, steps - 1), 0, 0)),
            pl.BlockSpec((block, width_y, SPAN), lambda s: (jnp.minimum(s, steps - 1), 0, 0)),
            pl.BlockSpec((block, width_y, SPAN), lambda s: (jnp.minimum(s, steps - 1), 0, 0)),
            pl.BlockSpec((block, width_y, SPAN), lambda s: (jnp.minimum(s, steps - 1), 0, 0)),
            pl.BlockSpec((width_y, SPAN), lambda s: (0, 0)),
            pl.BlockSpec((2, 3 * SPAN, SPAN), lambda s: (0, 0, 0)),
            pl.BlockSpec((2, SPAN, SPAN), lambda s: (0, 0, 0)),
            pl.BlockSpec((SPAN, SPAN), lambda s: (0, 0)),
        ],
        out_specs=pl.BlockSpec((block, width_y, cells), lambda s: (jnp.maximum(s - 1, 0), 0, 0)),
        out_shape=jax.ShapeDtypeStruct(field.shape, BF16),
        scratch_shapes=[pltpu.VMEM((rows, 4 * modes_y, cells), BF16)]
        + 2 * [pltpu.VMEM(wide, F32)]
        + 2 * [pltpu.VMEM(wide, F32)]
        + 2 * [pltpu.VMEM((unit, 4 * SPAN), BF16)]
        + 2 * [pltpu.VMEM(wide, F32)]
        + 2 * [pltpu.VMEM(narrow, BF16)],
        compiler_params=pltpu.CompilerParams(vmem_limit_bytes=58 * 2**20),
        name="tail",
    )(
        returned,
        local_near,
        local_far,
        field,
        mirrored,
        by_back,
        jnp.stack([depth_matrix(0), depth_matrix(1)]),
        place,
        flip,
    )


def solution(mesh):
    placed = (P(("group", "lat"), None, None), P(), P(), P(), P(), P())
    return jax.shard_map(
        shards,
        mesh=mesh,
        in_specs=placed,
        out_specs=P(("group", "lat"), None, None),
        check_vma=False,
    )
```

```python
import functools
import math

import jax
import jax.numpy as jnp
import ml_dtypes
import numpy as np
from jax import lax
from jax.experimental import pallas as pl
from jax.experimental.pallas import tpu as pltpu
from jax.sharding import PartitionSpec as P


def cosine_basis(length, modes):
    order = jnp.arange(modes, dtype=jnp.float32)[:, None]
    place = jnp.arange(length, dtype=jnp.float32)[None, :]
    scales = jnp.where(order == 0.0, math.sqrt(1.0 / length), math.sqrt(2.0 / length))
    return jnp.cos(math.pi * order * (place + 0.5) / length) * scales


def row_tail(u_rows, spect, lat_local, depth_modes, depth_local, depth_basis):
    highest = lax.Precision.HIGHEST
    rows, width, cells = u_rows.shape
    chans = lat_local.shape[0]
    depth = cells // chans
    u4 = u_rows.reshape(rows, width, depth, chans)
    s4 = spect.reshape(rows, width, depth, chans)
    first = u4 + jax.nn.gelu(s4 + jnp.einsum("xyzc,cd->xyzd", u4, lat_local, precision=highest))
    dcoef = jnp.einsum("kz,xyzc->xykc", depth_basis, first, precision=highest)
    dmix = jnp.einsum("xykc,kcd->xykd", dcoef, depth_modes, precision=highest)
    dspect = jnp.einsum("kz,xykd->xyzd", depth_basis, dmix, precision=highest)
    final = first + jax.nn.gelu(
        dspect + jnp.einsum("xyzc,cd->xyzd", first, depth_local, precision=highest)
    )
    return final.reshape(rows, width, cells).astype(jnp.bfloat16)


def one_hot(ids, count):
    return (ids[:, None] == jnp.arange(count, dtype=jnp.int32)[None, :]).astype(jnp.float32)


def plain_shards(field, lat_modes, lat_gains, lat_local, depth_modes, depth_local):
    highest = lax.Precision.HIGHEST
    devices = lax.axis_size("lat")
    rows_dev, width_y, cells = field.shape
    modes_x, chans, _ = lat_modes.shape
    modes_y = lat_gains.shape[0]
    modes_z = depth_modes.shape[0]
    depth = cells // chans
    width_x = rows_dev * devices
    basis_x = cosine_basis(width_x, modes_x)
    basis_y = cosine_basis(width_y, modes_y)
    basis_z = cosine_basis(depth, modes_z)
    start = lax.axis_index("lat")
    u_rows = field.astype(jnp.float32)
    coef_y = jnp.einsum("qy,xyw->xqw", basis_y, u_rows, precision=highest)
    packed = coef_y.reshape(rows_dev, modes_y * cells)
    gathered = lax.all_to_all(packed, "lat", split_axis=1, concat_axis=0, tiled=True)
    span = gathered.shape[1]
    pairs = span // chans
    coef = jnp.dot(basis_x, gathered, precision=highest).reshape(modes_x, pairs, chans)
    mode_ids = (start * pairs + jnp.arange(pairs, dtype=jnp.int32)) // depth
    gain_rows = jnp.dot(one_hot(mode_ids, modes_y), lat_gains, precision=highest)
    mixed = jnp.einsum("jpc,jcd->jpd", coef * gain_rows[None, :, :], lat_modes, precision=highest)
    back_x = jnp.dot(basis_x.T, mixed.reshape(modes_x, span), precision=highest)
    returned = lax.all_to_all(back_x, "lat", split_axis=0, concat_axis=1, tiled=True)
    spect = jnp.einsum(
        "qy,xqw->xyw", basis_y, returned.reshape(rows_dev, modes_y, cells), precision=highest
    )
    return row_tail(u_rows, spect, lat_local, depth_modes, depth_local, basis_z)


BF16 = jnp.bfloat16
F32 = jnp.float32
LANE = 128
GROUP = 8
SPAN = 256
TANH_A = 2.0 * math.sqrt(2.0 / math.pi)
TANH_B = 8.0 * 0.044715 * math.sqrt(2.0 / math.pi)


def basis64(length, modes):
    order = np.arange(modes)[:, None]
    place = np.arange(length)[None, :]
    scales = np.where(order == 0, math.sqrt(1.0 / length), math.sqrt(2.0 / length))
    return np.cos(math.pi * order * (place + 0.5) / length) * scales


def split64(array):
    high = array.astype(ml_dtypes.bfloat16)
    return high, (array - high.astype(np.float64)).astype(ml_dtypes.bfloat16)


def split(array):
    high = array.astype(BF16)
    return high, (array - high.astype(F32)).astype(BF16)


def split_outside(array):
    high = lax.reduce_precision(array, 8, 7)
    return high.astype(BF16), (array - high).astype(BF16)


def window_modes(rows, length, modes):
    place = np.arange(rows) - (rows - 1) / 2
    order = np.arange(modes)[:, None]
    _, se, ve = np.linalg.svd(np.cos(math.pi * order * place / length))
    _, so, vo = np.linalg.svd(np.sin(math.pi * order * place / length))
    top = max(se[0], so[0])
    both = sorted([(-w, 2 * n) for n, w in enumerate(se[: rows // 2])] + [(-w, 2 * n + 1) for n, w in enumerate(so[: rows // 2])])
    weights = np.array([-w for w, _ in both])
    count = int(np.sum(weights > top * 2.0**-23))
    fine = int(np.sum(weights > top * 0.25))
    fine += (count + fine) % 2
    funcs = np.stack([ve[: rows // 2], vo[: rows // 2]], axis=1).reshape(rows // 2 * 2, rows)
    assert [n for _, n in both[:count]] == list(range(count))
    return funcs[:count], fine


def forward_kernel(funcs, fine, by_ref, near_ref, far_ref, o_ref, cy_ref, acc_ref):
    step = pl.program_id(0)
    pairs = near_ref.shape[0]
    steps = funcs.shape[1] // (2 * pairs)
    modes_y = by_ref.shape[0] // 2
    count = funcs.shape[0]
    halves = cy_ref.shape[2] // SPAN

    def compress(before):
        for g in range(modes_y // GROUP):
            rows = slice(g * GROUP, (g + 1) * GROUP)
            for c in range(halves * SPAN // LANE):
                lanes = slice(c * LANE, (c + 1) * LANE)
                totals = [None if before == 0 else acc_ref[j, rows, lanes] for j in range(count)]
                for r in range(pairs):
                    x, y = cy_ref[r, rows, lanes], cy_ref[pairs + r, rows, lanes]
                    pair = (x + y, x - y)
                    for j in range(count):
                        term = pair[j % 2] * float(funcs[j, before * pairs + r])
                        totals[j] = term if totals[j] is None else totals[j] + term
                if before < steps - 1:
                    for j in range(count):
                        acc_ref[j, rows, lanes] = totals[j]
                    continue
                h, k = divmod(c, SPAN // LANE)
                place = slice(k * LANE, (k + 1) * LANE)
                slots = [total.astype(BF16).astype(F32) for total in totals]
                slots += [totals[j] - slots[j] for j in range(fine)]
                for j in range(0, count + fine, 2):
                    two = jnp.concatenate(slots[j : j + 2], axis=0).astype(BF16)
                    o_ref[g * halves + h, j * GROUP : (j + 2) * GROUP, place] = two

    def body(at):
        if at > 0:
            compress(at - 1)
        if at < steps:
            for r in range(pairs):
                for slot, row in ((r, near_ref[r]), (pairs + r, far_ref[pairs - 1 - r])):
                    z = jnp.dot(by_ref[...], row, preferred_element_type=F32)
                    cy_ref[slot] = z[:modes_y] + z[modes_y:]

    for at in range(steps + 1):
        pl.when(step == at)(functools.partial(body, at))


def mix_kernel(count, fine, r_ref, a_ref, b_ref, g_ref, w_ref, order_ref, place_ref, after_ref, o_ref, m_ref, back_ref):
    devices, packed, span = r_ref.shape
    modes_x = w_ref.shape[1]
    depth = a_ref.shape[1]
    highs, lows = count * GROUP, fine * GROUP
    tiles = [(k, slice(k * LANE, (k + 1) * LANE)) for k in range(span // LANE)]
    for i in range(devices):
        got = jnp.dot(r_ref[i], order_ref[...], preferred_element_type=F32)
        for k, lanes in tiles:
            m_ref[k, i * highs : i * highs + lows] = got[:lows, lanes] + got[highs:, lanes]
            m_ref[k, i * highs + lows : (i + 1) * highs] = got[lows:highs, lanes]
    if depth > devices * count:
        for k, _ in tiles:
            m_ref[k, devices * highs :] = jnp.zeros((depth * GROUP - devices * highs, LANE), F32)
    shifts = w_ref.shape[0]
    for q in range(GROUP):
        modes = [m_ref[k, pl.ds(q, depth, stride=GROUP), :] for k, _ in tiles]
        high, low = split(jnp.concatenate(modes, axis=1))
        z = jnp.dot(a_ref[...], jnp.concatenate([high, low], axis=1), preferred_element_type=F32)
        coef = z[:modes_x, :span] + z[modes_x:, :span] + z[:modes_x, span:]
        coef = coef * g_ref[q : q + 1, :]
        mixed = []
        for k, lanes in tiles:
            part = coef[:, lanes]
            total = part * w_ref[0]
            for n in range(1, shifts):
                total = total + pltpu.roll(part, n * (LANE // shifts), 1) * w_ref[n]
            mixed.append(total)
        high, low = split(jnp.concatenate(mixed, axis=1))
        right = jnp.concatenate([high, high, low, low], axis=0)
        z = jnp.dot(b_ref[...], right, preferred_element_type=F32)
        for k, lanes in tiles:
            back_ref[k, pl.ds(q, devices * count, stride=GROUP), :] = z[:, lanes]
    for i in range(devices):
        z = jnp.concatenate([back_ref[k, i * highs : (i + 1) * highs] for k, _ in tiles], axis=1)
        high = z.astype(BF16).astype(F32)
        both = jnp.concatenate([high, z[:lows] - high[:lows]], axis=0).astype(BF16)
        o_ref[i] = jnp.dot(both, place_ref[...], preferred_element_type=F32).astype(BF16)


def expand(funcs, fine, r_ref, b_ref):
    count, rows = funcs.shape
    modes_y = b_ref.shape[1] // 4
    halves = b_ref.shape[2] // SPAN

    def some(g, carry):
        at = pl.multiple_of(g * 2 * GROUP, 2 * GROUP)
        for h in range(halves):
            got = []
            for k in range(2):
                block = r_ref[(2 * g + k) * halves + h]
                got.append(block.astype(F32))
            for c in range(SPAN // LANE):
                part = slice(c * LANE, (c + 1) * LANE)
                modes = []
                for j in range(count):
                    pieces = []
                    for k in range(2):
                        piece = got[k][j * GROUP : (j + 1) * GROUP, part]
                        if j < fine:
                            low = got[k][(count + j) * GROUP : (count + j + 1) * GROUP, part]
                            piece = piece + low
                        pieces.append(piece)
                    modes.append(jnp.concatenate(pieces, axis=0))
                lanes = slice(h * SPAN + c * LANE, h * SPAN + (c + 1) * LANE)
                for t in range(rows // 2):
                    sums = []
                    for parity in range(2):
                        total = modes[parity] * float(0.5 * funcs[parity, t])
                        for j in range(parity + 2, count, 2):
                            total = total + modes[j] * float(0.5 * funcs[j, t])
                        sums.append(total)
                    for row, value in ((t, sums[0] + sums[1]), (rows - 1 - t, sums[0] - sums[1])):
                        high, low = split(value)
                        for n, half in enumerate((high, high, low, low)):
                            b_ref[row, pl.ds(at + n * modes_y, 2 * GROUP), lanes] = half
        return carry

    lax.fori_loop(0, modes_y // (2 * GROUP), some, 0)


def local_near_kernel(u_ref, l_ref, x_ref):
    rows, width, _ = u_ref.shape
    u = u_ref[...].reshape(rows * width, SPAN)
    x = jnp.dot(jnp.concatenate([u, u], axis=1), l_ref[...], preferred_element_type=F32)
    x_ref[...] = x.reshape(rows, width, SPAN)


def local_far_kernel(u_ref, l_ref, flip_ref, after_ref, x_ref, f_ref):
    local_near_kernel(u_ref, l_ref, x_ref)
    rows, width, _ = u_ref.shape
    u = u_ref[...].reshape(rows * width, SPAN)
    f = jnp.dot(u, flip_ref[...], preferred_element_type=F32)
    f_ref[...] = f.astype(BF16).reshape(rows, width, SPAN)


def weave(one, other):
    done = 0
    for n, step in enumerate(one):
        step()
        until = len(other) * (n + 1) // len(one)
        for at in range(done, until):
            other[at]()
        done = until


def tail_kernel(funcs, fine, chunk, r_ref, x0_ref, x1_ref, u_ref, f_ref, by_ref, w_ref, flip_ref, o_ref, b_ref, *scratch):
    step = pl.program_id(0)
    rows, width, _ = u_ref.shape
    first, parts, done = scratch[0:2], scratch[2:4], scratch[4:6]
    size = done[0].shape[0]
    count = rows * width // size
    near, far = slice(0, SPAN), slice(SPAN, 2 * SPAN)
    pieces = [(n, slice(y, y + chunk)) for n, y in enumerate(range(0, size, chunk))]
    units = range(2)

    def place(part, ys):
        row, y = divmod(part * size + ys.start, width)
        return row, slice(y, y + chunk)

    @pl.when(step == 0)
    def _():
        expand(funcs, fine, r_ref, b_ref)

    def run(lateral, depth):
        def stream(weights, passes):
            steps = []

            def push(n):
                for unit in units:
                    pltpu.matmul_push_rhs(weights(n, unit), n % 2, unit)

            def multiply(n, load, acc, left):
                for unit in units:
                    pltpu.matmul_acc_lhs(acc(unit), left(unit), load_staged_rhs=load)

            for n, batch in enumerate(passes):
                steps.append(functools.partial(push, n))
                for m, (acc, left) in enumerate(batch):
                    steps.append(functools.partial(multiply, n, n % 2 if m == 0 else None, acc, left))
            return steps

        def lateral_product(part):
            row = place(part, pieces[0][1])[0]
            batch = [
                (
                    lambda unit, n=n: lateral[part % 2][unit][n],
                    lambda unit, ys=ys: by_ref[place(part, ys)[1]],
                )
                for n, ys in pieces
            ]
            lanes = (near, far)
            return stream(lambda n, unit: b_ref[rows * step + row, :, lanes[unit]], [batch])

        def depth_product(part):
            def batch(low):
                def left(unit, ys):
                    at = (2 * unit + low) * SPAN
                    return parts[part % 2][ys, at : at + SPAN]

                return [
                    (lambda unit, n=n: depth[part % 2][unit][n], lambda unit, ys=ys: left(unit, ys))
                    for n, ys in pieces
                ]

            return stream(
                lambda n, unit: w_ref[unit, n * SPAN : (n + 1) * SPAN], [batch(0) + batch(1), batch(0)]
            )

        def finish(part):
            half = len(pieces) // 2
            accs = lateral[part % 2 ^ 1]
            batch = [
                (
                    lambda unit, n=n: accs[unit][n],
                    lambda unit, n=n: done[part % 2][pieces[n + half * unit][1]],
                )
                for n in range(half)
            ]

            def pop(n):
                for unit in units:
                    row, at = place(part, pieces[n + half * unit][1])
                    o_ref[row, at, far] = pltpu.matmul_pop(accs[unit][n]).astype(BF16)

            return stream(lambda n, unit: flip_ref[...], [batch]) + [functools.partial(pop, n) for n in range(half)]

        def lateral_points(part):
            def piece(n, ys):
                row, at = place(part, ys)
                h0 = pltpu.matmul_pop(lateral[part % 2][0][n]) + x0_ref[row, at]
                h1 = pltpu.matmul_pop(lateral[part % 2][1][n]) + x1_ref[row, at]
                f0 = u_ref[row, at].astype(F32) + twice_gelu(h0)
                f1 = f_ref[row, at].astype(F32) + twice_gelu(h1)
                first[part % 2][ys, near] = f0
                first[part % 2][ys, far] = f1
                for m, value in enumerate((f0 + f1, f0 - f1)):
                    high, low = split(value)
                    parts[part % 2][ys, 2 * m * SPAN : (2 * m + 1) * SPAN] = high
                    parts[part % 2][ys, (2 * m + 1) * SPAN : (2 * m + 2) * SPAN] = low

            return [functools.partial(piece, n, ys) for n, ys in pieces]

        def depth_points(part):
            def piece(n, ys):
                row, at = place(part, ys)
                even, odd = pltpu.matmul_pop(depth[part % 2][0][n]), pltpu.matmul_pop(depth[part % 2][1][n])
                o_ref[row, at, near] = (first[part % 2][ys, near] + twice_gelu(even + odd)).astype(BF16)
                done[part % 2][ys] = (first[part % 2][ys, far] + twice_gelu(even - odd)).astype(BF16)

            return [functools.partial(piece, n, ys) for n, ys in pieces]

        weave(lateral_product(0), [])
        weave(lateral_product(1), lateral_points(0))
        weave(depth_product(0), lateral_points(1))
        for part in range(count - 2):
            weave(depth_product(part + 1) + lateral_product(part + 2), depth_points(part))
            weave(finish(part), lateral_points(part + 2))
        weave(depth_product(count - 1), depth_points(count - 2))
        weave(finish(count - 2), depth_points(count - 1))
        weave(finish(count - 1), [])

    accs = [[[pltpu.ACC(unit)((chunk, SPAN), F32) for _ in pieces] for unit in units] for _ in range(2)]
    pl.run_scoped(run, accs, accs)


def twice_gelu(half):
    return half + half * jnp.tanh(half * (TANH_A + TANH_B * (half * half)))


def diagonals(matrices):
    n = matrices.shape[1]
    ids = np.arange(n)
    picks = (ids[None, :, None] == (ids[None, None, :] - ids[:, None, None]) % n).astype(np.float32)
    rows = jnp.sum(matrices[None] * picks[:, None], axis=2)
    return jnp.repeat(rows, LANE // n, axis=2)


def kron_eye(matrix, count):
    *lead, n, m = matrix.shape
    eye = jnp.eye(count, dtype=matrix.dtype)
    return (eye[:, None, :, None] * matrix[..., None, :, None, :]).reshape(*lead, count * n, count * m)


def fits(mesh_lat, rows, width_y, cells, chans, modes_x, modes_y):
    return (
        cells == 2 * SPAN
        and SPAN % (LANE // chans * chans) == 0
        and mesh_lat * GROUP * SPAN == modes_y * cells
        and rows % 4 == 0
        and rows >= 16
        and width_y % 256 == 0
        and 4 * modes_y == SPAN
        and modes_x % 8 == 0
    )


def shards(field, lat_modes, lat_gains, lat_local, depth_modes, depth_local):
    highest = lax.Precision.HIGHEST
    devices = lax.axis_size("lat")
    rows, width_y, cells = field.shape
    modes_x, chans, _ = lat_modes.shape
    modes_y = lat_gains.shape[0]
    modes_z = depth_modes.shape[0]
    if not fits(devices, rows, width_y, cells, chans, modes_x, modes_y):
        return plain_shards(field, lat_modes, lat_gains, lat_local, depth_modes, depth_local)
    depth = cells // chans
    width_x = rows * devices
    basis_x = basis64(width_x, modes_x)
    basis_y = basis64(width_y, modes_y)
    basis_z = basis64(depth, modes_z)
    funcs, fine = window_modes(rows, width_x, modes_x)
    count = funcs.shape[0]
    packed = (count + fine) * GROUP
    halves = cells // SPAN
    me = lax.axis_index("lat")

    by_high, by_low = split64(basis_y)
    by_forward = np.concatenate([by_high, by_low], axis=0)
    pairs = 4
    steps = rows // (2 * pairs)
    sent = pl.pallas_call(
        functools.partial(forward_kernel, funcs, fine),
        grid=(steps + 1,),
        in_specs=[
            pl.BlockSpec((2 * modes_y, width_y), lambda s: (0, 0)),
            pl.BlockSpec((pairs, width_y, cells), lambda s: (jnp.minimum(s, steps - 1), 0, 0)),
            pl.BlockSpec((pairs, width_y, cells), lambda s: (2 * steps - 1 - jnp.minimum(s, steps - 1), 0, 0)),
        ],
        out_specs=pl.BlockSpec((devices, packed, SPAN), lambda s: (0, 0, 0)),
        out_shape=jax.ShapeDtypeStruct((devices, packed, SPAN), BF16),
        scratch_shapes=[
            pltpu.VMEM((2 * pairs, modes_y, cells), F32),
            pltpu.VMEM((count, modes_y, cells), F32),
        ],
        compiler_params=pltpu.CompilerParams(vmem_limit_bytes=48 * 2**20),
        name="forward",
    )(by_forward, field, field)
    gathered = lax.all_to_all(sent, "lat", split_axis=0, concat_axis=0, tiled=True)

    per = SPAN // chans
    flip = np.kron(np.eye(per)[::-1], np.eye(chans)).astype(ml_dtypes.bfloat16)
    local_high, local_low = split_outside(kron_eye(0.5 * lat_local, per))
    local = jnp.concatenate([local_high, local_low], axis=0)
    turned = local.reshape(2 * SPAN, per, chans)[:, ::-1].reshape(2 * SPAN, SPAN)
    four = 4
    local_near = pl.pallas_call(
        local_near_kernel,
        grid=(rows // four,),
        in_specs=[
            pl.BlockSpec((four, width_y, SPAN), lambda s: (s, 0, 0)),
            pl.BlockSpec((2 * SPAN, SPAN), lambda s: (0, 0)),
        ],
        out_specs=pl.BlockSpec((four, width_y, SPAN), lambda s: (s, 0, 0)),
        out_shape=jax.ShapeDtypeStruct((rows, width_y, SPAN), F32),
        compiler_params=pltpu.CompilerParams(vmem_limit_bytes=48 * 2**20),
        name="local_near",
    )(field, local)

    weights = np.einsum("pit,jt->pij", basis_x.reshape(modes_x, devices, rows), funcs)
    flat = weights.reshape(modes_x, devices * count)
    ah, al = split64(np.pad(flat, ((0, 0), (0, -flat.shape[1] % LANE))))
    a_forward = np.concatenate([ah, al], axis=0)
    bh, bl = split64(flat.T)
    a_back = np.concatenate([bh, bl, bh, bl], axis=1)
    gains = lax.dynamic_slice_in_dim(lat_gains, (me // halves) * GROUP, GROUP, axis=0)
    gains = jnp.tile(jnp.repeat(gains, LANE // chans, axis=1), (1, SPAN // LANE))
    per_lane = LANE // chans
    ids = np.arange(LANE)
    order = np.zeros((LANE, LANE))
    order[ids, ids % chans * per_lane + ids // chans] = 1
    order = np.kron(np.eye(SPAN // LANE), order).astype(ml_dtypes.bfloat16)
    place = jnp.where(me % halves == 1, order.T @ flip, order.T)
    mixed = pl.pallas_call(
        functools.partial(mix_kernel, count, fine),
        in_specs=7 * [pl.BlockSpec(memory_space=pltpu.VMEM)] + [pl.BlockSpec(memory_space=pl.ANY)],
        out_shape=jax.ShapeDtypeStruct((devices, packed, SPAN), BF16),
        scratch_shapes=[
            pltpu.VMEM((SPAN // LANE, a_forward.shape[1] * GROUP, LANE), F32),
            pltpu.VMEM((SPAN // LANE, devices * count * GROUP, LANE), F32),
        ],
        compiler_params=pltpu.CompilerParams(vmem_limit_bytes=48 * 2**20),
        name="mix",
    )(gathered, a_forward, a_back, gains, diagonals(lat_modes), order, place, local_near)
    returned = lax.all_to_all(mixed, "lat", split_axis=0, concat_axis=0, tiled=True)

    local_far, mirrored = pl.pallas_call(
        local_far_kernel,
        grid=(rows // four,),
        in_specs=[
            pl.BlockSpec((four, width_y, SPAN), lambda s: (s, 0, 1)),
            pl.BlockSpec((2 * SPAN, SPAN), lambda s: (0, 0)),
            pl.BlockSpec((SPAN, SPAN), lambda s: (0, 0)),
            pl.BlockSpec(memory_space=pl.ANY),
        ],
        out_specs=2 * [pl.BlockSpec((four, width_y, SPAN), lambda s: (s, 0, 0))],
        out_shape=[
            jax.ShapeDtypeStruct((rows, width_y, SPAN), F32),
            jax.ShapeDtypeStruct((rows, width_y, SPAN), BF16),
        ],
        compiler_params=pltpu.CompilerParams(vmem_limit_bytes=48 * 2**20),
        name="local_far",
    )(field, turned, flip, mixed)

    by_back = np.concatenate([by_high, by_low, by_high, by_low], axis=0).T.copy()
    near_z = basis_z[:, :per].astype(np.float32)

    def depth_matrix(parity):
        b = near_z[parity::2]
        full = 0.5 * jnp.einsum(
            "kz,kw,kcd->zcwd", b, b, depth_modes[parity::2], precision=highest
        ).reshape(SPAN, SPAN) + 0.25 * kron_eye(depth_local, per)
        high, low = split_outside(full)
        return jnp.concatenate([high, low], axis=0)

    block = 4
    size = 256
    return pl.pallas_call(
        functools.partial(tail_kernel, funcs, fine, 32),
        grid=(rows // block,),
        in_specs=[
            pl.BlockSpec((devices, packed, SPAN), lambda s: (0, 0, 0)),
            pl.BlockSpec((block, width_y, SPAN), lambda s: (s, 0, 0)),
            pl.BlockSpec((block, width_y, SPAN), lambda s: (s, 0, 0)),
            pl.BlockSpec((block, width_y, SPAN), lambda s: (s, 0, 0)),
            pl.BlockSpec((block, width_y, SPAN), lambda s: (s, 0, 0)),
            pl.BlockSpec((width_y, SPAN), lambda s: (0, 0)),
            pl.BlockSpec((2, 2 * SPAN, SPAN), lambda s: (0, 0, 0)),
            pl.BlockSpec((SPAN, SPAN), lambda s: (0, 0)),
        ],
        out_specs=pl.BlockSpec((block, width_y, cells), lambda s: (s, 0, 0)),
        out_shape=jax.ShapeDtypeStruct(field.shape, BF16),
        scratch_shapes=[pltpu.VMEM((rows, 4 * modes_y, cells), BF16)]
        + 2 * [pltpu.VMEM((size, cells), F32)]
        + 2 * [pltpu.VMEM((size, 4 * SPAN), BF16)]
        + 2 * [pltpu.VMEM((size, SPAN), BF16)],
        compiler_params=pltpu.CompilerParams(vmem_limit_bytes=52 * 2**20),
        name="tail",
    )(
        returned,
        local_near,
        local_far,
        field,
        mirrored,
        by_back,
        jnp.stack([depth_matrix(0), depth_matrix(1)]),
        flip,
    )


def solution(mesh):
    placed = (P(("group", "lat"), None, None), P(), P(), P(), P(), P())
    return jax.shard_map(
        shards,
        mesh=mesh,
        in_specs=placed,
        out_specs=P(("group", "lat"), None, None),
        check_vma=False,
    )
```

```python
import functools
import math

import jax
import jax.numpy as jnp
import ml_dtypes
import numpy as np
from jax import lax
from jax.experimental import pallas as pl
from jax.experimental.pallas import tpu as pltpu
from jax.sharding import PartitionSpec as P


def cosine_basis(length, modes):
    order = jnp.arange(modes, dtype=jnp.float32)[:, None]
    place = jnp.arange(length, dtype=jnp.float32)[None, :]
    scales = jnp.where(order == 0.0, math.sqrt(1.0 / length), math.sqrt(2.0 / length))
    return jnp.cos(math.pi * order * (place + 0.5) / length) * scales


def row_tail(u_rows, spect, lat_local, depth_modes, depth_local, depth_basis):
    highest = lax.Precision.HIGHEST
    rows, width, cells = u_rows.shape
    chans = lat_local.shape[0]
    depth = cells // chans
    u4 = u_rows.reshape(rows, width, depth, chans)
    s4 = spect.reshape(rows, width, depth, chans)
    first = u4 + jax.nn.gelu(s4 + jnp.einsum("xyzc,cd->xyzd", u4, lat_local, precision=highest))
    dcoef = jnp.einsum("kz,xyzc->xykc", depth_basis, first, precision=highest)
    dmix = jnp.einsum("xykc,kcd->xykd", dcoef, depth_modes, precision=highest)
    dspect = jnp.einsum("kz,xykd->xyzd", depth_basis, dmix, precision=highest)
    final = first + jax.nn.gelu(
        dspect + jnp.einsum("xyzc,cd->xyzd", first, depth_local, precision=highest)
    )
    return final.reshape(rows, width, cells).astype(jnp.bfloat16)


def one_hot(ids, count):
    return (ids[:, None] == jnp.arange(count, dtype=jnp.int32)[None, :]).astype(jnp.float32)


def plain_shards(field, lat_modes, lat_gains, lat_local, depth_modes, depth_local):
    highest = lax.Precision.HIGHEST
    devices = lax.axis_size("lat")
    rows_dev, width_y, cells = field.shape
    modes_x, chans, _ = lat_modes.shape
    modes_y = lat_gains.shape[0]
    modes_z = depth_modes.shape[0]
    depth = cells // chans
    width_x = rows_dev * devices
    basis_x = cosine_basis(width_x, modes_x)
    basis_y = cosine_basis(width_y, modes_y)
    basis_z = cosine_basis(depth, modes_z)
    start = lax.axis_index("lat")
    u_rows = field.astype(jnp.float32)
    coef_y = jnp.einsum("qy,xyw->xqw", basis_y, u_rows, precision=highest)
    packed = coef_y.reshape(rows_dev, modes_y * cells)
    gathered = lax.all_to_all(packed, "lat", split_axis=1, concat_axis=0, tiled=True)
    span = gathered.shape[1]
    pairs = span // chans
    coef = jnp.dot(basis_x, gathered, precision=highest).reshape(modes_x, pairs, chans)
    mode_ids = (start * pairs + jnp.arange(pairs, dtype=jnp.int32)) // depth
    gain_rows = jnp.dot(one_hot(mode_ids, modes_y), lat_gains, precision=highest)
    mixed = jnp.einsum("jpc,jcd->jpd", coef * gain_rows[None, :, :], lat_modes, precision=highest)
    back_x = jnp.dot(basis_x.T, mixed.reshape(modes_x, span), precision=highest)
    returned = lax.all_to_all(back_x, "lat", split_axis=0, concat_axis=1, tiled=True)
    spect = jnp.einsum(
        "qy,xqw->xyw", basis_y, returned.reshape(rows_dev, modes_y, cells), precision=highest
    )
    return row_tail(u_rows, spect, lat_local, depth_modes, depth_local, basis_z)


BF16 = jnp.bfloat16
F32 = jnp.float32
LANE = 128
GROUP = 8
SPAN = 256
TANH_A = 2.0 * math.sqrt(2.0 / math.pi)
TANH_B = 8.0 * 0.044715 * math.sqrt(2.0 / math.pi)


def basis64(length, modes):
    order = np.arange(modes)[:, None]
    place = np.arange(length)[None, :]
    scales = np.where(order == 0, math.sqrt(1.0 / length), math.sqrt(2.0 / length))
    return np.cos(math.pi * order * (place + 0.5) / length) * scales


def split64(array):
    high = array.astype(ml_dtypes.bfloat16)
    return high, (array - high.astype(np.float64)).astype(ml_dtypes.bfloat16)


def split(array):
    high = array.astype(BF16)
    return high, (array - high.astype(F32)).astype(BF16)


def window_modes(rows, length, modes):
    place = np.arange(rows) - (rows - 1) / 2
    order = np.arange(modes)[:, None]
    _, se, ve = np.linalg.svd(np.cos(math.pi * order * place / length))
    _, so, vo = np.linalg.svd(np.sin(math.pi * order * place / length))
    top = max(se[0], so[0])
    both = sorted([(-w, 2 * n) for n, w in enumerate(se[: rows // 2])] + [(-w, 2 * n + 1) for n, w in enumerate(so[: rows // 2])])
    weights = np.array([-w for w, _ in both])
    count = int(np.sum(weights > top * 2.0**-23))
    fine = int(np.sum(weights > top * 0.25))
    fine += (count + fine) % 2
    funcs = np.stack([ve[: rows // 2], vo[: rows // 2]], axis=1).reshape(rows // 2 * 2, rows)
    assert [n for _, n in both[:count]] == list(range(count))
    return funcs[:count], fine


def forward_kernel(funcs, fine, by_ref, near_ref, far_ref, o_ref, cy_ref, acc_ref):
    step = pl.program_id(0)
    pairs = near_ref.shape[0]
    steps = funcs.shape[1] // (2 * pairs)
    modes_y = by_ref.shape[0] // 2
    count = funcs.shape[0]
    halves = cy_ref.shape[2] // SPAN

    def compress(before):
        for g in range(modes_y // GROUP):
            rows = slice(g * GROUP, (g + 1) * GROUP)
            for c in range(halves * SPAN // LANE):
                lanes = slice(c * LANE, (c + 1) * LANE)
                totals = [None if before == 0 else acc_ref[j, rows, lanes] for j in range(count)]
                for r in range(pairs):
                    x, y = cy_ref[r, rows, lanes], cy_ref[pairs + r, rows, lanes]
                    pair = (x + y, x - y)
                    for j in range(count):
                        term = pair[j % 2] * float(funcs[j, before * pairs + r])
                        totals[j] = term if totals[j] is None else totals[j] + term
                if before < steps - 1:
                    for j in range(count):
                        acc_ref[j, rows, lanes] = totals[j]
                    continue
                h, k = divmod(c, SPAN // LANE)
                place = slice(k * LANE, (k + 1) * LANE)
                slots = [total.astype(BF16).astype(F32) for total in totals]
                slots += [totals[j] - slots[j] for j in range(fine)]
                for j in range(0, count + fine, 2):
                    two = jnp.concatenate(slots[j : j + 2], axis=0).astype(BF16)
                    o_ref[g * halves + h, j * GROUP : (j + 2) * GROUP, place] = two

    def body(at):
        if at > 0:
            compress(at - 1)
        if at < steps:
            for r in range(pairs):
                for slot, row in ((r, near_ref[r]), (pairs + r, far_ref[pairs - 1 - r])):
                    z = jnp.dot(by_ref[...], row, preferred_element_type=F32)
                    cy_ref[slot] = z[:modes_y] + z[modes_y:]

    for at in range(steps + 1):
        pl.when(step == at)(functools.partial(body, at))


def mix_kernel(count, fine, r_ref, a_ref, b_ref, g_ref, w_ref, order_ref, place_ref, after_ref, o_ref, m_ref, back_ref):
    devices, packed, span = r_ref.shape
    modes_x = w_ref.shape[1]
    depth = a_ref.shape[1]
    highs, lows = count * GROUP, fine * GROUP
    tiles = [(k, slice(k * LANE, (k + 1) * LANE)) for k in range(span // LANE)]
    for i in range(devices):
        got = jnp.dot(r_ref[i], order_ref[...], preferred_element_type=F32)
        for k, lanes in tiles:
            m_ref[k, i * highs : i * highs + lows] = got[:lows, lanes] + got[highs:, lanes]
            m_ref[k, i * highs + lows : (i + 1) * highs] = got[lows:highs, lanes]
    if depth > devices * count:
        for k, _ in tiles:
            m_ref[k, devices * highs :] = jnp.zeros((depth * GROUP - devices * highs, LANE), F32)
    shifts = w_ref.shape[0]
    for q in range(GROUP):
        modes = [m_ref[k, pl.ds(q, depth, stride=GROUP), :] for k, _ in tiles]
        high, low = split(jnp.concatenate(modes, axis=1))
        z = jnp.dot(a_ref[...], jnp.concatenate([high, low], axis=1), preferred_element_type=F32)
        coef = z[:modes_x, :span] + z[modes_x:, :span] + z[:modes_x, span:]
        coef = coef * g_ref[q : q + 1, :]
        mixed = []
        for k, lanes in tiles:
            part = coef[:, lanes]
            total = part * w_ref[0]
            for n in range(1, shifts):
                total = total + pltpu.roll(part, n * (LANE // shifts), 1) * w_ref[n]
            mixed.append(total)
        high, low = split(jnp.concatenate(mixed, axis=1))
        right = jnp.concatenate([high, high, low, low], axis=0)
        z = jnp.dot(b_ref[...], right, preferred_element_type=F32)
        for k, lanes in tiles:
            back_ref[k, pl.ds(q, devices * count, stride=GROUP), :] = z[:, lanes]
    for i in range(devices):
        z = jnp.concatenate([back_ref[k, i * highs : (i + 1) * highs] for k, _ in tiles], axis=1)
        high = z.astype(BF16).astype(F32)
        both = jnp.concatenate([high, z[:lows] - high[:lows]], axis=0).astype(BF16)
        o_ref[i] = jnp.dot(both, place_ref[...], preferred_element_type=F32).astype(BF16)


def expand(funcs, fine, r_ref, b_ref):
    count, rows = funcs.shape
    modes_y = b_ref.shape[1] // 4
    halves = b_ref.shape[2] // SPAN

    def some(g, carry):
        at = pl.multiple_of(g * 2 * GROUP, 2 * GROUP)
        for h in range(halves):
            got = []
            for k in range(2):
                block = r_ref[(2 * g + k) * halves + h]
                got.append(block.astype(F32))
            for c in range(SPAN // LANE):
                part = slice(c * LANE, (c + 1) * LANE)
                modes = []
                for j in range(count):
                    pieces = []
                    for k in range(2):
                        piece = got[k][j * GROUP : (j + 1) * GROUP, part]
                        if j < fine:
                            low = got[k][(count + j) * GROUP : (count + j + 1) * GROUP, part]
                            piece = piece + low
                        pieces.append(piece)
                    modes.append(jnp.concatenate(pieces, axis=0))
                lanes = slice(h * SPAN + c * LANE, h * SPAN + (c + 1) * LANE)
                for t in range(rows // 2):
                    sums = []
                    for parity in range(2):
                        total = modes[parity] * float(0.5 * funcs[parity, t])
                        for j in range(parity + 2, count, 2):
                            total = total + modes[j] * float(0.5 * funcs[j, t])
                        sums.append(total)
                    for row, value in ((t, sums[0] + sums[1]), (rows - 1 - t, sums[0] - sums[1])):
                        high, low = split(value)
                        for n, half in enumerate((high, high, low, low)):
                            b_ref[row, pl.ds(at + n * modes_y, 2 * GROUP), lanes] = half
        return carry

    lax.fori_loop(0, modes_y // (2 * GROUP), some, 0)


def local_near_kernel(u_ref, l_ref, x_ref):
    rows, width, _ = u_ref.shape
    u = u_ref[...].reshape(rows * width, SPAN)
    x = jnp.dot(jnp.concatenate([u, u], axis=1), l_ref[...], preferred_element_type=F32)
    x_ref[...] = x.reshape(rows, width, SPAN)


def local_far_kernel(u_ref, l_ref, flip_ref, after_ref, x_ref, f_ref):
    local_near_kernel(u_ref, l_ref, x_ref)
    rows, width, _ = u_ref.shape
    u = u_ref[...].reshape(rows * width, SPAN)
    f = jnp.dot(u, flip_ref[...], preferred_element_type=F32)
    f_ref[...] = f.astype(BF16).reshape(rows, width, SPAN)


def weave(one, other):
    done = 0
    for n, step in enumerate(one):
        step()
        until = len(other) * (n + 1) // len(one)
        for at in range(done, until):
            other[at]()
        done = until


def prepare_kernel(l_ref, m_ref, d_ref, e_ref, et_ref, mask_ref, a_ref, b_ref, flip_ref, after_ref, near_ref, far_ref, w_ref):
    highest = lax.Precision.HIGHEST

    def dot(x, y):
        return jnp.dot(x, y, preferred_element_type=F32, precision=highest)

    def spread(ref):
        return dot(dot(et_ref[...], ref[...]), e_ref[...]) * mask_ref[...]

    for n, half in enumerate(split(0.5 * spread(l_ref))):
        near_ref[n * SPAN : (n + 1) * SPAN] = half
        far_ref[n * SPAN : (n + 1) * SPAN] = jnp.dot(half, flip_ref[...], preferred_element_type=F32).astype(BF16)
    local = 0.25 * spread(d_ref)
    for parity in range(2):
        modes = jnp.concatenate([m_ref[k] for k in range(parity, m_ref.shape[0], 2)], axis=0)
        full = dot(a_ref[parity], dot(modes, e_ref[...]) * b_ref[parity]) + local
        high, low = split(full)
        for n, half in enumerate((high, high, low)):
            w_ref[parity, n * SPAN : (n + 1) * SPAN] = half


def tail_kernel(funcs, fine, chunk, r_ref, x0_ref, x1_ref, u_ref, f_ref, by_ref, w_ref, flip_ref, o_ref, b_ref, *scratch):
    step = pl.program_id(0)
    last = pl.num_programs(0) - 1
    width = u_ref.shape[1]
    pre, first, parts, post, done = (scratch[n : n + 2] for n in range(0, 10, 2))
    near, far = slice(0, SPAN), slice(SPAN, 2 * SPAN)
    unit = pre[0].shape[0]
    pieces = range(0, unit, chunk)

    def where(n, y):
        return divmod(n * unit + y, width)

    def lateral_product(n):
        tall = min(unit, width)

        def piece(at, lanes):
            r, y = where(n, at)
            right = b_ref[u_ref.shape[0] * step + r, :, lanes]
            z = jnp.dot(by_ref[y : y + tall], right, preferred_element_type=F32)
            pre[n][at : at + tall, lanes] = z

        return [functools.partial(piece, at, lanes) for at in range(0, unit, tall) for lanes in (near, far)]

    def lateral_points(n):
        def piece(y):
            r, y0 = where(n, y)
            at, ys = slice(y, y + chunk), slice(y0, y0 + chunk)
            f0 = u_ref[r, ys].astype(F32) + twice_gelu(pre[n][at, near] + x0_ref[r, ys])
            f1 = f_ref[r, ys].astype(F32) + twice_gelu(pre[n][at, far] + x1_ref[r, ys])
            first[n][at, near] = f0
            first[n][at, far] = f1
            for m, value in enumerate((f0 + f1, f0 - f1)):
                high, low = split(value)
                parts[n][at, 2 * m * SPAN : (2 * m + 1) * SPAN] = high
                parts[n][at, (2 * m + 1) * SPAN : (2 * m + 2) * SPAN] = low

        return [functools.partial(piece, y) for y in pieces]

    def depth_product(n):
        def piece(m, lanes):
            high = parts[n][:, 2 * m * SPAN : (2 * m + 1) * SPAN]
            low = parts[n][:, (2 * m + 1) * SPAN : (2 * m + 2) * SPAN]
            left = jnp.concatenate([high, low, high], axis=1)
            post[n][:, lanes] = jnp.dot(left, w_ref[m], preferred_element_type=F32)

        return [functools.partial(piece, m, lanes) for m, lanes in enumerate((near, far))]

    def depth_points(n):
        def piece(y):
            r, y0 = where(n, y)
            at, ys = slice(y, y + chunk), slice(y0, y0 + chunk)
            even, odd = post[n][at, near], post[n][at, far]
            o_ref[r, ys, near] = (first[n][at, near] + twice_gelu(even + odd)).astype(BF16)
            done[n][at] = (first[n][at, far] + twice_gelu(even - odd)).astype(BF16)

        return [functools.partial(piece, y) for y in pieces]

    def finish(n):
        def piece():
            z = jnp.dot(done[n][...], flip_ref[...], preferred_element_type=F32).astype(BF16)
            for at in range(0, unit, min(unit, width)):
                r, y0 = where(n, at)
                o_ref[r, y0 : y0 + min(unit, width), far] = z[at : at + min(unit, width)]

        return [piece]

    @pl.when(step == 0)
    def _():
        expand(funcs, fine, r_ref, b_ref)
        weave(lateral_product(0), [])
        weave(lateral_product(1), lateral_points(0))
        weave(depth_product(0), lateral_points(1))

    @pl.when(jnp.logical_and(step > 0, step < last))
    def _():
        weave(depth_product(1), depth_points(0))
        weave(lateral_product(0) + finish(0), depth_points(1))
        weave(lateral_product(1) + finish(1), lateral_points(0))
        weave(depth_product(0), lateral_points(1))

    @pl.when(step == last)
    def _():
        weave(depth_product(1), depth_points(0))
        weave(finish(0), depth_points(1))
        weave(finish(1), [])


def twice_gelu(half):
    return half + half * jnp.tanh(half * (TANH_A + TANH_B * (half * half)))


def diagonals(matrices):
    n = matrices.shape[1]
    ids = np.arange(n)
    picks = (ids[None, :, None] == (ids[None, None, :] - ids[:, None, None]) % n).astype(np.float32)
    rows = jnp.sum(matrices[None] * picks[:, None], axis=2)
    return jnp.repeat(rows, LANE // n, axis=2)


def fits(mesh_lat, rows, width_y, cells, chans, modes_x, modes_y):
    return (
        cells == 2 * SPAN
        and SPAN % (LANE // chans * chans) == 0
        and mesh_lat * GROUP * SPAN == modes_y * cells
        and rows % 4 == 0
        and rows >= 16
        and width_y % 256 == 0
        and 4 * modes_y == SPAN
        and modes_x % 8 == 0
    )


def shards(field, lat_modes, lat_gains, lat_local, depth_modes, depth_local):
    devices = lax.axis_size("lat")
    rows, width_y, cells = field.shape
    modes_x, chans, _ = lat_modes.shape
    modes_y = lat_gains.shape[0]
    modes_z = depth_modes.shape[0]
    if not fits(devices, rows, width_y, cells, chans, modes_x, modes_y):
        return plain_shards(field, lat_modes, lat_gains, lat_local, depth_modes, depth_local)
    depth = cells // chans
    width_x = rows * devices
    basis_x = basis64(width_x, modes_x)
    basis_y = basis64(width_y, modes_y)
    basis_z = basis64(depth, modes_z)
    funcs, fine = window_modes(rows, width_x, modes_x)
    count = funcs.shape[0]
    packed = (count + fine) * GROUP
    halves = cells // SPAN
    me = lax.axis_index("lat")

    by_high, by_low = split64(basis_y)
    by_forward = np.concatenate([by_high, by_low], axis=0)
    pairs = 4
    steps = rows // (2 * pairs)
    sent = pl.pallas_call(
        functools.partial(forward_kernel, funcs, fine),
        grid=(steps + 1,),
        in_specs=[
            pl.BlockSpec((2 * modes_y, width_y), lambda s: (0, 0)),
            pl.BlockSpec((pairs, width_y, cells), lambda s: (jnp.minimum(s, steps - 1), 0, 0)),
            pl.BlockSpec((pairs, width_y, cells), lambda s: (2 * steps - 1 - jnp.minimum(s, steps - 1), 0, 0)),
        ],
        out_specs=pl.BlockSpec((devices, packed, SPAN), lambda s: (0, 0, 0)),
        out_shape=jax.ShapeDtypeStruct((devices, packed, SPAN), BF16),
        scratch_shapes=[
            pltpu.VMEM((2 * pairs, modes_y, cells), F32),
            pltpu.VMEM((count, modes_y, cells), F32),
        ],
        compiler_params=pltpu.CompilerParams(vmem_limit_bytes=48 * 2**20),
        name="forward",
    )(by_forward, field, field)
    gathered = lax.all_to_all(sent, "lat", split_axis=0, concat_axis=0, tiled=True)

    per = SPAN // chans
    flip = np.kron(np.eye(per)[::-1], np.eye(chans)).astype(ml_dtypes.bfloat16)
    near_z = basis_z[:, :per]
    ids = np.arange(SPAN)
    pick = (np.arange(chans)[:, None] == ids[None, :] % chans).astype(np.float32)
    mask = (ids[:, None] // chans == ids[None, :] // chans).astype(np.float32)
    halved = [near_z[parity::2] for parity in range(2)]
    outer = np.stack([0.5 * np.kron(b.T, np.eye(chans)) for b in halved]).astype(np.float32)
    inner = np.stack([np.kron(b, np.ones((chans, chans))) for b in halved]).astype(np.float32)
    anywhere = pl.BlockSpec(memory_space=pl.ANY)
    local, turned, depth_weights = pl.pallas_call(
        prepare_kernel,
        in_specs=9 * [pl.BlockSpec(memory_space=pltpu.VMEM)] + [anywhere],
        out_shape=[
            jax.ShapeDtypeStruct((2 * SPAN, SPAN), BF16),
            jax.ShapeDtypeStruct((2 * SPAN, SPAN), BF16),
            jax.ShapeDtypeStruct((2, 3 * SPAN, SPAN), BF16),
        ],
        compiler_params=pltpu.CompilerParams(vmem_limit_bytes=24 * 2**20),
        name="prepare",
    )(lat_local, depth_modes, depth_local, pick, pick.T.copy(), mask, outer, inner, flip, sent)
    four = 4
    local_near = pl.pallas_call(
        local_near_kernel,
        grid=(rows // four,),
        in_specs=[
            pl.BlockSpec((four, width_y, SPAN), lambda s: (s, 0, 0)),
            pl.BlockSpec((2 * SPAN, SPAN), lambda s: (0, 0)),
        ],
        out_specs=pl.BlockSpec((four, width_y, SPAN), lambda s: (s, 0, 0)),
        out_shape=jax.ShapeDtypeStruct((rows, width_y, SPAN), F32),
        compiler_params=pltpu.CompilerParams(vmem_limit_bytes=48 * 2**20),
        name="local_near",
    )(field, local)

    weights = np.einsum("pit,jt->pij", basis_x.reshape(modes_x, devices, rows), funcs)
    flat = weights.reshape(modes_x, devices * count)
    ah, al = split64(np.pad(flat, ((0, 0), (0, -flat.shape[1] % LANE))))
    a_forward = np.concatenate([ah, al], axis=0)
    bh, bl = split64(flat.T)
    a_back = np.concatenate([bh, bl, bh, bl], axis=1)
    gains = lax.dynamic_slice_in_dim(lat_gains, (me // halves) * GROUP, GROUP, axis=0)
    gains = jnp.tile(jnp.repeat(gains, LANE // chans, axis=1), (1, SPAN // LANE))
    per_lane = LANE // chans
    ids = np.arange(LANE)
    order = np.zeros((LANE, LANE))
    order[ids, ids % chans * per_lane + ids // chans] = 1
    order = np.kron(np.eye(SPAN // LANE), order).astype(ml_dtypes.bfloat16)
    place = jnp.where(me % halves == 1, order.T @ flip, order.T)
    mixed = pl.pallas_call(
        functools.partial(mix_kernel, count, fine),
        in_specs=7 * [pl.BlockSpec(memory_space=pltpu.VMEM)] + [pl.BlockSpec(memory_space=pl.ANY)],
        out_shape=jax.ShapeDtypeStruct((devices, packed, SPAN), BF16),
        scratch_shapes=[
            pltpu.VMEM((SPAN // LANE, a_forward.shape[1] * GROUP, LANE), F32),
            pltpu.VMEM((SPAN // LANE, devices * count * GROUP, LANE), F32),
        ],
        compiler_params=pltpu.CompilerParams(vmem_limit_bytes=48 * 2**20),
        name="mix",
    )(gathered, a_forward, a_back, gains, diagonals(lat_modes), order, place, local_near)
    returned = lax.all_to_all(mixed, "lat", split_axis=0, concat_axis=0, tiled=True)

    local_far, mirrored = pl.pallas_call(
        local_far_kernel,
        grid=(rows // four,),
        in_specs=[
            pl.BlockSpec((four, width_y, SPAN), lambda s: (s, 0, 1)),
            pl.BlockSpec((2 * SPAN, SPAN), lambda s: (0, 0)),
            pl.BlockSpec((SPAN, SPAN), lambda s: (0, 0)),
            pl.BlockSpec(memory_space=pl.ANY),
        ],
        out_specs=2 * [pl.BlockSpec((four, width_y, SPAN), lambda s: (s, 0, 0))],
        out_shape=[
            jax.ShapeDtypeStruct((rows, width_y, SPAN), F32),
            jax.ShapeDtypeStruct((rows, width_y, SPAN), BF16),
        ],
        compiler_params=pltpu.CompilerParams(vmem_limit_bytes=48 * 2**20),
        name="local_far",
    )(field, turned, flip, mixed)

    by_back = np.concatenate([by_high, by_low, by_high, by_low], axis=0).T.copy()
    block = 4
    unit = block * width_y // 2
    wide = (unit, cells)
    narrow = (unit, SPAN)
    steps = rows // block
    return pl.pallas_call(
        functools.partial(tail_kernel, funcs, fine, 16),
        grid=(steps + 1,),
        in_specs=[
            pl.BlockSpec((devices, packed, SPAN), lambda s: (0, 0, 0)),
            pl.BlockSpec((block, width_y, SPAN), lambda s: (jnp.minimum(s, steps - 1), 0, 0)),
            pl.BlockSpec((block, width_y, SPAN), lambda s: (jnp.minimum(s, steps - 1), 0, 0)),
            pl.BlockSpec((block, width_y, SPAN), lambda s: (jnp.minimum(s, steps - 1), 0, 0)),
            pl.BlockSpec((block, width_y, SPAN), lambda s: (jnp.minimum(s, steps - 1), 0, 0)),
            pl.BlockSpec((width_y, SPAN), lambda s: (0, 0)),
            pl.BlockSpec((2, 3 * SPAN, SPAN), lambda s: (0, 0, 0)),
            pl.BlockSpec((SPAN, SPAN), lambda s: (0, 0)),
        ],
        out_specs=pl.BlockSpec((block, width_y, cells), lambda s: (jnp.maximum(s - 1, 0), 0, 0)),
        out_shape=jax.ShapeDtypeStruct(field.shape, BF16),
        scratch_shapes=[pltpu.VMEM((rows, 4 * modes_y, cells), BF16)]
        + 2 * [pltpu.VMEM(wide, F32)]
        + 2 * [pltpu.VMEM(wide, F32)]
        + 2 * [pltpu.VMEM((unit, 4 * SPAN), BF16)]
        + 2 * [pltpu.VMEM(wide, F32)]
        + 2 * [pltpu.VMEM(narrow, BF16)],
        compiler_params=pltpu.CompilerParams(vmem_limit_bytes=58 * 2**20),
        name="tail",
    )(
        returned,
        local_near,
        local_far,
        field,
        mirrored,
        by_back,
        depth_weights,
        flip,
    )


def solution(mesh):
    placed = (P(("group", "lat"), None, None), P(), P(), P(), P(), P())
    return jax.shard_map(
        shards,
        mesh=mesh,
        in_specs=placed,
        out_specs=P(("group", "lat"), None, None),
        check_vma=False,
    )
```

```python
import functools
import math

import jax
import jax.numpy as jnp
import ml_dtypes
import numpy as np
from jax import lax
from jax.experimental import pallas as pl
from jax.experimental.pallas import tpu as pltpu
from jax.sharding import PartitionSpec as P


def cosine_basis(length, modes):
    order = jnp.arange(modes, dtype=jnp.float32)[:, None]
    place = jnp.arange(length, dtype=jnp.float32)[None, :]
    scales = jnp.where(order == 0.0, math.sqrt(1.0 / length), math.sqrt(2.0 / length))
    return jnp.cos(math.pi * order * (place + 0.5) / length) * scales


def row_tail(u_rows, spect, lat_local, depth_modes, depth_local, depth_basis):
    highest = lax.Precision.HIGHEST
    rows, width, cells = u_rows.shape
    chans = lat_local.shape[0]
    depth = cells // chans
    u4 = u_rows.reshape(rows, width, depth, chans)
    s4 = spect.reshape(rows, width, depth, chans)
    first = u4 + jax.nn.gelu(s4 + jnp.einsum("xyzc,cd->xyzd", u4, lat_local, precision=highest))
    dcoef = jnp.einsum("kz,xyzc->xykc", depth_basis, first, precision=highest)
    dmix = jnp.einsum("xykc,kcd->xykd", dcoef, depth_modes, precision=highest)
    dspect = jnp.einsum("kz,xykd->xyzd", depth_basis, dmix, precision=highest)
    final = first + jax.nn.gelu(
        dspect + jnp.einsum("xyzc,cd->xyzd", first, depth_local, precision=highest)
    )
    return final.reshape(rows, width, cells).astype(jnp.bfloat16)


def one_hot(ids, count):
    return (ids[:, None] == jnp.arange(count, dtype=jnp.int32)[None, :]).astype(jnp.float32)


def plain_shards(field, lat_modes, lat_gains, lat_local, depth_modes, depth_local):
    highest = lax.Precision.HIGHEST
    devices = lax.axis_size("lat")
    rows_dev, width_y, cells = field.shape
    modes_x, chans, _ = lat_modes.shape
    modes_y = lat_gains.shape[0]
    modes_z = depth_modes.shape[0]
    depth = cells // chans
    width_x = rows_dev * devices
    basis_x = cosine_basis(width_x, modes_x)
    basis_y = cosine_basis(width_y, modes_y)
    basis_z = cosine_basis(depth, modes_z)
    start = lax.axis_index("lat")
    u_rows = field.astype(jnp.float32)
    coef_y = jnp.einsum("qy,xyw->xqw", basis_y, u_rows, precision=highest)
    packed = coef_y.reshape(rows_dev, modes_y * cells)
    gathered = lax.all_to_all(packed, "lat", split_axis=1, concat_axis=0, tiled=True)
    span = gathered.shape[1]
    pairs = span // chans
    coef = jnp.dot(basis_x, gathered, precision=highest).reshape(modes_x, pairs, chans)
    mode_ids = (start * pairs + jnp.arange(pairs, dtype=jnp.int32)) // depth
    gain_rows = jnp.dot(one_hot(mode_ids, modes_y), lat_gains, precision=highest)
    mixed = jnp.einsum("jpc,jcd->jpd", coef * gain_rows[None, :, :], lat_modes, precision=highest)
    back_x = jnp.dot(basis_x.T, mixed.reshape(modes_x, span), precision=highest)
    returned = lax.all_to_all(back_x, "lat", split_axis=0, concat_axis=1, tiled=True)
    spect = jnp.einsum(
        "qy,xqw->xyw", basis_y, returned.reshape(rows_dev, modes_y, cells), precision=highest
    )
    return row_tail(u_rows, spect, lat_local, depth_modes, depth_local, basis_z)


BF16 = jnp.bfloat16
F32 = jnp.float32
LANE = 128
GROUP = 8
SPAN = 256
TANH_A = 2.0 * math.sqrt(2.0 / math.pi)
TANH_B = 8.0 * 0.044715 * math.sqrt(2.0 / math.pi)


def basis64(length, modes):
    order = np.arange(modes)[:, None]
    place = np.arange(length)[None, :]
    scales = np.where(order == 0, math.sqrt(1.0 / length), math.sqrt(2.0 / length))
    return np.cos(math.pi * order * (place + 0.5) / length) * scales


def split64(array):
    high = array.astype(ml_dtypes.bfloat16)
    return high, (array - high.astype(np.float64)).astype(ml_dtypes.bfloat16)


def split(array):
    high = array.astype(BF16)
    return high, (array - high.astype(F32)).astype(BF16)


def window_modes(rows, length, modes):
    place = np.arange(rows) - (rows - 1) / 2
    order = np.arange(modes)[:, None]
    _, se, ve = np.linalg.svd(np.cos(math.pi * order * place / length))
    _, so, vo = np.linalg.svd(np.sin(math.pi * order * place / length))
    top = max(se[0], so[0])
    both = sorted([(-w, 2 * n) for n, w in enumerate(se[: rows // 2])] + [(-w, 2 * n + 1) for n, w in enumerate(so[: rows // 2])])
    weights = np.array([-w for w, _ in both])
    count = int(np.sum(weights > top * 2.0**-23))
    fine = int(np.sum(weights > top * 0.25))
    fine += (count + fine) % 2
    funcs = np.stack([ve[: rows // 2], vo[: rows // 2]], axis=1).reshape(rows // 2 * 2, rows)
    assert [n for _, n in both[:count]] == list(range(count))
    return funcs[:count], fine


def forward_kernel(funcs, fine, by_ref, near_ref, far_ref, o_ref, cy_ref, acc_ref):
    step = pl.program_id(0)
    pairs = near_ref.shape[0]
    steps = funcs.shape[1] // (2 * pairs)
    modes_y = by_ref.shape[0] // 2
    count = funcs.shape[0]
    halves = cy_ref.shape[2] // SPAN

    def compress(before):
        for g in range(modes_y // GROUP):
            rows = slice(g * GROUP, (g + 1) * GROUP)
            for c in range(halves * SPAN // LANE):
                lanes = slice(c * LANE, (c + 1) * LANE)
                totals = [None if before == 0 else acc_ref[j, rows, lanes] for j in range(count)]
                for r in range(pairs):
                    x, y = cy_ref[r, rows, lanes], cy_ref[pairs + r, rows, lanes]
                    pair = (x + y, x - y)
                    for j in range(count):
                        term = pair[j % 2] * float(funcs[j, before * pairs + r])
                        totals[j] = term if totals[j] is None else totals[j] + term
                if before < steps - 1:
                    for j in range(count):
                        acc_ref[j, rows, lanes] = totals[j]
                    continue
                h, k = divmod(c, SPAN // LANE)
                place = slice(k * LANE, (k + 1) * LANE)
                slots = [total.astype(BF16).astype(F32) for total in totals]
                slots += [totals[j] - slots[j] for j in range(fine)]
                for j in range(0, count + fine, 2):
                    two = jnp.concatenate(slots[j : j + 2], axis=0).astype(BF16)
                    o_ref[g * halves + h, j * GROUP : (j + 2) * GROUP, place] = two

    def body(at):
        if at > 0:
            compress(at - 1)
        if at < steps:
            for r in range(pairs):
                for slot, row in ((r, near_ref[r]), (pairs + r, far_ref[pairs - 1 - r])):
                    z = jnp.dot(by_ref[...], row, preferred_element_type=F32)
                    cy_ref[slot] = z[:modes_y] + z[modes_y:]

    for at in range(steps + 1):
        pl.when(step == at)(functools.partial(body, at))


def mix_kernel(count, fine, r_ref, a_ref, b_ref, g_ref, w_ref, order_ref, place_ref, after_ref, o_ref, m_ref, back_ref):
    devices, packed, span = r_ref.shape
    modes_x = w_ref.shape[1]
    depth = a_ref.shape[1]
    highs, lows = count * GROUP, fine * GROUP
    tiles = [(k, slice(k * LANE, (k + 1) * LANE)) for k in range(span // LANE)]
    for i in range(devices):
        got = jnp.dot(r_ref[i], order_ref[...], preferred_element_type=F32)
        for k, lanes in tiles:
            m_ref[k, i * highs : i * highs + lows] = got[:lows, lanes] + got[highs:, lanes]
            m_ref[k, i * highs + lows : (i + 1) * highs] = got[lows:highs, lanes]
    if depth > devices * count:
        for k, _ in tiles:
            m_ref[k, devices * highs :] = jnp.zeros((depth * GROUP - devices * highs, LANE), F32)
    shifts = w_ref.shape[0]
    for q in range(GROUP):
        modes = [m_ref[k, pl.ds(q, depth, stride=GROUP), :] for k, _ in tiles]
        high, low = split(jnp.concatenate(modes, axis=1))
        z = jnp.dot(a_ref[...], jnp.concatenate([high, low], axis=1), preferred_element_type=F32)
        coef = z[:modes_x, :span] + z[modes_x:, :span] + z[:modes_x, span:]
        coef = coef * g_ref[q : q + 1, :]
        mixed = []
        for k, lanes in tiles:
            part = coef[:, lanes]
            total = part * w_ref[0]
            for n in range(1, shifts):
                total = total + pltpu.roll(part, n * (LANE // shifts), 1) * w_ref[n]
            mixed.append(total)
        high, low = split(jnp.concatenate(mixed, axis=1))
        right = jnp.concatenate([high, high, low, low], axis=0)
        z = jnp.dot(b_ref[...], right, preferred_element_type=F32)
        for k, lanes in tiles:
            back_ref[k, pl.ds(q, devices * count, stride=GROUP), :] = z[:, lanes]
    for i in range(devices):
        z = jnp.concatenate([back_ref[k, i * highs : (i + 1) * highs] for k, _ in tiles], axis=1)
        high = z.astype(BF16).astype(F32)
        both = jnp.concatenate([high, z[:lows] - high[:lows]], axis=0).astype(BF16)
        o_ref[i] = jnp.dot(both, place_ref[...], preferred_element_type=F32).astype(BF16)


def expand(r_ref, v_ref, b_ref):
    rows = b_ref.shape[0]
    modes_y = b_ref.shape[1] // 2
    halves = b_ref.shape[2] // SPAN
    for g in range(modes_y // (2 * GROUP)):
        at = g * 2 * GROUP
        for h in range(halves):
            got = []
            for k in range(2):
                block = r_ref[(2 * g + k) * halves + h]
                z = jnp.dot(v_ref[...], block, preferred_element_type=F32)
                got.append(z[: rows * GROUP] + z[rows * GROUP :])
            lanes = slice(h * SPAN, (h + 1) * SPAN)
            for t in range(rows):
                part = slice(t * GROUP, (t + 1) * GROUP)
                high, low = split(jnp.concatenate([got[0][part], got[1][part]], axis=0))
                b_ref[t, at : at + 2 * GROUP, lanes] = high
                b_ref[t, modes_y + at : modes_y + at + 2 * GROUP, lanes] = low


def local_near_kernel(u_ref, l_ref, x_ref):
    rows, width, _ = u_ref.shape
    u = u_ref[...].reshape(rows * width, SPAN)
    x = jnp.dot(jnp.concatenate([u, u], axis=1), l_ref[...], preferred_element_type=F32)
    x_ref[...] = x.reshape(rows, width, SPAN)


def local_far_kernel(u_ref, l_ref, flip_ref, after_ref, x_ref, f_ref):
    local_near_kernel(u_ref, l_ref, x_ref)
    rows, width, _ = u_ref.shape
    u = u_ref[...].reshape(rows * width, SPAN)
    f = jnp.dot(u, flip_ref[...], preferred_element_type=F32)
    f_ref[...] = f.astype(BF16).reshape(rows, width, SPAN)


def weave(one, other):
    done = 0
    for n, step in enumerate(one):
        step()
        until = len(other) * (n + 1) // len(one)
        for at in range(done, until):
            other[at]()
        done = until


def prepare_kernel(l_ref, m_ref, d_ref, e_ref, et_ref, mask_ref, a_ref, b_ref, flip_ref, after_ref, near_ref, far_ref, w_ref):
    highest = lax.Precision.HIGHEST

    def dot(x, y):
        return jnp.dot(x, y, preferred_element_type=F32, precision=highest)

    def spread(ref):
        return dot(dot(et_ref[...], ref[...]), e_ref[...]) * mask_ref[...]

    for n, half in enumerate(split(0.5 * spread(l_ref))):
        near_ref[n * SPAN : (n + 1) * SPAN] = half
        far_ref[n * SPAN : (n + 1) * SPAN] = jnp.dot(half, flip_ref[...], preferred_element_type=F32).astype(BF16)
    local = 0.25 * spread(d_ref)
    for parity in range(2):
        modes = jnp.concatenate([m_ref[k] for k in range(parity, m_ref.shape[0], 2)], axis=0)
        full = dot(a_ref[parity], dot(modes, e_ref[...]) * b_ref[parity]) + local
        high, low = split(full)
        for n, half in enumerate((high, high, low)):
            w_ref[parity, n * SPAN : (n + 1) * SPAN] = half


def tail_kernel(chunk, r_ref, x0_all, x1_all, u_all, f_all, by_ref, w_ref, flip_ref, v_ref, o_ref, b_ref, *scratch):
    step = pl.program_id(0)
    last = pl.num_programs(0) - 1
    pre, first, parts, post, done = (scratch[n : n + 2] for n in range(0, 10, 2))
    held, arrived = scratch[10:14], scratch[14]
    block, width = held[0].shape[1:3]
    modes_y = b_ref.shape[1] // 2
    x0_ref, x1_ref, u_ref, f_ref = (ref.at[lax.rem(step, 2)] for ref in held)

    def copies(at):
        slot = lax.rem(at, 2)
        return [
            pltpu.make_async_copy(
                source.at[pl.ds(at * block, block), :, pl.ds(0, SPAN)], ref.at[slot], arrived.at[slot, n]
            )
            for n, (source, ref) in enumerate(zip((x0_all, x1_all, u_all, f_all), held))
        ]

    near, far = slice(0, SPAN), slice(SPAN, 2 * SPAN)
    unit = pre[0].shape[0]
    pieces = range(0, unit, chunk)

    def where(n, y):
        return divmod(n * unit + y, width)

    def lateral_product(n):
        tall = min(unit, width)

        def piece(at, lanes):
            r, y = where(n, at)
            high, low = b_ref[block * step + r, :modes_y, lanes], b_ref[block * step + r, modes_y:, lanes]
            right = jnp.concatenate([high, high, low, low], axis=0)
            z = jnp.dot(by_ref[y : y + tall], right, preferred_element_type=F32)
            pre[n][at : at + tall, lanes] = z

        return [functools.partial(piece, at, lanes) for at in range(0, unit, tall) for lanes in (near, far)]

    def lateral_points(n):
        def piece(y):
            r, y0 = where(n, y)
            at, ys = slice(y, y + chunk), slice(y0, y0 + chunk)
            f0 = u_ref[r, ys].astype(F32) + twice_gelu(pre[n][at, near] + x0_ref[r, ys])
            f1 = f_ref[r, ys].astype(F32) + twice_gelu(pre[n][at, far] + x1_ref[r, ys])
            first[n][at, near] = f0
            first[n][at, far] = f1
            for m, value in enumerate((f0 + f1, f0 - f1)):
                high, low = split(value)
                parts[n][at, 2 * m * SPAN : (2 * m + 1) * SPAN] = high
                parts[n][at, (2 * m + 1) * SPAN : (2 * m + 2) * SPAN] = low

        return [functools.partial(piece, y) for y in pieces]

    def depth_product(n):
        def piece(m, lanes):
            high = parts[n][:, 2 * m * SPAN : (2 * m + 1) * SPAN]
            low = parts[n][:, (2 * m + 1) * SPAN : (2 * m + 2) * SPAN]
            left = jnp.concatenate([high, low, high], axis=1)
            post[n][:, lanes] = jnp.dot(left, w_ref[m], preferred_element_type=F32)

        return [functools.partial(piece, m, lanes) for m, lanes in enumerate((near, far))]

    def depth_points(n):
        def piece(y):
            r, y0 = where(n, y)
            at, ys = slice(y, y + chunk), slice(y0, y0 + chunk)
            even, odd = post[n][at, near], post[n][at, far]
            o_ref[r, ys, near] = (first[n][at, near] + twice_gelu(even + odd)).astype(BF16)
            done[n][at] = (first[n][at, far] + twice_gelu(even - odd)).astype(BF16)

        return [functools.partial(piece, y) for y in pieces]

    def finish(n):
        def piece():
            z = jnp.dot(done[n][...], flip_ref[...], preferred_element_type=F32).astype(BF16)
            for at in range(0, unit, min(unit, width)):
                r, y0 = where(n, at)
                o_ref[r, y0 : y0 + min(unit, width), far] = z[at : at + min(unit, width)]

        return [piece]

    @pl.when(step == 0)
    def _():
        for copy in copies(step):
            copy.start()

    @pl.when(step < last - 1)
    def _():
        for copy in copies(step + 1):
            copy.start()

    @pl.when(step == 0)
    def _():
        expand(r_ref, v_ref, b_ref)

    @pl.when(step < last)
    def _():
        for copy in copies(step):
            copy.wait()

    @pl.when(step == 0)
    def _():
        weave(lateral_product(0), [])
        weave(lateral_product(1), lateral_points(0))
        weave(depth_product(0), lateral_points(1))

    @pl.when(jnp.logical_and(step > 0, step < last))
    def _():
        weave(depth_product(1), depth_points(0))
        weave(lateral_product(0) + finish(0), depth_points(1))
        weave(lateral_product(1) + finish(1), lateral_points(0))
        weave(depth_product(0), lateral_points(1))

    @pl.when(step == last)
    def _():
        weave(depth_product(1), depth_points(0))
        weave(finish(0), depth_points(1))
        weave(finish(1), [])


def twice_gelu(half):
    return half + half * jnp.tanh(half * (TANH_A + TANH_B * (half * half)))


def diagonals(matrices):
    n = matrices.shape[1]
    ids = np.arange(n)
    picks = (ids[None, :, None] == (ids[None, None, :] - ids[:, None, None]) % n).astype(np.float32)
    rows = jnp.sum(matrices[None] * picks[:, None], axis=2)
    return jnp.repeat(rows, LANE // n, axis=2)


def fits(mesh_lat, rows, width_y, cells, chans, modes_x, modes_y):
    return (
        cells == 2 * SPAN
        and SPAN % (LANE // chans * chans) == 0
        and mesh_lat * GROUP * SPAN == modes_y * cells
        and rows % 4 == 0
        and rows >= 16
        and width_y % 256 == 0
        and 4 * modes_y == SPAN
        and modes_x % 8 == 0
    )


def shards(field, lat_modes, lat_gains, lat_local, depth_modes, depth_local):
    devices = lax.axis_size("lat")
    rows, width_y, cells = field.shape
    modes_x, chans, _ = lat_modes.shape
    modes_y = lat_gains.shape[0]
    modes_z = depth_modes.shape[0]
    if not fits(devices, rows, width_y, cells, chans, modes_x, modes_y):
        return plain_shards(field, lat_modes, lat_gains, lat_local, depth_modes, depth_local)
    depth = cells // chans
    width_x = rows * devices
    basis_x = basis64(width_x, modes_x)
    basis_y = basis64(width_y, modes_y)
    basis_z = basis64(depth, modes_z)
    funcs, fine = window_modes(rows, width_x, modes_x)
    count = funcs.shape[0]
    packed = (count + fine) * GROUP
    halves = cells // SPAN
    me = lax.axis_index("lat")

    by_high, by_low = split64(basis_y)
    by_forward = np.concatenate([by_high, by_low], axis=0)
    pairs = 4
    steps = rows // (2 * pairs)
    sent = pl.pallas_call(
        functools.partial(forward_kernel, funcs, fine),
        grid=(steps + 1,),
        in_specs=[
            pl.BlockSpec((2 * modes_y, width_y), lambda s: (0, 0)),
            pl.BlockSpec((pairs, width_y, cells), lambda s: (jnp.minimum(s, steps - 1), 0, 0)),
            pl.BlockSpec((pairs, width_y, cells), lambda s: (2 * steps - 1 - jnp.minimum(s, steps - 1), 0, 0)),
        ],
        out_specs=pl.BlockSpec((devices, packed, SPAN), lambda s: (0, 0, 0)),
        out_shape=jax.ShapeDtypeStruct((devices, packed, SPAN), BF16),
        scratch_shapes=[
            pltpu.VMEM((2 * pairs, modes_y, cells), F32),
            pltpu.VMEM((count, modes_y, cells), F32),
        ],
        compiler_params=pltpu.CompilerParams(vmem_limit_bytes=48 * 2**20),
        name="forward",
    )(by_forward, field, field)
    gathered = lax.all_to_all(sent, "lat", split_axis=0, concat_axis=0, tiled=True)

    per = SPAN // chans
    flip = np.kron(np.eye(per)[::-1], np.eye(chans)).astype(ml_dtypes.bfloat16)
    near_z = basis_z[:, :per]
    ids = np.arange(SPAN)
    pick = (np.arange(chans)[:, None] == ids[None, :] % chans).astype(np.float32)
    mask = (ids[:, None] // chans == ids[None, :] // chans).astype(np.float32)
    halved = [near_z[parity::2] for parity in range(2)]
    outer = np.stack([0.5 * np.kron(b.T, np.eye(chans)) for b in halved]).astype(np.float32)
    inner = np.stack([np.kron(b, np.ones((chans, chans))) for b in halved]).astype(np.float32)
    anywhere = pl.BlockSpec(memory_space=pl.ANY)
    local, turned, depth_weights = pl.pallas_call(
        prepare_kernel,
        in_specs=9 * [pl.BlockSpec(memory_space=pltpu.VMEM)] + [anywhere],
        out_shape=[
            jax.ShapeDtypeStruct((2 * SPAN, SPAN), BF16),
            jax.ShapeDtypeStruct((2 * SPAN, SPAN), BF16),
            jax.ShapeDtypeStruct((2, 3 * SPAN, SPAN), BF16),
        ],
        compiler_params=pltpu.CompilerParams(vmem_limit_bytes=24 * 2**20),
        name="prepare",
    )(lat_local, depth_modes, depth_local, pick, pick.T.copy(), mask, outer, inner, flip, sent)
    four = 4
    local_near = pl.pallas_call(
        local_near_kernel,
        grid=(rows // four,),
        in_specs=[
            pl.BlockSpec((four, width_y, SPAN), lambda s: (s, 0, 0)),
            pl.BlockSpec((2 * SPAN, SPAN), lambda s: (0, 0)),
        ],
        out_specs=pl.BlockSpec((four, width_y, SPAN), lambda s: (s, 0, 0)),
        out_shape=jax.ShapeDtypeStruct((rows, width_y, SPAN), F32),
        compiler_params=pltpu.CompilerParams(vmem_limit_bytes=48 * 2**20),
        name="local_near",
    )(field, local)

    weights = np.einsum("pit,jt->pij", basis_x.reshape(modes_x, devices, rows), funcs)
    flat = weights.reshape(modes_x, devices * count)
    ah, al = split64(np.pad(flat, ((0, 0), (0, -flat.shape[1] % LANE))))
    a_forward = np.concatenate([ah, al], axis=0)
    bh, bl = split64(flat.T)
    a_back = np.concatenate([bh, bl, bh, bl], axis=1)
    gains = lax.dynamic_slice_in_dim(lat_gains, (me // halves) * GROUP, GROUP, axis=0)
    gains = jnp.tile(jnp.repeat(gains, LANE // chans, axis=1), (1, SPAN // LANE))
    per_lane = LANE // chans
    ids = np.arange(LANE)
    order = np.zeros((LANE, LANE))
    order[ids, ids % chans * per_lane + ids // chans] = 1
    order = np.kron(np.eye(SPAN // LANE), order).astype(ml_dtypes.bfloat16)
    place = jnp.where(me % halves == 1, order.T @ flip, order.T)
    mixed = pl.pallas_call(
        functools.partial(mix_kernel, count, fine),
        in_specs=7 * [pl.BlockSpec(memory_space=pltpu.VMEM)] + [pl.BlockSpec(memory_space=pl.ANY)],
        out_shape=jax.ShapeDtypeStruct((devices, packed, SPAN), BF16),
        scratch_shapes=[
            pltpu.VMEM((SPAN // LANE, a_forward.shape[1] * GROUP, LANE), F32),
            pltpu.VMEM((SPAN // LANE, devices * count * GROUP, LANE), F32),
        ],
        compiler_params=pltpu.CompilerParams(vmem_limit_bytes=48 * 2**20),
        name="mix",
    )(gathered, a_forward, a_back, gains, diagonals(lat_modes), order, place, local_near)
    returned = lax.all_to_all(mixed, "lat", split_axis=0, concat_axis=0, tiled=True)

    local_far, mirrored = pl.pallas_call(
        local_far_kernel,
        grid=(rows // four,),
        in_specs=[
            pl.BlockSpec((four, width_y, SPAN), lambda s: (s, 0, 1)),
            pl.BlockSpec((2 * SPAN, SPAN), lambda s: (0, 0)),
            pl.BlockSpec((SPAN, SPAN), lambda s: (0, 0)),
            pl.BlockSpec(memory_space=pl.ANY),
        ],
        out_specs=2 * [pl.BlockSpec((four, width_y, SPAN), lambda s: (s, 0, 0))],
        out_shape=[
            jax.ShapeDtypeStruct((rows, width_y, SPAN), F32),
            jax.ShapeDtypeStruct((rows, width_y, SPAN), BF16),
        ],
        compiler_params=pltpu.CompilerParams(vmem_limit_bytes=48 * 2**20),
        name="local_far",
    )(field, turned, flip, mixed)

    by_back = np.concatenate([by_high, by_low, by_high, by_low], axis=0).T.copy()
    slots = np.concatenate([funcs, funcs[:fine]], axis=0)
    spread = np.concatenate(split64(np.kron(0.5 * slots.T, np.eye(GROUP))), axis=0)
    block = 4
    unit = block * width_y // 2
    wide = (unit, cells)
    narrow = (unit, SPAN)
    steps = rows // block
    return pl.pallas_call(
        functools.partial(tail_kernel, 16),
        grid=(steps + 1,),
        in_specs=[
            pl.BlockSpec((devices, packed, SPAN), lambda s: (0, 0, 0)),
            *(4 * [anywhere]),
            pl.BlockSpec((width_y, SPAN), lambda s: (0, 0)),
            pl.BlockSpec((2, 3 * SPAN, SPAN), lambda s: (0, 0, 0)),
            pl.BlockSpec((SPAN, SPAN), lambda s: (0, 0)),
            pl.BlockSpec(spread.shape, lambda s: (0, 0)),
        ],
        out_specs=pl.BlockSpec((block, width_y, cells), lambda s: (jnp.maximum(s - 1, 0), 0, 0)),
        out_shape=jax.ShapeDtypeStruct(field.shape, BF16),
        scratch_shapes=[pltpu.VMEM((rows, 2 * modes_y, cells), BF16)]
        + 2 * [pltpu.VMEM(wide, F32)]
        + 2 * [pltpu.VMEM(wide, F32)]
        + 2 * [pltpu.VMEM((unit, 4 * SPAN), BF16)]
        + 2 * [pltpu.VMEM(wide, F32)]
        + 2 * [pltpu.VMEM(narrow, BF16)]
        + 2 * [pltpu.VMEM((2, block, width_y, SPAN), F32)]
        + 2 * [pltpu.VMEM((2, block, width_y, SPAN), BF16)]
        + [pltpu.SemaphoreType.DMA((2, 4))],
        compiler_params=pltpu.CompilerParams(vmem_limit_bytes=58 * 2**20),
        name="tail",
    )(
        returned,
        local_near,
        local_far,
        field,
        mirrored,
        by_back,
        depth_weights,
        flip,
        spread,
    )


def solution(mesh):
    placed = (P(("group", "lat"), None, None), P(), P(), P(), P(), P())
    return jax.shard_map(
        shards,
        mesh=mesh,
        in_specs=placed,
        out_specs=P(("group", "lat"), None, None),
        check_vma=False,
    )
```

```python
import functools
import math

import jax
import jax.numpy as jnp
import ml_dtypes
import numpy as np
from jax import lax
from jax.experimental import pallas as pl
from jax.experimental.pallas import tpu as pltpu
from jax.sharding import PartitionSpec as P


def cosine_basis(length, modes):
    order = jnp.arange(modes, dtype=jnp.float32)[:, None]
    place = jnp.arange(length, dtype=jnp.float32)[None, :]
    scales = jnp.where(order == 0.0, math.sqrt(1.0 / length), math.sqrt(2.0 / length))
    return jnp.cos(math.pi * order * (place + 0.5) / length) * scales


def row_tail(u_rows, spect, lat_local, depth_modes, depth_local, depth_basis):
    highest = lax.Precision.HIGHEST
    rows, width, cells = u_rows.shape
    chans = lat_local.shape[0]
    depth = cells // chans
    u4 = u_rows.reshape(rows, width, depth, chans)
    s4 = spect.reshape(rows, width, depth, chans)
    first = u4 + jax.nn.gelu(s4 + jnp.einsum("xyzc,cd->xyzd", u4, lat_local, precision=highest))
    dcoef = jnp.einsum("kz,xyzc->xykc", depth_basis, first, precision=highest)
    dmix = jnp.einsum("xykc,kcd->xykd", dcoef, depth_modes, precision=highest)
    dspect = jnp.einsum("kz,xykd->xyzd", depth_basis, dmix, precision=highest)
    final = first + jax.nn.gelu(
        dspect + jnp.einsum("xyzc,cd->xyzd", first, depth_local, precision=highest)
    )
    return final.reshape(rows, width, cells).astype(jnp.bfloat16)


def one_hot(ids, count):
    return (ids[:, None] == jnp.arange(count, dtype=jnp.int32)[None, :]).astype(jnp.float32)


def plain_shards(field, lat_modes, lat_gains, lat_local, depth_modes, depth_local):
    highest = lax.Precision.HIGHEST
    devices = lax.axis_size("lat")
    rows_dev, width_y, cells = field.shape
    modes_x, chans, _ = lat_modes.shape
    modes_y = lat_gains.shape[0]
    modes_z = depth_modes.shape[0]
    depth = cells // chans
    width_x = rows_dev * devices
    basis_x = cosine_basis(width_x, modes_x)
    basis_y = cosine_basis(width_y, modes_y)
    basis_z = cosine_basis(depth, modes_z)
    start = lax.axis_index("lat")
    u_rows = field.astype(jnp.float32)
    coef_y = jnp.einsum("qy,xyw->xqw", basis_y, u_rows, precision=highest)
    packed = coef_y.reshape(rows_dev, modes_y * cells)
    gathered = lax.all_to_all(packed, "lat", split_axis=1, concat_axis=0, tiled=True)
    span = gathered.shape[1]
    pairs = span // chans
    coef = jnp.dot(basis_x, gathered, precision=highest).reshape(modes_x, pairs, chans)
    mode_ids = (start * pairs + jnp.arange(pairs, dtype=jnp.int32)) // depth
    gain_rows = jnp.dot(one_hot(mode_ids, modes_y), lat_gains, precision=highest)
    mixed = jnp.einsum("jpc,jcd->jpd", coef * gain_rows[None, :, :], lat_modes, precision=highest)
    back_x = jnp.dot(basis_x.T, mixed.reshape(modes_x, span), precision=highest)
    returned = lax.all_to_all(back_x, "lat", split_axis=0, concat_axis=1, tiled=True)
    spect = jnp.einsum(
        "qy,xqw->xyw", basis_y, returned.reshape(rows_dev, modes_y, cells), precision=highest
    )
    return row_tail(u_rows, spect, lat_local, depth_modes, depth_local, basis_z)


BF16 = jnp.bfloat16
F32 = jnp.float32
LANE = 128
GROUP = 8
SPAN = 256
TANH_A = 2.0 * math.sqrt(2.0 / math.pi)
TANH_B = 8.0 * 0.044715 * math.sqrt(2.0 / math.pi)


def basis64(length, modes):
    order = np.arange(modes)[:, None]
    place = np.arange(length)[None, :]
    scales = np.where(order == 0, math.sqrt(1.0 / length), math.sqrt(2.0 / length))
    return np.cos(math.pi * order * (place + 0.5) / length) * scales


def split64(array):
    high = array.astype(ml_dtypes.bfloat16)
    return high, (array - high.astype(np.float64)).astype(ml_dtypes.bfloat16)


def split(array):
    high = array.astype(BF16)
    return high, (array - high.astype(F32)).astype(BF16)


def window_modes(rows, length, modes):
    place = np.arange(rows) - (rows - 1) / 2
    order = np.arange(modes)[:, None]
    _, se, ve = np.linalg.svd(np.cos(math.pi * order * place / length))
    _, so, vo = np.linalg.svd(np.sin(math.pi * order * place / length))
    top = max(se[0], so[0])
    both = sorted([(-w, 2 * n) for n, w in enumerate(se[: rows // 2])] + [(-w, 2 * n + 1) for n, w in enumerate(so[: rows // 2])])
    weights = np.array([-w for w, _ in both])
    count = int(np.sum(weights > top * 2.0**-23))
    fine = int(np.sum(weights > top * 0.25))
    fine += (count + fine) % 2
    funcs = np.stack([ve[: rows // 2], vo[: rows // 2]], axis=1).reshape(rows // 2 * 2, rows)
    assert [n for _, n in both[:count]] == list(range(count))
    return funcs[:count], fine


def forward_kernel(funcs, fine, by_ref, near_ref, far_ref, o_ref, cy_ref, acc_ref):
    step = pl.program_id(0)
    pairs = near_ref.shape[0]
    steps = funcs.shape[1] // (2 * pairs)
    modes_y = by_ref.shape[0] // 2
    count = funcs.shape[0]
    halves = cy_ref.shape[2] // SPAN

    def compress(before):
        for g in range(modes_y // GROUP):
            rows = slice(g * GROUP, (g + 1) * GROUP)
            for c in range(halves * SPAN // LANE):
                lanes = slice(c * LANE, (c + 1) * LANE)
                totals = [None if before == 0 else acc_ref[j, rows, lanes] for j in range(count)]
                for r in range(pairs):
                    x, y = cy_ref[r, rows, lanes], cy_ref[pairs + r, rows, lanes]
                    pair = (x + y, x - y)
                    for j in range(count):
                        term = pair[j % 2] * float(funcs[j, before * pairs + r])
                        totals[j] = term if totals[j] is None else totals[j] + term
                if before < steps - 1:
                    for j in range(count):
                        acc_ref[j, rows, lanes] = totals[j]
                    continue
                h, k = divmod(c, SPAN // LANE)
                place = slice(k * LANE, (k + 1) * LANE)
                slots = [total.astype(BF16).astype(F32) for total in totals]
                slots += [totals[j] - slots[j] for j in range(fine)]
                for j in range(0, count + fine, 2):
                    two = jnp.concatenate(slots[j : j + 2], axis=0).astype(BF16)
                    o_ref[g * halves + h, j * GROUP : (j + 2) * GROUP, place] = two

    def body(at):
        if at > 0:
            compress(at - 1)
        if at < steps:
            for r in range(pairs):
                for slot, row in ((r, near_ref[r]), (pairs + r, far_ref[pairs - 1 - r])):
                    z = jnp.dot(by_ref[...], row, preferred_element_type=F32)
                    cy_ref[slot] = z[:modes_y] + z[modes_y:]

    for at in range(steps + 1):
        pl.when(step == at)(functools.partial(body, at))


def mix_kernel(count, fine, r_ref, a_ref, b_ref, g_ref, w_ref, order_ref, place_ref, after_ref, o_ref, m_ref, back_ref, send_ref):
    devices, packed, span = r_ref.shape
    modes_x = w_ref.shape[1]
    depth = a_ref.shape[1]
    highs, lows = count * GROUP, fine * GROUP
    tiles = [(k, slice(k * LANE, (k + 1) * LANE)) for k in range(span // LANE)]
    ordered = r_ref[...].reshape(devices * packed, span)
    ordered = jnp.dot(ordered, order_ref[...], preferred_element_type=F32)
    for i in range(devices):
        got = ordered[i * packed : (i + 1) * packed]
        for k, lanes in tiles:
            m_ref[k, i * highs : i * highs + lows] = got[:lows, lanes] + got[highs:, lanes]
            m_ref[k, i * highs + lows : (i + 1) * highs] = got[lows:highs, lanes]
    if depth > devices * count:
        for k, _ in tiles:
            m_ref[k, devices * highs :] = jnp.zeros((depth * GROUP - devices * highs, LANE), F32)
    shifts = w_ref.shape[0]
    for q in range(GROUP):
        modes = [m_ref[k, pl.ds(q, depth, stride=GROUP), :] for k, _ in tiles]
        high, low = split(jnp.concatenate(modes, axis=1))
        z = jnp.dot(a_ref[...], jnp.concatenate([high, low], axis=1), preferred_element_type=F32)
        coef = z[:modes_x, :span] + z[modes_x:, :span] + z[:modes_x, span:]
        coef = coef * g_ref[q : q + 1, :]
        mixed = []
        for k, lanes in tiles:
            part = coef[:, lanes]
            total = part * w_ref[0]
            for n in range(1, shifts):
                total = total + pltpu.roll(part, n * (LANE // shifts), 1) * w_ref[n]
            mixed.append(total)
        high, low = split(jnp.concatenate(mixed, axis=1))
        right = jnp.concatenate([high, high, low, low], axis=0)
        z = jnp.dot(b_ref[...], right, preferred_element_type=F32)
        for k, lanes in tiles:
            back_ref[k, pl.ds(q, devices * count, stride=GROUP), :] = z[:, lanes]
    for i in range(devices):
        z = jnp.concatenate([back_ref[k, i * highs : (i + 1) * highs] for k, _ in tiles], axis=1)
        high = z.astype(BF16).astype(F32)
        send_ref[i * packed : (i + 1) * packed] = jnp.concatenate([high, z[:lows] - high[:lows]], axis=0).astype(BF16)
    z = jnp.dot(send_ref[...], place_ref[...], preferred_element_type=F32)
    o_ref[...] = z.astype(BF16).reshape(devices, packed, span)


def expand(r_ref, v_ref, b_ref):
    rows = b_ref.shape[0]
    modes_y = b_ref.shape[1] // 2
    halves = b_ref.shape[2] // SPAN
    for g in range(modes_y // (2 * GROUP)):
        at = g * 2 * GROUP
        for h in range(halves):
            got = []
            for k in range(2):
                block = r_ref[(2 * g + k) * halves + h]
                z = jnp.dot(v_ref[...], block, preferred_element_type=F32)
                got.append(z[: rows * GROUP] + z[rows * GROUP :])
            lanes = slice(h * SPAN, (h + 1) * SPAN)
            for t in range(rows):
                part = slice(t * GROUP, (t + 1) * GROUP)
                high, low = split(jnp.concatenate([got[0][part], got[1][part]], axis=0))
                b_ref[t, at : at + 2 * GROUP, lanes] = high
                b_ref[t, modes_y + at : modes_y + at + 2 * GROUP, lanes] = low


def local_near_kernel(u_ref, l_ref, x_ref):
    rows, width, _ = u_ref.shape
    u = u_ref[...].reshape(rows * width, SPAN)
    x = jnp.dot(jnp.concatenate([u, u], axis=1), l_ref[...], preferred_element_type=F32)
    x_ref[...] = x.reshape(rows, width, SPAN)


def local_far_kernel(u_ref, l_ref, flip_ref, after_ref, x_ref, f_ref):
    local_near_kernel(u_ref, l_ref, x_ref)
    rows, width, _ = u_ref.shape
    u = u_ref[...].reshape(rows * width, SPAN)
    f = jnp.dot(u, flip_ref[...], preferred_element_type=F32)
    f_ref[...] = f.astype(BF16).reshape(rows, width, SPAN)


def weave(one, other):
    done = 0
    for n, step in enumerate(one):
        step()
        until = len(other) * (n + 1) // len(one)
        for at in range(done, until):
            other[at]()
        done = until


def prepare_kernel(l_ref, m_ref, d_ref, e_ref, et_ref, mask_ref, a_ref, b_ref, flip_ref, after_ref, near_ref, far_ref, w_ref):
    highest = lax.Precision.HIGHEST

    def dot(x, y):
        return jnp.dot(x, y, preferred_element_type=F32, precision=highest)

    def spread(ref):
        return dot(dot(et_ref[...], ref[...]), e_ref[...]) * mask_ref[...]

    for n, half in enumerate(split(0.5 * spread(l_ref))):
        near_ref[n * SPAN : (n + 1) * SPAN] = half
        far_ref[n * SPAN : (n + 1) * SPAN] = jnp.dot(half, flip_ref[...], preferred_element_type=F32).astype(BF16)
    local = 0.25 * spread(d_ref)
    for parity in range(2):
        modes = jnp.concatenate([m_ref[k] for k in range(parity, m_ref.shape[0], 2)], axis=0)
        full = dot(a_ref[parity], dot(modes, e_ref[...]) * b_ref[parity]) + local
        high, low = split(full)
        for n, half in enumerate((high, high, low)):
            w_ref[parity, n * SPAN : (n + 1) * SPAN] = half


def tail_kernel(chunk, r_ref, x0_all, x1_all, u_all, f_all, by_ref, w_ref, flip_ref, v_ref, o_ref, b_ref, *scratch):
    step = pl.program_id(0)
    last = pl.num_programs(0) - 1
    pre, first, parts, post, done = (scratch[n : n + 2] for n in range(0, 10, 2))
    held, arrived = scratch[10:14], scratch[14]
    block, width = held[0].shape[1:3]
    modes_y = b_ref.shape[1] // 2
    x0_ref, x1_ref, u_ref, f_ref = (ref.at[lax.rem(step, 2)] for ref in held)

    def copies(at):
        slot = lax.rem(at, 2)
        return [
            pltpu.make_async_copy(
                source.at[pl.ds(at * block, block), :, pl.ds(0, SPAN)], ref.at[slot], arrived.at[slot, n]
            )
            for n, (source, ref) in enumerate(zip((x0_all, x1_all, u_all, f_all), held))
        ]

    near, far = slice(0, SPAN), slice(SPAN, 2 * SPAN)
    unit = pre[0].shape[0]
    pieces = range(0, unit, chunk)

    def where(n, y):
        return divmod(n * unit + y, width)

    def lateral_product(n):
        tall = min(unit, width)

        def piece(at, lanes):
            r, y = where(n, at)
            high, low = b_ref[block * step + r, :modes_y, lanes], b_ref[block * step + r, modes_y:, lanes]
            right = jnp.concatenate([high, high, low, low], axis=0)
            z = jnp.dot(by_ref[y : y + tall], right, preferred_element_type=F32)
            pre[n][at : at + tall, lanes] = z

        return [functools.partial(piece, at, lanes) for at in range(0, unit, tall) for lanes in (near, far)]

    def lateral_points(n):
        def piece(y):
            r, y0 = where(n, y)
            at, ys = slice(y, y + chunk), slice(y0, y0 + chunk)
            f0 = u_ref[r, ys].astype(F32) + twice_gelu(pre[n][at, near] + x0_ref[r, ys])
            f1 = f_ref[r, ys].astype(F32) + twice_gelu(pre[n][at, far] + x1_ref[r, ys])
            first[n][at, near] = f0
            first[n][at, far] = f1
            for m, value in enumerate((f0 + f1, f0 - f1)):
                high, low = split(value)
                parts[n][at, 2 * m * SPAN : (2 * m + 1) * SPAN] = high
                parts[n][at, (2 * m + 1) * SPAN : (2 * m + 2) * SPAN] = low

        return [functools.partial(piece, y) for y in pieces]

    def depth_product(n):
        def piece(m, lanes):
            high = parts[n][:, 2 * m * SPAN : (2 * m + 1) * SPAN]
            low = parts[n][:, (2 * m + 1) * SPAN : (2 * m + 2) * SPAN]
            left = jnp.concatenate([high, low, high], axis=1)
            post[n][:, lanes] = jnp.dot(left, w_ref[m], preferred_element_type=F32)

        return [functools.partial(piece, m, lanes) for m, lanes in enumerate((near, far))]

    def depth_points(n):
        def piece(y):
            r, y0 = where(n, y)
            at, ys = slice(y, y + chunk), slice(y0, y0 + chunk)
            even, odd = post[n][at, near], post[n][at, far]
            o_ref[r, ys, near] = (first[n][at, near] + twice_gelu(even + odd)).astype(BF16)
            done[n][at] = (first[n][at, far] + twice_gelu(even - odd)).astype(BF16)

        return [functools.partial(piece, y) for y in pieces]

    def finish(n):
        def piece():
            z = jnp.dot(done[n][...], flip_ref[...], preferred_element_type=F32).astype(BF16)
            for at in range(0, unit, min(unit, width)):
                r, y0 = where(n, at)
                o_ref[r, y0 : y0 + min(unit, width), far] = z[at : at + min(unit, width)]

        return [piece]

    @pl.when(step == 0)
    def _():
        for copy in copies(step):
            copy.start()

    @pl.when(step < last - 1)
    def _():
        for copy in copies(step + 1):
            copy.start()

    @pl.when(step == 0)
    def _():
        expand(r_ref, v_ref, b_ref)

    @pl.when(step < last)
    def _():
        for copy in copies(step):
            copy.wait()

    @pl.when(step == 0)
    def _():
        weave(lateral_product(0), [])
        weave(lateral_product(1), lateral_points(0))
        weave(depth_product(0), lateral_points(1))

    @pl.when(jnp.logical_and(step > 0, step < last))
    def _():
        weave(depth_product(1), depth_points(0))
        weave(lateral_product(0) + finish(0), depth_points(1))
        weave(lateral_product(1) + finish(1), lateral_points(0))
        weave(depth_product(0), lateral_points(1))

    @pl.when(step == last)
    def _():
        weave(depth_product(1), depth_points(0))
        weave(finish(0), depth_points(1))
        weave(finish(1), [])


def twice_gelu(half):
    return half + half * jnp.tanh(half * (TANH_A + TANH_B * (half * half)))


def diagonals(matrices):
    n = matrices.shape[1]
    ids = np.arange(n)
    picks = (ids[None, :, None] == (ids[None, None, :] - ids[:, None, None]) % n).astype(np.float32)
    rows = jnp.sum(matrices[None] * picks[:, None], axis=2)
    return jnp.repeat(rows, LANE // n, axis=2)


def fits(mesh_lat, rows, width_y, cells, chans, modes_x, modes_y):
    return (
        cells == 2 * SPAN
        and SPAN % (LANE // chans * chans) == 0
        and mesh_lat * GROUP * SPAN == modes_y * cells
        and rows % 4 == 0
        and rows >= 16
        and width_y % 256 == 0
        and 4 * modes_y == SPAN
        and modes_x % 8 == 0
    )


def shards(field, lat_modes, lat_gains, lat_local, depth_modes, depth_local):
    devices = lax.axis_size("lat")
    rows, width_y, cells = field.shape
    modes_x, chans, _ = lat_modes.shape
    modes_y = lat_gains.shape[0]
    modes_z = depth_modes.shape[0]
    if not fits(devices, rows, width_y, cells, chans, modes_x, modes_y):
        return plain_shards(field, lat_modes, lat_gains, lat_local, depth_modes, depth_local)
    depth = cells // chans
    width_x = rows * devices
    basis_x = basis64(width_x, modes_x)
    basis_y = basis64(width_y, modes_y)
    basis_z = basis64(depth, modes_z)
    funcs, fine = window_modes(rows, width_x, modes_x)
    count = funcs.shape[0]
    packed = (count + fine) * GROUP
    halves = cells // SPAN
    me = lax.axis_index("lat")

    by_high, by_low = split64(basis_y)
    by_forward = np.concatenate([by_high, by_low], axis=0)
    pairs = 4
    steps = rows // (2 * pairs)
    sent = pl.pallas_call(
        functools.partial(forward_kernel, funcs, fine),
        grid=(steps + 1,),
        in_specs=[
            pl.BlockSpec((2 * modes_y, width_y), lambda s: (0, 0)),
            pl.BlockSpec((pairs, width_y, cells), lambda s: (jnp.minimum(s, steps - 1), 0, 0)),
            pl.BlockSpec((pairs, width_y, cells), lambda s: (2 * steps - 1 - jnp.minimum(s, steps - 1), 0, 0)),
        ],
        out_specs=pl.BlockSpec((devices, packed, SPAN), lambda s: (0, 0, 0)),
        out_shape=jax.ShapeDtypeStruct((devices, packed, SPAN), BF16),
        scratch_shapes=[
            pltpu.VMEM((2 * pairs, modes_y, cells), F32),
            pltpu.VMEM((count, modes_y, cells), F32),
        ],
        compiler_params=pltpu.CompilerParams(vmem_limit_bytes=48 * 2**20),
        name="forward",
    )(by_forward, field, field)
    gathered = lax.all_to_all(sent, "lat", split_axis=0, concat_axis=0, tiled=True)

    per = SPAN // chans
    flip = np.kron(np.eye(per)[::-1], np.eye(chans)).astype(ml_dtypes.bfloat16)
    near_z = basis_z[:, :per]
    ids = np.arange(SPAN)
    pick = (np.arange(chans)[:, None] == ids[None, :] % chans).astype(np.float32)
    mask = (ids[:, None] // chans == ids[None, :] // chans).astype(np.float32)
    halved = [near_z[parity::2] for parity in range(2)]
    outer = np.stack([0.5 * np.kron(b.T, np.eye(chans)) for b in halved]).astype(np.float32)
    inner = np.stack([np.kron(b, np.ones((chans, chans))) for b in halved]).astype(np.float32)
    anywhere = pl.BlockSpec(memory_space=pl.ANY)
    local, turned, depth_weights = pl.pallas_call(
        prepare_kernel,
        in_specs=9 * [pl.BlockSpec(memory_space=pltpu.VMEM)] + [anywhere],
        out_shape=[
            jax.ShapeDtypeStruct((2 * SPAN, SPAN), BF16),
            jax.ShapeDtypeStruct((2 * SPAN, SPAN), BF16),
            jax.ShapeDtypeStruct((2, 3 * SPAN, SPAN), BF16),
        ],
        compiler_params=pltpu.CompilerParams(vmem_limit_bytes=24 * 2**20),
        name="prepare",
    )(lat_local, depth_modes, depth_local, pick, pick.T.copy(), mask, outer, inner, flip, sent)
    four = 4
    local_near = pl.pallas_call(
        local_near_kernel,
        grid=(rows // four,),
        in_specs=[
            pl.BlockSpec((four, width_y, SPAN), lambda s: (s, 0, 0)),
            pl.BlockSpec((2 * SPAN, SPAN), lambda s: (0, 0)),
        ],
        out_specs=pl.BlockSpec((four, width_y, SPAN), lambda s: (s, 0, 0)),
        out_shape=jax.ShapeDtypeStruct((rows, width_y, SPAN), F32),
        compiler_params=pltpu.CompilerParams(vmem_limit_bytes=48 * 2**20),
        name="local_near",
    )(field, local)

    weights = np.einsum("pit,jt->pij", basis_x.reshape(modes_x, devices, rows), funcs)
    flat = weights.reshape(modes_x, devices * count)
    ah, al = split64(np.pad(flat, ((0, 0), (0, -flat.shape[1] % LANE))))
    a_forward = np.concatenate([ah, al], axis=0)
    bh, bl = split64(flat.T)
    a_back = np.concatenate([bh, bl, bh, bl], axis=1)
    gains = lax.dynamic_slice_in_dim(lat_gains, (me // halves) * GROUP, GROUP, axis=0)
    gains = jnp.tile(jnp.repeat(gains, LANE // chans, axis=1), (1, SPAN // LANE))
    per_lane = LANE // chans
    ids = np.arange(LANE)
    order = np.zeros((LANE, LANE))
    order[ids, ids % chans * per_lane + ids // chans] = 1
    order = np.kron(np.eye(SPAN // LANE), order).astype(ml_dtypes.bfloat16)
    place = jnp.where(me % halves == 1, order.T @ flip, order.T)
    mixed = pl.pallas_call(
        functools.partial(mix_kernel, count, fine),
        in_specs=7 * [pl.BlockSpec(memory_space=pltpu.VMEM)] + [pl.BlockSpec(memory_space=pl.ANY)],
        out_shape=jax.ShapeDtypeStruct((devices, packed, SPAN), BF16),
        scratch_shapes=[
            pltpu.VMEM((SPAN // LANE, a_forward.shape[1] * GROUP, LANE), F32),
            pltpu.VMEM((SPAN // LANE, devices * count * GROUP, LANE), F32),
            pltpu.VMEM((devices * packed, SPAN), BF16),
        ],
        compiler_params=pltpu.CompilerParams(vmem_limit_bytes=48 * 2**20),
        name="mix",
    )(gathered, a_forward, a_back, gains, diagonals(lat_modes), order, place, local_near)
    returned = lax.all_to_all(mixed, "lat", split_axis=0, concat_axis=0, tiled=True)

    local_far, mirrored = pl.pallas_call(
        local_far_kernel,
        grid=(rows // four,),
        in_specs=[
            pl.BlockSpec((four, width_y, SPAN), lambda s: (s, 0, 1)),
            pl.BlockSpec((2 * SPAN, SPAN), lambda s: (0, 0)),
            pl.BlockSpec((SPAN, SPAN), lambda s: (0, 0)),
            pl.BlockSpec(memory_space=pl.ANY),
        ],
        out_specs=2 * [pl.BlockSpec((four, width_y, SPAN), lambda s: (s, 0, 0))],
        out_shape=[
            jax.ShapeDtypeStruct((rows, width_y, SPAN), F32),
            jax.ShapeDtypeStruct((rows, width_y, SPAN), BF16),
        ],
        compiler_params=pltpu.CompilerParams(vmem_limit_bytes=48 * 2**20),
        name="local_far",
    )(field, turned, flip, mixed)

    by_back = np.concatenate([by_high, by_low, by_high, by_low], axis=0).T.copy()
    slots = np.concatenate([funcs, funcs[:fine]], axis=0)
    spread = np.concatenate(split64(np.kron(0.5 * slots.T, np.eye(GROUP))), axis=0)
    block = 4
    unit = block * width_y // 2
    wide = (unit, cells)
    narrow = (unit, SPAN)
    steps = rows // block
    return pl.pallas_call(
        functools.partial(tail_kernel, 16),
        grid=(steps + 1,),
        in_specs=[
            pl.BlockSpec((devices, packed, SPAN), lambda s: (0, 0, 0)),
            *(4 * [anywhere]),
            pl.BlockSpec((width_y, SPAN), lambda s: (0, 0)),
            pl.BlockSpec((2, 3 * SPAN, SPAN), lambda s: (0, 0, 0)),
            pl.BlockSpec((SPAN, SPAN), lambda s: (0, 0)),
            pl.BlockSpec(spread.shape, lambda s: (0, 0)),
        ],
        out_specs=pl.BlockSpec((block, width_y, cells), lambda s: (jnp.maximum(s - 1, 0), 0, 0)),
        out_shape=jax.ShapeDtypeStruct(field.shape, BF16),
        scratch_shapes=[pltpu.VMEM((rows, 2 * modes_y, cells), BF16)]
        + 2 * [pltpu.VMEM(wide, F32)]
        + 2 * [pltpu.VMEM(wide, F32)]
        + 2 * [pltpu.VMEM((unit, 4 * SPAN), BF16)]
        + 2 * [pltpu.VMEM(wide, F32)]
        + 2 * [pltpu.VMEM(narrow, BF16)]
        + 2 * [pltpu.VMEM((2, block, width_y, SPAN), F32)]
        + 2 * [pltpu.VMEM((2, block, width_y, SPAN), BF16)]
        + [pltpu.SemaphoreType.DMA((2, 4))],
        compiler_params=pltpu.CompilerParams(vmem_limit_bytes=50 * 2**20),
        name="tail",
    )(
        returned,
        local_near,
        local_far,
        field,
        mirrored,
        by_back,
        depth_weights,
        flip,
        spread,
    )


def solution(mesh):
    placed = (P(("group", "lat"), None, None), P(), P(), P(), P(), P())
    return jax.shard_map(
        shards,
        mesh=mesh,
        in_specs=placed,
        out_specs=P(("group", "lat"), None, None),
        check_vma=False,
    )
```

```python
import functools
import math

import jax
import jax.numpy as jnp
import ml_dtypes
import numpy as np
from jax import lax
from jax.experimental import pallas as pl
from jax.experimental.pallas import tpu as pltpu
from jax.sharding import PartitionSpec as P


def cosine_basis(length, modes):
    order = jnp.arange(modes, dtype=jnp.float32)[:, None]
    place = jnp.arange(length, dtype=jnp.float32)[None, :]
    scales = jnp.where(order == 0.0, math.sqrt(1.0 / length), math.sqrt(2.0 / length))
    return jnp.cos(math.pi * order * (place + 0.5) / length) * scales


def row_tail(u_rows, spect, lat_local, depth_modes, depth_local, depth_basis):
    highest = lax.Precision.HIGHEST
    rows, width, cells = u_rows.shape
    chans = lat_local.shape[0]
    depth = cells // chans
    u4 = u_rows.reshape(rows, width, depth, chans)
    s4 = spect.reshape(rows, width, depth, chans)
    first = u4 + jax.nn.gelu(s4 + jnp.einsum("xyzc,cd->xyzd", u4, lat_local, precision=highest))
    dcoef = jnp.einsum("kz,xyzc->xykc", depth_basis, first, precision=highest)
    dmix = jnp.einsum("xykc,kcd->xykd", dcoef, depth_modes, precision=highest)
    dspect = jnp.einsum("kz,xykd->xyzd", depth_basis, dmix, precision=highest)
    final = first + jax.nn.gelu(
        dspect + jnp.einsum("xyzc,cd->xyzd", first, depth_local, precision=highest)
    )
    return final.reshape(rows, width, cells).astype(jnp.bfloat16)


def one_hot(ids, count):
    return (ids[:, None] == jnp.arange(count, dtype=jnp.int32)[None, :]).astype(jnp.float32)


def plain_shards(field, lat_modes, lat_gains, lat_local, depth_modes, depth_local):
    highest = lax.Precision.HIGHEST
    devices = lax.axis_size("lat")
    rows_dev, width_y, cells = field.shape
    modes_x, chans, _ = lat_modes.shape
    modes_y = lat_gains.shape[0]
    modes_z = depth_modes.shape[0]
    depth = cells // chans
    width_x = rows_dev * devices
    basis_x = cosine_basis(width_x, modes_x)
    basis_y = cosine_basis(width_y, modes_y)
    basis_z = cosine_basis(depth, modes_z)
    start = lax.axis_index("lat")
    u_rows = field.astype(jnp.float32)
    coef_y = jnp.einsum("qy,xyw->xqw", basis_y, u_rows, precision=highest)
    packed = coef_y.reshape(rows_dev, modes_y * cells)
    gathered = lax.all_to_all(packed, "lat", split_axis=1, concat_axis=0, tiled=True)
    span = gathered.shape[1]
    pairs = span // chans
    coef = jnp.dot(basis_x, gathered, precision=highest).reshape(modes_x, pairs, chans)
    mode_ids = (start * pairs + jnp.arange(pairs, dtype=jnp.int32)) // depth
    gain_rows = jnp.dot(one_hot(mode_ids, modes_y), lat_gains, precision=highest)
    mixed = jnp.einsum("jpc,jcd->jpd", coef * gain_rows[None, :, :], lat_modes, precision=highest)
    back_x = jnp.dot(basis_x.T, mixed.reshape(modes_x, span), precision=highest)
    returned = lax.all_to_all(back_x, "lat", split_axis=0, concat_axis=1, tiled=True)
    spect = jnp.einsum(
        "qy,xqw->xyw", basis_y, returned.reshape(rows_dev, modes_y, cells), precision=highest
    )
    return row_tail(u_rows, spect, lat_local, depth_modes, depth_local, basis_z)


BF16 = jnp.bfloat16
F32 = jnp.float32
LANE = 128
GROUP = 8
SPAN = 256
TANH_A = 2.0 * math.sqrt(2.0 / math.pi)
TANH_B = 8.0 * 0.044715 * math.sqrt(2.0 / math.pi)


def basis64(length, modes):
    order = np.arange(modes)[:, None]
    place = np.arange(length)[None, :]
    scales = np.where(order == 0, math.sqrt(1.0 / length), math.sqrt(2.0 / length))
    return np.cos(math.pi * order * (place + 0.5) / length) * scales


def split64(array):
    high = array.astype(ml_dtypes.bfloat16)
    return high, (array - high.astype(np.float64)).astype(ml_dtypes.bfloat16)


def split(array):
    high = array.astype(BF16)
    return high, (array - high.astype(F32)).astype(BF16)


def window_modes(rows, length, modes):
    place = np.arange(rows) - (rows - 1) / 2
    order = np.arange(modes)[:, None]
    _, se, ve = np.linalg.svd(np.cos(math.pi * order * place / length))
    _, so, vo = np.linalg.svd(np.sin(math.pi * order * place / length))
    top = max(se[0], so[0])
    both = sorted([(-w, 2 * n) for n, w in enumerate(se[: rows // 2])] + [(-w, 2 * n + 1) for n, w in enumerate(so[: rows // 2])])
    weights = np.array([-w for w, _ in both])
    count = int(np.sum(weights > top * 2.0**-23))
    fine = int(np.sum(weights > top * 0.25))
    fine += (count + fine) % 2
    funcs = np.stack([ve[: rows // 2], vo[: rows // 2]], axis=1).reshape(rows // 2 * 2, rows)
    assert [n for _, n in both[:count]] == list(range(count))
    return funcs[:count], fine


def forward_kernel(funcs, fine, by_ref, near_ref, far_ref, o_ref, cy_ref, acc_ref):
    step = pl.program_id(0)
    pairs = near_ref.shape[0]
    steps = funcs.shape[1] // (2 * pairs)
    modes_y = by_ref.shape[0] // 2
    count = funcs.shape[0]
    halves = cy_ref.shape[2] // SPAN

    def compress(before):
        for g in range(modes_y // GROUP):
            rows = slice(g * GROUP, (g + 1) * GROUP)
            for c in range(halves * SPAN // LANE):
                lanes = slice(c * LANE, (c + 1) * LANE)
                totals = [None if before == 0 else acc_ref[j, rows, lanes] for j in range(count)]
                for r in range(pairs):
                    x, y = cy_ref[r, rows, lanes], cy_ref[pairs + r, rows, lanes]
                    pair = (x + y, x - y)
                    for j in range(count):
                        term = pair[j % 2] * float(funcs[j, before * pairs + r])
                        totals[j] = term if totals[j] is None else totals[j] + term
                if before < steps - 1:
                    for j in range(count):
                        acc_ref[j, rows, lanes] = totals[j]
                    continue
                h, k = divmod(c, SPAN // LANE)
                place = slice(k * LANE, (k + 1) * LANE)
                slots = [total.astype(BF16).astype(F32) for total in totals]
                slots += [totals[j] - slots[j] for j in range(fine)]
                for j in range(0, count + fine, 2):
                    two = jnp.concatenate(slots[j : j + 2], axis=0).astype(BF16)
                    o_ref[g * halves + h, j * GROUP : (j + 2) * GROUP, place] = two

    def body(at):
        if at > 0:
            compress(at - 1)
        if at < steps:
            for r in range(pairs):
                for slot, row in ((r, near_ref[r]), (pairs + r, far_ref[pairs - 1 - r])):
                    z = jnp.dot(by_ref[...], row, preferred_element_type=F32)
                    cy_ref[slot] = z[:modes_y] + z[modes_y:]

    for at in range(steps + 1):
        pl.when(step == at)(functools.partial(body, at))


def mix_kernel(count, fine, r_ref, a_ref, b_ref, g_ref, w_ref, order_ref, place_ref, after_ref, o_ref, m_ref, back_ref, send_ref):
    devices, packed, span = r_ref.shape
    modes_x = w_ref.shape[1]
    depth = a_ref.shape[1]
    highs, lows = count * GROUP, fine * GROUP
    tiles = [(k, slice(k * LANE, (k + 1) * LANE)) for k in range(span // LANE)]
    ordered = r_ref[...].reshape(devices * packed, span)
    ordered = jnp.dot(ordered, order_ref[...], preferred_element_type=F32)
    for i in range(devices):
        got = ordered[i * packed : (i + 1) * packed]
        for k, lanes in tiles:
            m_ref[k, i * highs : i * highs + lows] = got[:lows, lanes] + got[highs:, lanes]
            m_ref[k, i * highs + lows : (i + 1) * highs] = got[lows:highs, lanes]
    if depth > devices * count:
        for k, _ in tiles:
            m_ref[k, devices * highs :] = jnp.zeros((depth * GROUP - devices * highs, LANE), F32)
    shifts = w_ref.shape[0]
    few = math.isqrt(shifts)
    for q in range(GROUP):
        modes = [m_ref[k, pl.ds(q, depth, stride=GROUP), :] for k, _ in tiles]
        high, low = split(jnp.concatenate(modes, axis=1))
        z = jnp.dot(a_ref[...], jnp.concatenate([high, low], axis=1), preferred_element_type=F32)
        coef = z[:modes_x, :span] + z[modes_x:, :span] + z[:modes_x, span:]
        coef = coef * g_ref[q : q + 1, :]
        mixed = []
        for k, lanes in tiles:
            part = coef[:, lanes]
            turned = [part] + [pltpu.roll(part, n * (LANE // shifts), 1) for n in range(1, few)]
            total = None
            for far in range(0, shifts, few):
                inner = turned[0] * w_ref[far]
                for n in range(1, few):
                    inner = inner + turned[n] * w_ref[far + n]
                total = pltpu.roll(inner, far * (LANE // shifts), 1) + total if far else inner
            mixed.append(total)
        high, low = split(jnp.concatenate(mixed, axis=1))
        right = jnp.concatenate([high, high, low, low], axis=0)
        z = jnp.dot(b_ref[...], right, preferred_element_type=F32)
        for k, lanes in tiles:
            back_ref[k, pl.ds(q, devices * count, stride=GROUP), :] = z[:, lanes]
    for i in range(devices):
        z = jnp.concatenate([back_ref[k, i * highs : (i + 1) * highs] for k, _ in tiles], axis=1)
        high = z.astype(BF16).astype(F32)
        send_ref[i * packed : (i + 1) * packed] = jnp.concatenate([high, z[:lows] - high[:lows]], axis=0).astype(BF16)
    z = jnp.dot(send_ref[...], place_ref[...], preferred_element_type=F32)
    o_ref[...] = z.astype(BF16).reshape(devices, packed, span)


def expand(r_ref, v_ref, b_ref):
    rows = b_ref.shape[0]
    modes_y = b_ref.shape[1] // 2
    halves = b_ref.shape[2] // SPAN
    for g in range(modes_y // (2 * GROUP)):
        at = g * 2 * GROUP
        for h in range(halves):
            got = []
            for k in range(2):
                block = r_ref[(2 * g + k) * halves + h]
                z = jnp.dot(v_ref[...], block, preferred_element_type=F32)
                got.append(z[: rows * GROUP] + z[rows * GROUP :])
            lanes = slice(h * SPAN, (h + 1) * SPAN)
            for t in range(rows):
                part = slice(t * GROUP, (t + 1) * GROUP)
                high, low = split(jnp.concatenate([got[0][part], got[1][part]], axis=0))
                b_ref[t, at : at + 2 * GROUP, lanes] = high
                b_ref[t, modes_y + at : modes_y + at + 2 * GROUP, lanes] = low


def local_near_kernel(u_ref, l_ref, x_ref):
    rows, width, _ = u_ref.shape
    u = u_ref[...].reshape(rows * width, SPAN)
    x = jnp.dot(jnp.concatenate([u, u], axis=1), l_ref[...], preferred_element_type=F32)
    x_ref[...] = x.reshape(rows, width, SPAN)


def local_far_kernel(u_ref, l_ref, flip_ref, after_ref, x_ref, f_ref):
    local_near_kernel(u_ref, l_ref, x_ref)
    rows, width, _ = u_ref.shape
    u = u_ref[...].reshape(rows * width, SPAN)
    f = jnp.dot(u, flip_ref[...], preferred_element_type=F32)
    f_ref[...] = f.astype(BF16).reshape(rows, width, SPAN)


def weave(one, other):
    done = 0
    for n, step in enumerate(one):
        step()
        until = len(other) * (n + 1) // len(one)
        for at in range(done, until):
            other[at]()
        done = until


def prepare_kernel(l_ref, m_ref, d_ref, e_ref, et_ref, mask_ref, a_ref, b_ref, flip_ref, after_ref, near_ref, far_ref, w_ref):
    highest = lax.Precision.HIGHEST

    def dot(x, y):
        return jnp.dot(x, y, preferred_element_type=F32, precision=highest)

    def spread(ref):
        return dot(dot(et_ref[...], ref[...]), e_ref[...]) * mask_ref[...]

    for n, half in enumerate(split(0.5 * spread(l_ref))):
        near_ref[n * SPAN : (n + 1) * SPAN] = half
        far_ref[n * SPAN : (n + 1) * SPAN] = jnp.dot(half, flip_ref[...], preferred_element_type=F32).astype(BF16)
    local = 0.25 * spread(d_ref)
    for parity in range(2):
        modes = jnp.concatenate([m_ref[k] for k in range(parity, m_ref.shape[0], 2)], axis=0)
        full = dot(a_ref[parity], dot(modes, e_ref[...]) * b_ref[parity]) + local
        high, low = split(full)
        for n, half in enumerate((high, high, low)):
            w_ref[parity, n * SPAN : (n + 1) * SPAN] = half


def tail_kernel(chunk, r_ref, x0_all, x1_all, u_all, f_all, by_ref, w_ref, flip_ref, v_ref, o_ref, b_ref, *scratch):
    step = pl.program_id(0)
    last = pl.num_programs(0) - 1
    pre, first, parts, post, done = (scratch[n : n + 2] for n in range(0, 10, 2))
    held, arrived = scratch[10:14], scratch[14]
    block, width = held[0].shape[1:3]
    modes_y = b_ref.shape[1] // 2
    x0_ref, x1_ref, u_ref, f_ref = (ref.at[lax.rem(step, 2)] for ref in held)

    def copies(at):
        slot = lax.rem(at, 2)
        return [
            pltpu.make_async_copy(
                source.at[pl.ds(at * block, block), :, pl.ds(0, SPAN)], ref.at[slot], arrived.at[slot, n]
            )
            for n, (source, ref) in enumerate(zip((x0_all, x1_all, u_all, f_all), held))
        ]

    near, far = slice(0, SPAN), slice(SPAN, 2 * SPAN)
    unit = pre[0].shape[0]
    pieces = range(0, unit, chunk)

    def where(n, y):
        return divmod(n * unit + y, width)

    def lateral_product(n):
        tall = min(unit, width)

        def piece(at, lanes):
            r, y = where(n, at)
            high, low = b_ref[block * step + r, :modes_y, lanes], b_ref[block * step + r, modes_y:, lanes]
            right = jnp.concatenate([high, high, low, low], axis=0)
            z = jnp.dot(by_ref[y : y + tall], right, preferred_element_type=F32)
            pre[n][at : at + tall, lanes] = z

        return [functools.partial(piece, at, lanes) for at in range(0, unit, tall) for lanes in (near, far)]

    def lateral_points(n):
        def piece(y):
            r, y0 = where(n, y)
            at, ys = slice(y, y + chunk), slice(y0, y0 + chunk)
            f0 = u_ref[r, ys].astype(F32) + twice_gelu(pre[n][at, near] + x0_ref[r, ys])
            f1 = f_ref[r, ys].astype(F32) + twice_gelu(pre[n][at, far] + x1_ref[r, ys])
            first[n][at, near] = f0
            first[n][at, far] = f1
            for m, value in enumerate((f0 + f1, f0 - f1)):
                high, low = split(value)
                parts[n][at, 2 * m * SPAN : (2 * m + 1) * SPAN] = high
                parts[n][at, (2 * m + 1) * SPAN : (2 * m + 2) * SPAN] = low

        return [functools.partial(piece, y) for y in pieces]

    def depth_product(n):
        def piece(m, lanes):
            high = parts[n][:, 2 * m * SPAN : (2 * m + 1) * SPAN]
            low = parts[n][:, (2 * m + 1) * SPAN : (2 * m + 2) * SPAN]
            left = jnp.concatenate([high, low, high], axis=1)
            post[n][:, lanes] = jnp.dot(left, w_ref[m], preferred_element_type=F32)

        return [functools.partial(piece, m, lanes) for m, lanes in enumerate((near, far))]

    def depth_points(n):
        def piece(y):
            r, y0 = where(n, y)
            at, ys = slice(y, y + chunk), slice(y0, y0 + chunk)
            even, odd = post[n][at, near], post[n][at, far]
            o_ref[r, ys, near] = (first[n][at, near] + twice_gelu(even + odd)).astype(BF16)
            done[n][at] = (first[n][at, far] + twice_gelu(even - odd)).astype(BF16)

        return [functools.partial(piece, y) for y in pieces]

    def finish(n):
        def piece():
            z = jnp.dot(done[n][...], flip_ref[...], preferred_element_type=F32).astype(BF16)
            for at in range(0, unit, min(unit, width)):
                r, y0 = where(n, at)
                o_ref[r, y0 : y0 + min(unit, width), far] = z[at : at + min(unit, width)]

        return [piece]

    @pl.when(step == 0)
    def _():
        for copy in copies(step):
            copy.start()

    @pl.when(step < last - 1)
    def _():
        for copy in copies(step + 1):
            copy.start()

    @pl.when(step == 0)
    def _():
        expand(r_ref, v_ref, b_ref)

    @pl.when(step < last)
    def _():
        for copy in copies(step):
            copy.wait()

    @pl.when(step == 0)
    def _():
        weave(lateral_product(0), [])
        weave(lateral_product(1), lateral_points(0))
        weave(depth_product(0), lateral_points(1))

    @pl.when(jnp.logical_and(step > 0, step < last))
    def _():
        weave(depth_product(1), depth_points(0))
        weave(lateral_product(0) + finish(0), depth_points(1))
        weave(lateral_product(1) + finish(1), lateral_points(0))
        weave(depth_product(0), lateral_points(1))

    @pl.when(step == last)
    def _():
        weave(depth_product(1), depth_points(0))
        weave(finish(0), depth_points(1))
        weave(finish(1), [])


def twice_gelu(half):
    return half + half * jnp.tanh(half * (TANH_A + TANH_B * (half * half)))


def diagonals(matrices):
    n = matrices.shape[1]
    few = math.isqrt(n)
    shift, lane = np.divmod(np.arange(n * n), n)
    to = (lane + shift // few * few) % n
    picks = np.zeros((n * n, n * n), np.float32)
    picks[(to - shift) % n * n + to, np.arange(n * n)] = 1
    rows = jnp.dot(matrices.reshape(-1, n * n), picks, precision=lax.Precision.HIGHEST)
    return jnp.repeat(jnp.transpose(rows.reshape(-1, n, n), (1, 0, 2)), LANE // n, axis=2)


def fits(mesh_lat, rows, width_y, cells, chans, modes_x, modes_y):
    return (
        cells == 2 * SPAN
        and SPAN % (LANE // chans * chans) == 0
        and mesh_lat * GROUP * SPAN == modes_y * cells
        and rows % 4 == 0
        and rows >= 16
        and width_y % 256 == 0
        and 4 * modes_y == SPAN
        and modes_x % 8 == 0
        and math.isqrt(chans) ** 2 == chans
    )


def shards(field, lat_modes, lat_gains, lat_local, depth_modes, depth_local):
    devices = lax.axis_size("lat")
    rows, width_y, cells = field.shape
    modes_x, chans, _ = lat_modes.shape
    modes_y = lat_gains.shape[0]
    modes_z = depth_modes.shape[0]
    if not fits(devices, rows, width_y, cells, chans, modes_x, modes_y):
        return plain_shards(field, lat_modes, lat_gains, lat_local, depth_modes, depth_local)
    depth = cells // chans
    width_x = rows * devices
    basis_x = basis64(width_x, modes_x)
    basis_y = basis64(width_y, modes_y)
    basis_z = basis64(depth, modes_z)
    funcs, fine = window_modes(rows, width_x, modes_x)
    count = funcs.shape[0]
    packed = (count + fine) * GROUP
    halves = cells // SPAN
    me = lax.axis_index("lat")

    by_high, by_low = split64(basis_y)
    by_forward = np.concatenate([by_high, by_low], axis=0)
    pairs = 4
    steps = rows // (2 * pairs)
    sent = pl.pallas_call(
        functools.partial(forward_kernel, funcs, fine),
        grid=(steps + 1,),
        in_specs=[
            pl.BlockSpec((2 * modes_y, width_y), lambda s: (0, 0)),
            pl.BlockSpec((pairs, width_y, cells), lambda s: (jnp.minimum(s, steps - 1), 0, 0)),
            pl.BlockSpec((pairs, width_y, cells), lambda s: (2 * steps - 1 - jnp.minimum(s, steps - 1), 0, 0)),
        ],
        out_specs=pl.BlockSpec((devices, packed, SPAN), lambda s: (0, 0, 0)),
        out_shape=jax.ShapeDtypeStruct((devices, packed, SPAN), BF16),
        scratch_shapes=[
            pltpu.VMEM((2 * pairs, modes_y, cells), F32),
            pltpu.VMEM((count, modes_y, cells), F32),
        ],
        compiler_params=pltpu.CompilerParams(vmem_limit_bytes=48 * 2**20),
        name="forward",
    )(by_forward, field, field)
    gathered = lax.all_to_all(sent, "lat", split_axis=0, concat_axis=0, tiled=True)

    per = SPAN // chans
    flip = np.kron(np.eye(per)[::-1], np.eye(chans)).astype(ml_dtypes.bfloat16)
    near_z = basis_z[:, :per]
    ids = np.arange(SPAN)
    pick = (np.arange(chans)[:, None] == ids[None, :] % chans).astype(np.float32)
    mask = (ids[:, None] // chans == ids[None, :] // chans).astype(np.float32)
    halved = [near_z[parity::2] for parity in range(2)]
    outer = np.stack([0.5 * np.kron(b.T, np.eye(chans)) for b in halved]).astype(np.float32)
    inner = np.stack([np.kron(b, np.ones((chans, chans))) for b in halved]).astype(np.float32)
    anywhere = pl.BlockSpec(memory_space=pl.ANY)
    local, turned, depth_weights = pl.pallas_call(
        prepare_kernel,
        in_specs=9 * [pl.BlockSpec(memory_space=pltpu.VMEM)] + [anywhere],
        out_shape=[
            jax.ShapeDtypeStruct((2 * SPAN, SPAN), BF16),
            jax.ShapeDtypeStruct((2 * SPAN, SPAN), BF16),
            jax.ShapeDtypeStruct((2, 3 * SPAN, SPAN), BF16),
        ],
        compiler_params=pltpu.CompilerParams(vmem_limit_bytes=24 * 2**20),
        name="prepare",
    )(lat_local, depth_modes, depth_local, pick, pick.T.copy(), mask, outer, inner, flip, sent)
    four = 4
    local_near = pl.pallas_call(
        local_near_kernel,
        grid=(rows // four,),
        in_specs=[
            pl.BlockSpec((four, width_y, SPAN), lambda s: (s, 0, 0)),
            pl.BlockSpec((2 * SPAN, SPAN), lambda s: (0, 0)),
        ],
        out_specs=pl.BlockSpec((four, width_y, SPAN), lambda s: (s, 0, 0)),
        out_shape=jax.ShapeDtypeStruct((rows, width_y, SPAN), F32),
        compiler_params=pltpu.CompilerParams(vmem_limit_bytes=48 * 2**20),
        name="local_near",
    )(field, local)

    weights = np.einsum("pit,jt->pij", basis_x.reshape(modes_x, devices, rows), funcs)
    flat = weights.reshape(modes_x, devices * count)
    ah, al = split64(np.pad(flat, ((0, 0), (0, -flat.shape[1] % LANE))))
    a_forward = np.concatenate([ah, al], axis=0)
    bh, bl = split64(flat.T)
    a_back = np.concatenate([bh, bl, bh, bl], axis=1)
    gains = lax.dynamic_slice_in_dim(lat_gains, (me // halves) * GROUP, GROUP, axis=0)
    gains = jnp.tile(jnp.repeat(gains, LANE // chans, axis=1), (1, SPAN // LANE))
    per_lane = LANE // chans
    ids = np.arange(LANE)
    order = np.zeros((LANE, LANE))
    order[ids, ids % chans * per_lane + ids // chans] = 1
    order = np.kron(np.eye(SPAN // LANE), order).astype(ml_dtypes.bfloat16)
    place = jnp.where(me % halves == 1, order.T @ flip, order.T)
    mixed = pl.pallas_call(
        functools.partial(mix_kernel, count, fine),
        in_specs=7 * [pl.BlockSpec(memory_space=pltpu.VMEM)] + [pl.BlockSpec(memory_space=pl.ANY)],
        out_shape=jax.ShapeDtypeStruct((devices, packed, SPAN), BF16),
        scratch_shapes=[
            pltpu.VMEM((SPAN // LANE, a_forward.shape[1] * GROUP, LANE), F32),
            pltpu.VMEM((SPAN // LANE, devices * count * GROUP, LANE), F32),
            pltpu.VMEM((devices * packed, SPAN), BF16),
        ],
        compiler_params=pltpu.CompilerParams(vmem_limit_bytes=48 * 2**20),
        name="mix",
    )(gathered, a_forward, a_back, gains, diagonals(lat_modes), order, place, local_near)
    returned = lax.all_to_all(mixed, "lat", split_axis=0, concat_axis=0, tiled=True)

    local_far, mirrored = pl.pallas_call(
        local_far_kernel,
        grid=(rows // four,),
        in_specs=[
            pl.BlockSpec((four, width_y, SPAN), lambda s: (s, 0, 1)),
            pl.BlockSpec((2 * SPAN, SPAN), lambda s: (0, 0)),
            pl.BlockSpec((SPAN, SPAN), lambda s: (0, 0)),
            pl.BlockSpec(memory_space=pl.ANY),
        ],
        out_specs=2 * [pl.BlockSpec((four, width_y, SPAN), lambda s: (s, 0, 0))],
        out_shape=[
            jax.ShapeDtypeStruct((rows, width_y, SPAN), F32),
            jax.ShapeDtypeStruct((rows, width_y, SPAN), BF16),
        ],
        compiler_params=pltpu.CompilerParams(vmem_limit_bytes=48 * 2**20),
        name="local_far",
    )(field, turned, flip, mixed)

    by_back = np.concatenate([by_high, by_low, by_high, by_low], axis=0).T.copy()
    slots = np.concatenate([funcs, funcs[:fine]], axis=0)
    spread = np.concatenate(split64(np.kron(0.5 * slots.T, np.eye(GROUP))), axis=0)
    block = 4
    unit = block * width_y // 2
    wide = (unit, cells)
    narrow = (unit, SPAN)
    steps = rows // block
    return pl.pallas_call(
        functools.partial(tail_kernel, 16),
        grid=(steps + 1,),
        in_specs=[
            pl.BlockSpec((devices, packed, SPAN), lambda s: (0, 0, 0)),
            *(4 * [anywhere]),
            pl.BlockSpec((width_y, SPAN), lambda s: (0, 0)),
            pl.BlockSpec((2, 3 * SPAN, SPAN), lambda s: (0, 0, 0)),
            pl.BlockSpec((SPAN, SPAN), lambda s: (0, 0)),
            pl.BlockSpec(spread.shape, lambda s: (0, 0)),
        ],
        out_specs=pl.BlockSpec((block, width_y, cells), lambda s: (jnp.maximum(s - 1, 0), 0, 0)),
        out_shape=jax.ShapeDtypeStruct(field.shape, BF16),
        scratch_shapes=[pltpu.VMEM((rows, 2 * modes_y, cells), BF16)]
        + 2 * [pltpu.VMEM(wide, F32)]
        + 2 * [pltpu.VMEM(wide, F32)]
        + 2 * [pltpu.VMEM((unit, 4 * SPAN), BF16)]
        + 2 * [pltpu.VMEM(wide, F32)]
        + 2 * [pltpu.VMEM(narrow, BF16)]
        + 2 * [pltpu.VMEM((2, block, width_y, SPAN), F32)]
        + 2 * [pltpu.VMEM((2, block, width_y, SPAN), BF16)]
        + [pltpu.SemaphoreType.DMA((2, 4))],
        compiler_params=pltpu.CompilerParams(vmem_limit_bytes=50 * 2**20),
        name="tail",
    )(
        returned,
        local_near,
        local_far,
        field,
        mirrored,
        by_back,
        depth_weights,
        flip,
        spread,
    )


def solution(mesh):
    placed = (P(("group", "lat"), None, None), P(), P(), P(), P(), P())
    return jax.shard_map(
        shards,
        mesh=mesh,
        in_specs=placed,
        out_specs=P(("group", "lat"), None, None),
        check_vma=False,
    )
```
